512 devices in a mesh: gx: 64 (over x, z, y_lo), gz: 8 (over y_hi, core).
Axes of the slice: x: 4, y: 8 (y_hi: 4, y_lo: 2; y = y_hi * 2 + y_lo), z: 8, core: 2. Of those that a mesh axis runs over, the one named last changes fastest.
Arguments:
- velocity: float32 [3, 1024, 64, 256], P(None, 'gx', 'gz'), may hold values from -6 to 6
- pressure: float32 [1024, 64, 256], P('gx', 'gz'), may hold values from 1 to 3
- stress_old: float32 [6, 1024, 64, 256], P(None, 'gx', 'gz'), may hold values from -6 to 6
- plastic: float32 [1024, 64, 256], P('gx', 'gz'), may hold values from 0 to 2
- viscosity: float32 [1024, 64, 256], P('gx', 'gz'), may hold values from 1 to 30
- weak_seed: int32 [1024, 64, 256], P('gx', 'gz'), may hold values 0 or 1
Outputs:
- velocity_out: float32 [3, 1024, 64, 256], P(None, 'gx', 'gz')
- pressure_out: float32 [1024, 64, 256], P('gx', 'gz')
- stress_out: float32 [6, 1024, 64, 256], P(None, 'gx', 'gz')
- plastic_out: float32 [1024, 64, 256], P('gx', 'gz')
- yield_peak: float32 [2], replicated
The draws below stay inside these ranges and needn't reach their ends.
All inputs are finite; a program needn't handle non-finite values. No bound on the sum of `weak_seed` on one device may be relied on, other than what follows from the above.
Results may differ from the reference program's by a relative error of at most 0.000059.
Values sent between devices are 32-bit elements; how exact they have to be, the bound alone decides.
No kernel may reach another device: no remote copies, remote signals or barrier semaphores. Data moves between devices by JAX's collectives and lax.ppermute only.
A program may use at most 64 MiB of HBM per device.

```python
import math
import jax
import jax.numpy as jnp
from jax import lax

NY = 256
ITERS = 2
NX = 1024
NZ = 64


def draw_viscosity(key, part):
    xpos = jnp.arange(NX, dtype=jnp.float32) / max(NX - 1, 1)
    ramp = jnp.exp(jnp.log(10.0) * xpos)[:, None, None]
    rough = jnp.exp(jax.random.uniform(key, (NX, NZ, NY), jnp.float32, 0.0, jnp.log(3.0)))
    return (ramp * rough).astype(jnp.float32)


def touch_ends(array, rng, least, largest):
    longest = array.shape.index(max(array.shape))
    spots = []
    for shift in (0, 1):
        where = [jax.random.randint(jax.random.fold_in(rng, axis), (), 0, length) for axis, length in enumerate(array.shape)]
        where[longest] = (where[longest] + shift) % array.shape[longest]
        spots.append(tuple(where))
    return array.at[spots[0]].set(least).at[spots[1]].set(largest)


def level_of(own_key, extent, cuts, smallest, high):
    factor_of, own = 1.0, jax.random.fold_in(own_key, 6)
    for position, shards_of in cuts:
        draws = jnp.exp(jax.random.uniform(jax.random.fold_in(own, position), (shards_of,), jnp.float32, smallest / len(cuts), high / len(cuts)))
        factor_of = factor_of * jnp.repeat(draws, extent[position] // shards_of).reshape([-1 if axis == position else 1 for axis in range(len(extent))])
    return factor_of


def bell_draw(own_key, extent, deviation, limit, cuts=(), held_as=jnp.bfloat16):
    result = deviation * jax.random.normal(own_key, extent, jnp.float32)
    if cuts:
        result = result * level_of(own_key, extent, cuts, -0.22, 0.18)
    return jnp.clip(result, -limit, limit).astype(held_as)


def setup_inputs(seed: int = 0) -> dict:
    key_of = jax.random.split(jax.random.key(seed), 7)
    velocity = bell_draw(key_of[0], (3, NX, NZ, NY), 1.0, 6.0, ((1, 64), (2, 8)), jnp.float32)
    pressure = jnp.clip(1.0 + 2.0 * jax.random.uniform(key_of[1], (NX, NZ, NY), jnp.float32) ** level_of(key_of[1], (NX, NZ, NY), ((0, 64), (1, 8)), -0.2, 0.2), 1.0, 3.0)
    stress_old = bell_draw(key_of[2], (6, NX, NZ, NY), 1.0, 6.0, ((1, 64), (2, 8)), jnp.float32)
    plastic = jnp.clip(2.0 * jax.random.uniform(key_of[3], (NX, NZ, NY), jnp.float32) ** level_of(key_of[3], (NX, NZ, NY), ((0, 64), (1, 8)), -0.2, 0.2), 0.0, 2.0)
    viscosity = draw_viscosity(jax.random.fold_in(key_of[6], 71), 0)
    weak_seed = touch_ends((jax.random.randint(key_of[5], (NX, NZ, NY), 0, 8) < 1).astype(jnp.int32), jax.random.fold_in(key_of[5], 1), 0, 1)
    return {"velocity": velocity, "pressure": pressure, "stress_old": stress_old, "plastic": plastic, "viscosity": viscosity, "weak_seed": weak_seed}


unnormalized_weights = [math.exp(-(k * k) / 18.0) for k in range(-6, 7)]
weight_total = sum(unnormalized_weights)
gauss_weights = [value / weight_total for value in unnormalized_weights]
shear_time_increment = 20.0

def smooth_axis(field, axis):
    count = field.shape[axis]
    widths = [(0, 0)] * field.ndim
    widths[axis] = (6, 6)
    padded = jnp.pad(field, widths)
    total = gauss_weights[0] * lax.slice_in_dim(padded, 0, count, axis=axis)
    for index in range(1, 13):
        total = total + gauss_weights[index] * lax.slice_in_dim(padded, index, index + count, axis=axis)
    return total

def y_matrix(length):
    places = jnp.arange(length)
    gap = (places[:, None] - places[None, :]).astype(jnp.float32)
    return jnp.where(jnp.abs(gap) <= 6.0, jnp.exp(-gap * gap / 18.0) / weight_total, 0.0).astype(jnp.float32)

def smooth_y(field):
    length = field.shape[-1]
    flat = field.reshape(-1, length)
    return jnp.dot(flat, y_matrix(length), precision=lax.Precision.HIGHEST).reshape(field.shape)

def diff_axis(field, axis):
    count = field.shape[axis]
    widths = [(0, 0)] * field.ndim
    widths[axis] = (1, 1)
    padded = jnp.pad(field, widths)
    return (lax.slice_in_dim(padded, 2, count + 2, axis=axis) - lax.slice_in_dim(padded, 0, count, axis=axis)) * 0.5

def return_map(velocity_x_spacing, velocity_z_spacing, dyv, stress_old, eta_ve, pres, cohesion_strength):
    divv = velocity_x_spacing[0] + velocity_z_spacing[1] + dyv[2]
    pres = pres - 0.25 * divv
    strain = jnp.stack([velocity_x_spacing[0] - divv / 3.0, velocity_z_spacing[1] - divv / 3.0, dyv[2] - divv / 3.0, 0.5 * (velocity_x_spacing[1] + velocity_z_spacing[0]), 0.5 * (velocity_x_spacing[2] + dyv[0]), 0.5 * (velocity_z_spacing[2] + dyv[1])])
    trial = 2.0 * eta_ve * (strain + stress_old / (2.0 * shear_time_increment))
    tau_ii = jnp.sqrt(0.5 * (trial[0] ** 2 + trial[1] ** 2 + trial[2] ** 2) + trial[3] ** 2 + trial[4] ** 2 + trial[5] ** 2)
    yield_f = tau_ii - 0.5 * jnp.maximum(pres, 0.0) - 0.8660254 * cohesion_strength
    dlam = jnp.maximum(yield_f, 0.0) / (eta_ve + 0.5)
    shrink = 1.0 - eta_ve * dlam / jnp.maximum(tau_ii, 0.5)
    return (pres, trial * shrink, shrink, yield_f, dlam)

def reference(velocity, pressure, stress_old, plastic, viscosity, weak_seed):
    smoothed = smooth_y(smooth_axis(smooth_axis(plastic, 0), 1))
    eta_ve = 1.0 / (1.0 / viscosity + 1.0 / shear_time_increment)
    seeded = weak_seed.astype(jnp.float32)
    cohesion_strength = (1.0 - 0.6 * seeded) / (1.0 + 2.0 * smoothed)
    pres = pressure
    plastic_sum = plastic
    peaks = []
    tau = stress_old
    for step_index in range(ITERS):
        velocity_x_spacing = diff_axis(velocity, 1)
        velocity_z_spacing = diff_axis(velocity, 2)
        dyv = diff_axis(velocity, 3)
        pres, tau, shrink, yield_f, dlam = return_map(velocity_x_spacing, velocity_z_spacing, dyv, stress_old, eta_ve, pres, cohesion_strength)
        plastic_sum = plastic_sum + dlam
        peaks.append(jnp.max(yield_f))
        step = 0.125 / jnp.max(eta_ve * shrink)
        sxx = tau[0] - pres
        szz = tau[1] - pres
        syy = tau[2] - pres
        rx = diff_axis(sxx, 0) + diff_axis(tau[3], 1) + diff_axis(tau[4], 2)
        rz = diff_axis(tau[3], 0) + diff_axis(szz, 1) + diff_axis(tau[5], 2)
        ry = diff_axis(tau[4], 0) + diff_axis(tau[5], 1) + diff_axis(syy, 2)
        velocity = velocity + step * jnp.stack([rx, rz, ry])
    return (velocity, pres, tau, plastic_sum, jnp.stack(peaks))
```

```python
import math

import jax
import jax.numpy as jnp
from jax import lax
from jax.sharding import Mesh
from jax.sharding import PartitionSpec as P

ITERS = 2
GX = ("gx_0", "gx_1", "gx_2")
GZ = ("gz_0", "gz_1")
YCORE = ("gx_2", "gz_0", "gz_1")
XZ = ("gx_0", "gx_1")


unnormalized_weights = [math.exp(-(k * k) / 18.0) for k in range(-6, 7)]
weight_total = sum(unnormalized_weights)
gauss_weights = [value / weight_total for value in unnormalized_weights]
shear_time_increment = 20.0


def pairs(count, first):
    out = []
    for i in range(first, count - 1, 2):
        out += [(i, i + 1), (i + 1, i)]
    return out


def exchange(axis, first, last):
    count = lax.axis_size(axis)
    even = lax.axis_index(axis) % 2 == 0
    far = lax.ppermute(jnp.where(even, first, last), axis, pairs(count, 1))
    near = lax.ppermute(jnp.where(even, last, first), axis, pairs(count, 0))
    return jnp.where(even, far, near), jnp.where(even, near, far)


def global_max(a, b):
    row = jnp.where(jnp.arange(128) == 0, a, b)
    for axes in (YCORE, XZ):
        count = lax.axis_size(axes)
        sent = jnp.broadcast_to(row, (count, 1, 128))
        row = jnp.max(lax.all_to_all(sent, axes, 0, 0, tiled=True), axis=(0, 1))
    return row[0], row[1]


def smooth_slices(padded, axis, count):
    total = gauss_weights[0] * lax.slice_in_dim(padded, 0, count, axis=axis)
    for index in range(1, 13):
        total = total + gauss_weights[index] * lax.slice_in_dim(
            padded, index, index + count, axis=axis
        )
    return total


def y_matrix(length):
    places = jnp.arange(length)
    gap = (places[:, None] - places[None, :]).astype(jnp.float32)
    return jnp.where(jnp.abs(gap) <= 6.0, jnp.exp(-gap * gap / 18.0) / weight_total, 0.0)


def smooth_y(field):
    length = field.shape[-1]
    flat = field.reshape(-1, length)
    return jnp.dot(flat, y_matrix(length), precision=lax.Precision.HIGHEST).reshape(field.shape)


def diff_y(field):
    widths = [(0, 0)] * (field.ndim - 1) + [(1, 1)]
    padded = jnp.pad(field, widths)
    return (padded[..., 2:] - padded[..., :-2]) * 0.5


def diff(field, halo, dim):
    low, high = halo
    padded = jnp.concatenate([low, field, high], axis=dim)
    count = field.shape[dim]
    return (
        lax.slice_in_dim(padded, 2, count + 2, axis=dim)
        - lax.slice_in_dim(padded, 0, count, axis=dim)
    ) * 0.5


def edges(field, dim, width):
    count = field.shape[dim]
    return (
        lax.slice_in_dim(field, 0, width, axis=dim),
        lax.slice_in_dim(field, count - width, count, axis=dim),
    )


def return_map(dxv, dzv, dyv, stress_old, eta_ve, pres, cohesion_strength):
    divv = dxv[0] + dzv[1] + dyv[2]
    pres = pres - 0.25 * divv
    strain = jnp.stack(
        [
            dxv[0] - divv / 3.0,
            dzv[1] - divv / 3.0,
            dyv[2] - divv / 3.0,
            0.5 * (dxv[1] + dzv[0]),
            0.5 * (dxv[2] + dyv[0]),
            0.5 * (dzv[2] + dyv[1]),
        ]
    )
    trial = 2.0 * eta_ve * (strain + stress_old / (2.0 * shear_time_increment))
    tau_ii = jnp.sqrt(
        0.5 * (trial[0] ** 2 + trial[1] ** 2 + trial[2] ** 2)
        + trial[3] ** 2
        + trial[4] ** 2
        + trial[5] ** 2
    )
    yield_f = tau_ii - 0.5 * jnp.maximum(pres, 0.0) - 0.8660254 * cohesion_strength
    dlam = jnp.maximum(yield_f, 0.0) / (eta_ve + 0.5)
    shrink = 1.0 - eta_ve * dlam / jnp.maximum(tau_ii, 0.5)
    return (pres, trial * shrink, shrink, yield_f, dlam)


def per_device(velocity, pressure, stress_old, plastic, viscosity, weak_seed):
    rows_x, rows_z, length = plastic.shape
    v_first, v_last = edges(velocity, 1, 1)
    p_first, p_last = edges(plastic, 0, 6)
    x_low, x_high = exchange(
        GX,
        jnp.concatenate([v_first[:, 0], p_first]),
        jnp.concatenate([v_last[:, 0], p_last]),
    )
    v_x = (x_low[:3][:, None], x_high[:3][:, None])
    along_x = smooth_slices(jnp.concatenate([x_low[3:], plastic, x_high[3:]]), 0, rows_x)
    v_first, v_last = edges(velocity, 2, 1)
    p_first, p_last = edges(along_x, 1, 6)
    z_low, z_high = exchange(
        GZ,
        jnp.concatenate([v_first[:, :, 0], jnp.swapaxes(p_first, 0, 1)]),
        jnp.concatenate([v_last[:, :, 0], jnp.swapaxes(p_last, 0, 1)]),
    )
    v_z = (z_low[:3][:, :, None], z_high[:3][:, :, None])
    along_z = smooth_slices(
        jnp.concatenate(
            [jnp.swapaxes(z_low[3:], 0, 1), along_x, jnp.swapaxes(z_high[3:], 0, 1)], axis=1
        ),
        1,
        rows_z,
    )
    smoothed = smooth_y(along_z)
    eta_ve = 1.0 / (1.0 / viscosity + 1.0 / shear_time_increment)
    seeded = weak_seed.astype(jnp.float32)
    cohesion_strength = (1.0 - 0.6 * seeded) / (1.0 + 2.0 * smoothed)
    pres = pressure
    plastic_sum = plastic
    peaks = []
    dxv = diff(velocity, v_x, 1)
    dzv = diff(velocity, v_z, 2)
    dyv = diff_y(velocity)
    for step_index in range(ITERS):
        pres, tau, shrink, yield_f, dlam = return_map(
            dxv, dzv, dyv, stress_old, eta_ve, pres, cohesion_strength
        )
        plastic_sum = plastic_sum + dlam
        sxx = tau[0] - pres
        szz = tau[1] - pres
        syy = tau[2] - pres
        xs = jnp.stack([sxx, tau[3], tau[4]])
        zs = jnp.stack([tau[3], szz, tau[5]])
        ys = jnp.stack([tau[4], tau[5], syy])
        x_low, x_high = exchange(GX, *[e[:, 0] for e in edges(xs, 1, 1)])
        z_low, z_high = exchange(GZ, *[e[:, :, 0] for e in edges(zs, 2, 1)])
        top_yield, peak_eta = global_max(jnp.max(yield_f), jnp.max(eta_ve * shrink))
        peaks.append(top_yield)
        step = 0.125 / peak_eta
        residual = (
            diff(xs, (x_low[:, None], x_high[:, None]), 1)
            + diff(zs, (z_low[:, :, None], z_high[:, :, None]), 2)
            + diff_y(ys)
        )
        if step_index + 1 < ITERS:
            x_low, x_high = exchange(GX, *[e[:, 0] for e in edges(residual, 1, 1)])
            z_low, z_high = exchange(GZ, *[e[:, :, 0] for e in edges(residual, 2, 1)])
            dxv = dxv + step * diff(residual, (x_low[:, None], x_high[:, None]), 1)
            dzv = dzv + step * diff(residual, (z_low[:, :, None], z_high[:, :, None]), 2)
            dyv = dyv + step * diff_y(residual)
        velocity = velocity + step * residual
    return (velocity, pres, tau, plastic_sum, jnp.stack(peaks))


def solution(mesh):
    split = Mesh(mesh.devices.reshape(4, 8, 2, 4, 2), ("gx_0", "gx_1", "gx_2", "gz_0", "gz_1"))
    return jax.shard_map(
        per_device,
        mesh=split,
        in_specs=(
            P(None, GX, GZ, None),
            P(GX, GZ, None),
            P(None, GX, GZ, None),
            P(GX, GZ, None),
            P(GX, GZ, None),
            P(GX, GZ, None),
        ),
        out_specs=(
            P(None, GX, GZ, None),
            P(GX, GZ, None),
            P(None, GX, GZ, None),
            P(GX, GZ, None),
            P(),
        ),
        check_vma=False,
    )
```

```python
import math

import jax
import jax.numpy as jnp
from jax import lax
from jax.experimental import pallas as pl
from jax.experimental.pallas import tpu as pltpu
from jax.sharding import Mesh
from jax.sharding import PartitionSpec as P

GX = ("gx_0", "gx_1", "gx_2")
GZ = ("gz_0", "gz_1")
YCORE = ("gx_2", "gz_0", "gz_1")
XZ = ("gx_0", "gx_1")

WEIGHT_TOTAL = sum(math.exp(-(k * k) / 18.0) for k in range(-6, 7))
WEIGHTS = [math.exp(-(k * k) / 18.0) / WEIGHT_TOTAL for k in range(-6, 7)]
SHEAR = 20.0
F32 = jnp.float32
LX, LZ, NY = 16, 8, 256
ROWS = LX * LZ
CHUNK = 16
XX, ZZ, YY, XZ_, XY, ZY = range(6)
ALONG_X = (XX, XZ_, XY)
ALONG_Z = (XZ_, ZZ, ZY)
ALONG_Y = (XY, ZY, YY)
VMEM = pl.BlockSpec(memory_space=pltpu.VMEM)
SMEM = pl.BlockSpec(memory_space=pltpu.SMEM)


def call(kernel, outs, operands, flops, scratch=(), out_specs=None):
    size = sum(math.prod(a.shape) * 4 for a in operands)
    size += sum(math.prod(s) * 4 for s in outs)
    return pl.pallas_call(
        kernel,
        out_shape=[jax.ShapeDtypeStruct(s, F32) for s in outs],
        in_specs=[VMEM] * len(operands),
        out_specs=out_specs or [VMEM] * len(outs),
        scratch_shapes=list(scratch),
        compiler_params=pltpu.CompilerParams(vmem_limit_bytes=14 * 1024 * 1024),
        cost_estimate=pl.CostEstimate(flops=flops, bytes_accessed=size, transcendentals=0),
    )(*operands)


def pairs(count, first):
    out = []
    for i in range(first, count - 1, 2):
        out += [(i, i + 1), (i + 1, i)]
    return out


def exchange(axis, far, near):
    count = lax.axis_size(axis)
    return (
        lax.ppermute(far, axis, pairs(count, 1)),
        lax.ppermute(near, axis, pairs(count, 0)),
    )


def spread(row, axes):
    return lax.all_to_all(row, axes, 0, 0, tiled=True)


def even_x():
    return lax.axis_index("gx_2") == 0


def even_z():
    return lax.axis_index("gz_1") == 0


def facing(even, first, last):
    return jnp.where(even, first, last), jnp.where(even, last, first)


def sides(even, far, near):
    return jnp.where(even, far, near), jnp.where(even, near, far)


def iotas():
    row = lax.broadcasted_iota(jnp.int32, (CHUNK, NY), 0) % LZ
    col = lax.broadcasted_iota(jnp.int32, (CHUNK, NY), 1)
    return row == 0, row == LZ - 1, col == 0, col == NY - 1


def below(ref, f, start, low):
    if start == 0:
        return jnp.concatenate([low, ref[f, 0 : CHUNK - LZ]], axis=0)
    return ref[f, start - LZ : start - LZ + CHUNK]


def above(ref, f, start, high):
    if start == ROWS - CHUNK:
        return jnp.concatenate([ref[f, start + LZ : ROWS], high], axis=0)
    return ref[f, start + LZ : start + LZ + CHUNK]


def diff_x(ref, f, start, low, high):
    return (above(ref, f, start, high) - below(ref, f, start, low)) * 0.5


def diff_z(value, low, high, masks):
    up = jnp.where(masks[1], high, pltpu.roll(value, CHUNK - 1, 0))
    down = jnp.where(masks[0], low, pltpu.roll(value, 1, 0))
    return (up - down) * 0.5


def diff_y(value, masks):
    up = jnp.where(masks[3], 0.0, pltpu.roll(value, NY - 1, 1))
    down = jnp.where(masks[2], 0.0, pltpu.roll(value, 1, 1))
    return (up - down) * 0.5


def spread_rows(face, f, low, high):
    for h in range(2):
        lanes = slice(h * 128, (h + 1) * 128)
        face[0, f, h, pl.ds(0, LX, stride=LZ), :] = low[:, lanes]
        face[1, f, h, pl.ds(LZ - 1, LX, stride=LZ), :] = high[:, lanes]


def face_rows(face, side, f, here):
    return jnp.concatenate([face[side, f, h, here] for h in range(2)], axis=1)


def keep(slots, f, value):
    for h in range(2):
        slots[f, h] = value[:, h * 128 : (h + 1) * 128]


def layer(slots, f, z):
    return jnp.concatenate([slots[f, h, pl.ds(z, LX, stride=LZ), :] for h in range(2)], axis=1)


def send_x(ref, fields, far, near):
    even = even_x()
    for i, f in enumerate(fields):
        a, b = facing(even, ref[f, 0:LZ], ref[f, ROWS - LZ : ROWS])
        far[i * LZ : (i + 1) * LZ] = a
        near[i * LZ : (i + 1) * LZ] = b


def send_z(ref, fields, far, near, slots):
    even = even_z()
    for i, f in enumerate(fields):
        keep(slots, i, ref[f])
        a, b = facing(even, layer(slots, i, 0), layer(slots, i, LZ - 1))
        far[i * LX : (i + 1) * LX] = a
        near[i * LX : (i + 1) * LX] = b


def store_row(out, top_yield, top_eta):
    a = jnp.max(top_yield, axis=(0, 1), keepdims=True)
    b = jnp.max(top_eta, axis=(0, 1), keepdims=True)
    lane = lax.broadcasted_iota(jnp.int32, (1, 128), 1)
    row = jnp.where(lane == 0, a, b)
    out[...] = jnp.broadcast_to(row[None], out.shape)


def relay_row(ref, out):
    out[...] = jnp.broadcast_to(jnp.max(ref[...], axis=0, keepdims=True), out.shape)


def row_values(ref):
    row = jnp.max(ref[...], axis=0)
    lane = lax.broadcasted_iota(jnp.int32, (1, 128), 1)
    top = jnp.max(jnp.where(lane == 0, row, -jnp.inf), axis=(0, 1), keepdims=True)
    eta = jnp.max(jnp.where(lane == 1, row, -jnp.inf), axis=(0, 1), keepdims=True)
    return top, eta


def return_map(dxv, dzv, dyv, old, eta, pres, cohesion):
    div = dxv[0] + dzv[1] + dyv[2]
    pres = pres - 0.25 * div
    third = div / 3.0
    strain = [
        dxv[0] - third,
        dzv[1] - third,
        dyv[2] - third,
        0.5 * (dxv[1] + dzv[0]),
        0.5 * (dxv[2] + dyv[0]),
        0.5 * (dzv[2] + dyv[1]),
    ]
    trial = [2.0 * eta * (e + o / (2.0 * SHEAR)) for e, o in zip(strain, old)]
    tau_ii = jnp.sqrt(
        0.5 * (trial[0] * trial[0] + trial[1] * trial[1] + trial[2] * trial[2])
        + trial[3] * trial[3]
        + trial[4] * trial[4]
        + trial[5] * trial[5]
    )
    yield_f = tau_ii - 0.5 * jnp.maximum(pres, 0.0) - 0.8660254 * cohesion
    dlam = jnp.maximum(yield_f, 0.0) / (eta + 0.5)
    shrink = 1.0 - eta * dlam / jnp.maximum(tau_ii, 0.5)
    return pres, [t * shrink for t in trial], eta * shrink, yield_f, dlam


def smooth_x_kernel(v, plastic, x_far, x_near, along, z_far, z_near, slots):
    even = even_x()
    low, high = sides(even, x_far[3 * LZ :], x_near[3 * LZ :])
    padded = jnp.concatenate([low, plastic[...], high], axis=0)
    total = WEIGHTS[0] * padded[0:ROWS]
    for k in range(1, 13):
        total = total + WEIGHTS[k] * padded[k * LZ : k * LZ + ROWS]
    along[...] = total
    keep(slots, 3, total)
    even = even_z()
    for i in range(9):
        if i < 3:
            keep(slots, i, v[i])
            a, b = facing(even, layer(slots, i, 0), layer(slots, i, LZ - 1))
        else:
            a, b = facing(even, layer(slots, 3, i - 3), layer(slots, 3, i - 1))
        z_far[i * LX : (i + 1) * LX] = a
        z_near[i * LX : (i + 1) * LX] = b


def gauss(gap, inside):
    g = gap.astype(F32)
    return jnp.where(inside & (jnp.abs(gap) <= 6), jnp.exp(g * g * (-1.0 / 18.0)) / WEIGHT_TOTAL, 0.0)


def dot(a, b):
    return jnp.dot(a, b, precision=lax.Precision.HIGHEST, preferred_element_type=F32)


def first_kernel(
    v, pressure, old, along, plastic, viscosity, seed, x_far, x_near, z_far, z_near,
    held, pres, total, eta_out, cohesion_out, row_out, sx_far, sx_near, sz_far, sz_near,
    face, slots,
):
    low, high = sides(even_z(), z_far[...], z_near[...])
    r = lax.broadcasted_iota(jnp.int32, (ROWS, ROWS), 0)
    c = lax.broadcasted_iota(jnp.int32, (ROWS, ROWS), 1)
    own = gauss(c % LZ - r % LZ, c // LZ == r // LZ)
    r = lax.broadcasted_iota(jnp.int32, (ROWS, 6 * LX), 0)
    c = lax.broadcasted_iota(jnp.int32, (ROWS, 6 * LX), 1)
    same = c % LX == r // LZ
    from_low = gauss(c // LX - 6 - r % LZ, same)
    from_high = gauss(c // LX + LZ - r % LZ, same)
    along_z = dot(own, along[...]) + dot(from_low, low[3 * LX :]) + dot(from_high, high[3 * LX :])
    r = lax.broadcasted_iota(jnp.int32, (NY, NY), 0)
    c = lax.broadcasted_iota(jnp.int32, (NY, NY), 1)
    smoothed = dot(along_z, gauss(r - c, r >= 0))
    cohesion_out[...] = (1.0 - 0.6 * seed[...].astype(F32)) / (1.0 + 2.0 * smoothed)
    for f in range(3):
        spread_rows(face, f, low[f * LX : (f + 1) * LX], high[f * LX : (f + 1) * LX])
    x_low, x_high = sides(even_x(), x_far[0 : 3 * LZ], x_near[0 : 3 * LZ])
    masks = iotas()
    top_yield = jnp.full((CHUNK, NY), -jnp.inf, F32)
    top_eta = jnp.full((CHUNK, NY), -jnp.inf, F32)
    for start in range(0, ROWS, CHUNK):
        here = slice(start, start + CHUNK)
        eta = 1.0 / (1.0 / viscosity[here] + 1.0 / SHEAR)
        dxv, dzv, dyv = [], [], []
        for f in range(3):
            value = v[f, here]
            slab = slice(f * LZ, (f + 1) * LZ)
            dxv.append(diff_x(v, f, start, x_low[slab], x_high[slab]))
            dzv.append(diff_z(value, face_rows(face, 0, f, here), face_rows(face, 1, f, here), masks))
            dyv.append(diff_y(value, masks))
        p, tau, eta_shrink, yield_f, dlam = return_map(
            dxv, dzv, dyv, [old[i, here] for i in range(6)], eta, pressure[here], cohesion_out[here]
        )
        for i in range(6):
            held[i, here] = tau[i] - p if i < 3 else tau[i]
        pres[here] = p
        total[here] = plastic[here] + dlam
        eta_out[here] = eta
        top_yield = jnp.maximum(top_yield, yield_f)
        top_eta = jnp.maximum(top_eta, eta_shrink)
    store_row(row_out, top_yield, top_eta)
    send_x(held, ALONG_X, sx_far, sx_near)
    send_z(held, ALONG_Z, sz_far, sz_near, slots)


def residual(held, x_far, x_near, z_far, z_near, out, face):
    x_low, x_high = sides(even_x(), x_far[...], x_near[...])
    z_low, z_high = sides(even_z(), z_far[...], z_near[...])
    for f in range(3):
        rows = slice(f * LX, (f + 1) * LX)
        spread_rows(face, f, z_low[rows], z_high[rows])
    masks = iotas()
    for start in range(0, ROWS, CHUNK):
        here = slice(start, start + CHUNK)
        for f in range(3):
            slab = slice(f * LZ, (f + 1) * LZ)
            out[f, here] = (
                diff_x(held, ALONG_X[f], start, x_low[slab], x_high[slab])
                + diff_z(held[ALONG_Z[f], here], face_rows(face, 0, f, here), face_rows(face, 1, f, here), masks)
                + diff_y(held[ALONG_Y[f], here], masks)
            )


def residual_kernel(
    held, sx_far, sx_near, sz_far, sz_near, row,
    out, row_out, rx_far, rx_near, rz_far, rz_near, face, slots,
):
    relay_row(row, row_out)
    residual(held, sx_far, sx_near, sz_far, sz_near, out, face)
    send_x(out, range(3), rx_far, rx_near)
    send_z(out, range(3), rz_far, rz_near, slots)


def last_residual_kernel(held, sx_far, sx_near, sz_far, sz_near, out, face):
    residual(held, sx_far, sx_near, sz_far, sz_near, out, face)


def relay_kernel(row, row_out):
    relay_row(row, row_out)


def second_kernel(
    v, res, x_far, x_near, z_far, z_near, rx_far, rx_near, rz_far, rz_near, row,
    old, pressure, plastic, eta_in, cohesion,
    stress, pres, total, v_out, held, row_out, top_out, sx_far, sx_near, sz_far, sz_near,
    face, slots,
):
    top, peak = row_values(row)
    top_out[...] = jnp.broadcast_to(top, top_out.shape)
    step = 0.125 / peak
    for f in range(3):
        v_out[f] = v[f] + step * res[f]
    x_low, x_high = sides(
        even_x(),
        x_far[0 : 3 * LZ] + step * rx_far[...],
        x_near[0 : 3 * LZ] + step * rx_near[...],
    )
    z_low, z_high = sides(
        even_z(),
        z_far[0 : 3 * LX] + step * rz_far[...],
        z_near[0 : 3 * LX] + step * rz_near[...],
    )
    for f in range(3):
        rows = slice(f * LX, (f + 1) * LX)
        spread_rows(face, f, z_low[rows], z_high[rows])
    masks = iotas()
    top_yield = jnp.full((CHUNK, NY), -jnp.inf, F32)
    top_eta = jnp.full((CHUNK, NY), -jnp.inf, F32)
    for start in range(0, ROWS, CHUNK):
        here = slice(start, start + CHUNK)
        dxv, dzv, dyv = [], [], []
        for f in range(3):
            value = v_out[f, here]
            slab = slice(f * LZ, (f + 1) * LZ)
            dxv.append(diff_x(v_out, f, start, x_low[slab], x_high[slab]))
            dzv.append(diff_z(value, face_rows(face, 0, f, here), face_rows(face, 1, f, here), masks))
            dyv.append(diff_y(value, masks))
        p, tau, eta_shrink, yield_f, dlam = return_map(
            dxv, dzv, dyv, [old[i, here] for i in range(6)], eta_in[here], pressure[here], cohesion[here]
        )
        for i in range(6):
            stress[i, here] = tau[i]
            held[i, here] = tau[i] - p if i < 3 else tau[i]
        pres[here] = p
        total[here] = plastic[here] + dlam
        top_yield = jnp.maximum(top_yield, yield_f)
        top_eta = jnp.maximum(top_eta, eta_shrink)
    store_row(row_out, top_yield, top_eta)
    send_x(held, ALONG_X, sx_far, sx_near)
    send_z(held, ALONG_Z, sz_far, sz_near, slots)


def final_kernel(v, res, row, first_top, v_out, peaks):
    top, peak = row_values(row)
    step = 0.125 / peak
    for f in range(3):
        v_out[f] = v[f] + step * res[f]
    peaks[0] = jnp.max(first_top[...])
    peaks[1] = jnp.max(top)


def per_device(velocity, pressure, stress_old, plastic, viscosity, weak_seed):
    shapes = [a.shape for a in (velocity, pressure, stress_old, plastic)]
    one = (ROWS, NY)
    v = velocity.reshape((3,) + one)
    old = stress_old.reshape((6,) + one)
    pressure, plastic, viscosity, weak_seed = (
        a.reshape(one) for a in (pressure, plastic, viscosity, weak_seed)
    )
    three, six = (3,) + one, (6,) + one
    face = pltpu.VMEM((2, 3, 2, ROWS, 128), F32)
    slots = pltpu.VMEM((4, 2, ROWS, 128), F32)
    level_1, level_2 = lax.axis_size(YCORE), lax.axis_size(XZ)
    row_1, row_2 = (level_1, 1, 128), (level_2, 1, 128)
    x_3, z_3, x_9, z_9 = (3 * LZ, NY), (3 * LX, NY), (9 * LZ, NY), (9 * LX, NY)

    first = jnp.concatenate([v[:, :LZ].reshape(x_3), plastic[: 6 * LZ]])
    last = jnp.concatenate([v[:, ROWS - LZ :].reshape(x_3), plastic[ROWS - 6 * LZ :]])
    x_msgs = exchange(GX, *facing(even_x(), first, last))
    along, *z_msgs = call(smooth_x_kernel, [one, z_9, z_9], [v, plastic, *x_msgs], 10**6, [slots])
    z_msgs = exchange(GZ, *z_msgs)
    held, pres, total, eta, cohesion, row, *sent = call(
        first_kernel,
        [six, one, one, one, one, row_1, x_3, x_3, z_3, z_3],
        [v, pressure, old, along, plastic, viscosity, weak_seed, *x_msgs, *z_msgs],
        10**7,
        [face, slots],
    )
    row = spread(row, YCORE)
    got = exchange(GX, *sent[:2]) + exchange(GZ, *sent[2:])
    res, row, *sent = call(
        residual_kernel, [three, row_2, x_3, x_3, z_3, z_3], [held, *got, row], 10**6, [face, slots]
    )
    row = spread(row, XZ)
    got = exchange(GX, *sent[:2]) + exchange(GZ, *sent[2:])
    stress, pres, total, v, held, row, first_top, *sent = call(
        second_kernel,
        [six, one, one, three, six, row_1, (1, 128), x_3, x_3, z_3, z_3],
        [v, res, *x_msgs, *z_msgs, *got, row, old, pres, total, eta, cohesion],
        10**7,
        [face, slots],
    )
    row = spread(row, YCORE)
    got = exchange(GX, *sent[:2]) + exchange(GZ, *sent[2:])
    (row,) = call(relay_kernel, [row_2], [row], 10**4)
    row = spread(row, XZ)
    (res,) = call(last_residual_kernel, [three], [held, *got], 10**6, [face])
    v, peaks = call(final_kernel, [three, (2,)], [v, res, row, first_top], 10**5, (), [VMEM, SMEM])
    outs = [a.reshape(s) for a, s in zip((v, pres, stress, total), shapes)]
    return (*outs, peaks)


def solution(mesh):
    split = Mesh(mesh.devices.reshape(4, 8, 2, 4, 2), ("gx_0", "gx_1", "gx_2", "gz_0", "gz_1"))
    return jax.shard_map(
        per_device,
        mesh=split,
        in_specs=(
            P(None, GX, GZ, None),
            P(GX, GZ, None),
            P(None, GX, GZ, None),
            P(GX, GZ, None),
            P(GX, GZ, None),
            P(GX, GZ, None),
        ),
        out_specs=(
            P(None, GX, GZ, None),
            P(GX, GZ, None),
            P(None, GX, GZ, None),
            P(GX, GZ, None),
            P(),
        ),
        check_vma=False,
    )
```

```python
import math

import jax
import jax.numpy as jnp
from jax import lax
from jax.experimental import pallas as pl
from jax.experimental.pallas import tpu as pltpu
from jax.sharding import Mesh
from jax.sharding import PartitionSpec as P

GX = ("gx_0", "gx_1", "gx_2")
GZ = ("gz_0", "gz_1")
YCORE = ("gx_2", "gz_0", "gz_1")
XZ = ("gx_0", "gx_1")

WEIGHT_TOTAL = sum(math.exp(-(k * k) / 18.0) for k in range(-6, 7))
WEIGHTS = [math.exp(-(k * k) / 18.0) / WEIGHT_TOTAL for k in range(-6, 7)]
SHEAR = 20.0
F32 = jnp.float32
LX, LZ, NY = 16, 8, 256
ROWS = LX * LZ
CHUNK = 16
XX, ZZ, YY, XZ_, XY, ZY = range(6)
ALONG_X = (XX, XZ_, XY)
ALONG_Z = (XZ_, ZZ, ZY)
ALONG_Y = (XY, ZY, YY)
VMEM = pl.BlockSpec(memory_space=pltpu.VMEM)
SMEM = pl.BlockSpec(memory_space=pltpu.SMEM)
HBM = pl.BlockSpec(memory_space=pltpu.HBM)


def call(kernel, outs, operands, flops, scratch=(), out_specs=None, in_specs=None, limit=14):
    size = sum(math.prod(a.shape) * 4 for a in operands)
    size += sum(math.prod(s) * 4 for s in outs)
    return pl.pallas_call(
        kernel,
        out_shape=[jax.ShapeDtypeStruct(s, F32) for s in outs],
        in_specs=in_specs or [VMEM] * len(operands),
        out_specs=out_specs or [VMEM] * len(outs),
        scratch_shapes=list(scratch),
        compiler_params=pltpu.CompilerParams(vmem_limit_bytes=limit * 1024 * 1024),
        cost_estimate=pl.CostEstimate(flops=flops, bytes_accessed=size, transcendentals=0),
    )(*operands)


def pairs(count, first):
    out = []
    for i in range(first, count - 1, 2):
        out += [(i, i + 1), (i + 1, i)]
    return out


def exchange(axis, far, near):
    count = lax.axis_size(axis)
    return (
        lax.ppermute(far, axis, pairs(count, 1)),
        lax.ppermute(near, axis, pairs(count, 0)),
    )


def spread(row, axes):
    return lax.all_to_all(row, axes, 0, 0, tiled=True)


def even_x():
    return lax.axis_index("gx_2") == 0


def even_z():
    return lax.axis_index("gz_1") == 0


def facing(even, first, last):
    return jnp.where(even, first, last), jnp.where(even, last, first)


def sides(even, far, near):
    return jnp.where(even, far, near), jnp.where(even, near, far)


def iotas():
    row = lax.broadcasted_iota(jnp.int32, (CHUNK, NY), 0) % LZ
    col = lax.broadcasted_iota(jnp.int32, (CHUNK, NY), 1)
    return row == 0, row == LZ - 1, col == 0, col == NY - 1


def below(ref, f, start, low):
    if start == 0:
        return jnp.concatenate([low, ref[f, 0 : CHUNK - LZ]], axis=0)
    return ref[f, start - LZ : start - LZ + CHUNK]


def above(ref, f, start, high):
    if start == ROWS - CHUNK:
        return jnp.concatenate([ref[f, start + LZ : ROWS], high], axis=0)
    return ref[f, start + LZ : start + LZ + CHUNK]


def diff_x(ref, f, start, low, high):
    return (above(ref, f, start, high) - below(ref, f, start, low)) * 0.5


def diff_z(value, low, high, masks):
    up = jnp.where(masks[1], high, pltpu.roll(value, CHUNK - 1, 0))
    down = jnp.where(masks[0], low, pltpu.roll(value, 1, 0))
    return (up - down) * 0.5


def diff_y(value, masks):
    up = jnp.where(masks[3], 0.0, pltpu.roll(value, NY - 1, 1))
    down = jnp.where(masks[2], 0.0, pltpu.roll(value, 1, 1))
    return (up - down) * 0.5


def spread_rows(face, f, low, high):
    for h in range(2):
        lanes = slice(h * 128, (h + 1) * 128)
        face[0, f, h, pl.ds(0, LX, stride=LZ), :] = low[:, lanes]
        face[1, f, h, pl.ds(LZ - 1, LX, stride=LZ), :] = high[:, lanes]


def face_rows(face, side, f, here):
    return jnp.concatenate([face[side, f, h, here] for h in range(2)], axis=1)


def keep(slots, f, value):
    for h in range(2):
        slots[f, h] = value[:, h * 128 : (h + 1) * 128]


def layer(slots, f, z):
    return jnp.concatenate([slots[f, h, pl.ds(z, LX, stride=LZ), :] for h in range(2)], axis=1)


def place(axes):
    index, count = 0, 1
    for axis in axes:
        size = lax.axis_size(axis)
        index, count = index * size + lax.axis_index(axis), count * size
    return index > 0, index < count - 1


def x_faces(ref, fields, out):
    for i, f in enumerate(fields):
        out[0, i * LZ : (i + 1) * LZ] = ref[f, 0:LZ]
        out[1, i * LZ : (i + 1) * LZ] = ref[f, ROWS - LZ : ROWS]


def z_faces(ref, fields, out, slots):
    for i, f in enumerate(fields):
        keep(slots, i, ref[f])
        out[0, i * LX : (i + 1) * LX] = layer(slots, i, 0)
        out[1, i * LX : (i + 1) * LX] = layer(slots, i, LZ - 1)


def faces_kernel(v, plastic, x_far, x_near, sem):
    even = even_x()
    for i, (out, low) in enumerate(((x_far, even), (x_near, jnp.logical_not(even)))):
        top = pl.multiple_of(jnp.where(low, 0, ROWS - LZ), LZ)
        deep = pl.multiple_of(jnp.where(low, 0, ROWS - 6 * LZ), LZ)
        copies = [
            pltpu.make_async_copy(
                v.at[f, pl.ds(top, LZ)], out.at[pl.ds(f * LZ, LZ)], sem.at[4 * i + f]
            )
            for f in range(3)
        ]
        copies.append(
            pltpu.make_async_copy(
                plastic.at[pl.ds(deep, 6 * LZ)], out.at[pl.ds(3 * LZ, 6 * LZ)], sem.at[4 * i + 3]
            )
        )
        for copy in copies:
            copy.start()
    for i, out in enumerate((x_far, x_near)):
        for f in range(3):
            rows = pl.ds(f * LZ, LZ)
            pltpu.make_async_copy(v.at[f, pl.ds(0, LZ)], out.at[rows], sem.at[4 * i + f]).wait()
        rows = pl.ds(3 * LZ, 6 * LZ)
        pltpu.make_async_copy(plastic.at[pl.ds(0, 6 * LZ)], out.at[rows], sem.at[4 * i + 3]).wait()


def load_kernel(
    v_in, plastic_in, pressure_in, old_in, viscosity_in, seed_in,
    v, plastic, pressure, old, eta, weak, viscosity, seed, sem,
):
    ins = (viscosity_in, seed_in, v_in, plastic_in, pressure_in, old_in)
    outs = (viscosity, seed, v, plastic, pressure, old)
    copies = [pltpu.make_async_copy(a, b, sem.at[i]) for i, (a, b) in enumerate(zip(ins, outs))]
    for copy in copies:
        copy.start()
    copies[0].wait()
    eta[...] = 1.0 / (1.0 / viscosity[...] + 1.0 / SHEAR)
    copies[1].wait()
    weak[...] = 1.0 - 0.6 * seed[...].astype(F32)
    for copy in copies[2:]:
        copy.wait()


def store_row(out, top_yield, top_eta, earlier=None):
    a = jnp.max(top_yield, axis=(0, 1), keepdims=True)
    b = jnp.max(top_eta, axis=(0, 1), keepdims=True)
    lane = lax.broadcasted_iota(jnp.int32, (1, 128), 1)
    row = jnp.where(lane == 0, a, b)
    if earlier is not None:
        row = jnp.where(lane == 2, earlier, row)
    out[...] = jnp.broadcast_to(row[None], out.shape)


def relay_row(ref, out):
    row = jnp.max(ref[...], axis=0)[0:1]
    out[...] = jnp.broadcast_to(row[None], out.shape)


def row_values(ref, lanes):
    row = jnp.max(ref[...], axis=0)[0:1]
    lane = lax.broadcasted_iota(jnp.int32, (1, 128), 1)
    return [
        jnp.max(jnp.where(lane == i, row, -jnp.inf), axis=(0, 1), keepdims=True) for i in lanes
    ]


def return_map(dxv, dzv, dyv, old, eta, pres, cohesion):
    div = dxv[0] + dzv[1] + dyv[2]
    pres = pres - 0.25 * div
    third = div / 3.0
    strain = [
        dxv[0] - third,
        dzv[1] - third,
        dyv[2] - third,
        0.5 * (dxv[1] + dzv[0]),
        0.5 * (dxv[2] + dyv[0]),
        0.5 * (dzv[2] + dyv[1]),
    ]
    trial = [2.0 * eta * (e + o / (2.0 * SHEAR)) for e, o in zip(strain, old)]
    tau_ii = jnp.sqrt(
        0.5 * (trial[0] * trial[0] + trial[1] * trial[1] + trial[2] * trial[2])
        + trial[3] * trial[3]
        + trial[4] * trial[4]
        + trial[5] * trial[5]
    )
    yield_f = tau_ii - 0.5 * jnp.maximum(pres, 0.0) - 0.8660254 * cohesion
    dlam = jnp.maximum(yield_f, 0.0) / (eta + 0.5)
    shrink = 1.0 - eta * dlam / jnp.maximum(tau_ii, 0.5)
    return pres, [t * shrink for t in trial], eta * shrink, yield_f, dlam


def smooth_x_kernel(v, plastic, x_far, x_near, along, z_far, z_near, slots):
    even = even_x()
    low, high = sides(even, x_far[3 * LZ :], x_near[3 * LZ :])
    padded = jnp.concatenate([low, plastic[...], high], axis=0)
    total = WEIGHTS[0] * padded[0:ROWS]
    for k in range(1, 13):
        total = total + WEIGHTS[k] * padded[k * LZ : k * LZ + ROWS]
    along[...] = total
    keep(slots, 3, total)
    even = even_z()
    for i in range(9):
        if i < 3:
            keep(slots, i, v[i])
            a, b = facing(even, layer(slots, i, 0), layer(slots, i, LZ - 1))
        else:
            a, b = facing(even, layer(slots, 3, i - 3), layer(slots, 3, i - 1))
        z_far[i * LX : (i + 1) * LX] = a
        z_near[i * LX : (i + 1) * LX] = b


def gauss(gap, inside):
    g = gap.astype(F32)
    return jnp.where(inside & (jnp.abs(gap) <= 6), jnp.exp(g * g * (-1.0 / 18.0)) / WEIGHT_TOTAL, 0.0)


def dot(a, b):
    return jnp.dot(a, b, precision=lax.Precision.HIGHEST, preferred_element_type=F32)


def first_kernel(
    v, pressure, old, along, plastic, eta_in, weak, x_far, x_near, z_far, z_near,
    part, pres, total, cohesion_out, vx_out, vz_out, gx, fz, row_out, sz_far, sz_near,
    face, slots, held,
):
    low, high = sides(even_z(), z_far[...], z_near[...])
    r = lax.broadcasted_iota(jnp.int32, (ROWS, ROWS), 0)
    c = lax.broadcasted_iota(jnp.int32, (ROWS, ROWS), 1)
    own = gauss(c % LZ - r % LZ, c // LZ == r // LZ)
    r = lax.broadcasted_iota(jnp.int32, (ROWS, 6 * LX), 0)
    c = lax.broadcasted_iota(jnp.int32, (ROWS, 6 * LX), 1)
    same = c % LX == r // LZ
    from_low = gauss(c // LX - 6 - r % LZ, same)
    from_high = gauss(c // LX + LZ - r % LZ, same)
    along_z = dot(own, along[...]) + dot(from_low, low[3 * LX :]) + dot(from_high, high[3 * LX :])
    r = lax.broadcasted_iota(jnp.int32, (NY, NY), 0)
    c = lax.broadcasted_iota(jnp.int32, (NY, NY), 1)
    smoothed = dot(along_z, gauss(r - c, r >= 0))
    cohesion_out[...] = weak[...] / (1.0 + 2.0 * smoothed)
    for f in range(3):
        spread_rows(face, f, low[f * LX : (f + 1) * LX], high[f * LX : (f + 1) * LX])
    x_low, x_high = sides(even_x(), x_far[0 : 3 * LZ], x_near[0 : 3 * LZ])
    vx_out[0], vx_out[1] = x_low, x_high
    vz_out[0], vz_out[1] = low[0 : 3 * LX], high[0 : 3 * LX]
    masks = iotas()
    top_yield = jnp.full((CHUNK, NY), -jnp.inf, F32)
    top_eta = jnp.full((CHUNK, NY), -jnp.inf, F32)
    for start in range(0, ROWS, CHUNK):
        here = slice(start, start + CHUNK)
        eta = eta_in[here]
        dxv, dzv, dyv = [], [], []
        for f in range(3):
            value = v[f, here]
            slab = slice(f * LZ, (f + 1) * LZ)
            dxv.append(diff_x(v, f, start, x_low[slab], x_high[slab]))
            dzv.append(diff_z(value, face_rows(face, 0, f, here), face_rows(face, 1, f, here), masks))
            dyv.append(diff_y(value, masks))
        p, tau, eta_shrink, yield_f, dlam = return_map(
            dxv, dzv, dyv, [old[i, here] for i in range(6)], eta, pressure[here], cohesion_out[here]
        )
        for i in range(6):
            held[i, here] = tau[i] - p if i < 3 else tau[i]
        pres[here] = p
        total[here] = plastic[here] + dlam
        top_yield = jnp.maximum(top_yield, yield_f)
        top_eta = jnp.maximum(top_eta, eta_shrink)
    store_row(row_out, top_yield, top_eta)
    nothing = jnp.zeros((LZ, NY), F32)
    for start in range(0, ROWS, CHUNK):
        here = slice(start, start + CHUNK)
        for f in range(3):
            part[f, here] = (
                diff_x(held, ALONG_X[f], start, nothing, nothing)
                + diff_z(held[ALONG_Z[f], here], 0.0, 0.0, masks)
                + diff_y(held[ALONG_Y[f], here], masks)
            )
    x_faces(held, ALONG_X, gx)
    z_faces(held, ALONG_Z, fz, slots)
    even = even_z()
    a, b = facing(even, fz[0], fz[1])
    sz_far[0 : 3 * LX], sz_near[0 : 3 * LX] = a, b
    for i in range(3):
        keep(slots, 3 + i, part[i])
        a, b = facing(even, layer(slots, 3 + i, 0), layer(slots, 3 + i, LZ - 1))
        sz_far[(3 + i) * LX : (4 + i) * LX] = a
        sz_near[(3 + i) * LX : (4 + i) * LX] = b
    corners = []
    for z in (0, LZ - 1):
        ends = [held[f, x * LZ + z : x * LZ + z + 1] for f in (XX, XY) for x in (0, LX - 1)]
        corners.append(jnp.concatenate(ends + ends, axis=0))
    a, b = facing(even, *corners)
    sz_far[6 * LX :], sz_near[6 * LX :] = a, b


def residual(held, x_far, x_near, z_far, z_near, out, face):
    x_low, x_high = sides(even_x(), x_far[...], x_near[...])
    z_low, z_high = sides(even_z(), z_far[...], z_near[...])
    for f in range(3):
        rows = slice(f * LX, (f + 1) * LX)
        spread_rows(face, f, z_low[rows], z_high[rows])
    masks = iotas()
    for start in range(0, ROWS, CHUNK):
        here = slice(start, start + CHUNK)
        for f in range(3):
            slab = slice(f * LZ, (f + 1) * LZ)
            out[f, here] = (
                diff_x(held, ALONG_X[f], start, x_low[slab], x_high[slab])
                + diff_z(held[ALONG_Z[f], here], face_rows(face, 0, f, here), face_rows(face, 1, f, here), masks)
                + diff_y(held[ALONG_Y[f], here], masks)
            )


def x_pack_kernel(part, gx, sz_far, sz_near, row, row_out, sx_far, sx_near):
    relay_row(row, row_out)
    low, high = sides(even_z(), sz_far[...], sz_near[...])
    z = lax.broadcasted_iota(jnp.int32, (LZ, NY), 0)
    messages = []
    for e, x in enumerate((0, LX - 1)):
        pieces = [gx[e]]
        for f in range(3):
            below_z, above_z = (h[f * LX + x : f * LX + x + 1] for h in (low, high))
            pieces.append(
                part[f, x * LZ : (x + 1) * LZ]
                - jnp.where(z == 0, below_z * 0.5, 0.0)
                + jnp.where(z == LZ - 1, above_z * 0.5, 0.0)
            )
        ends = []
        for h in (low, high):
            ends += [h[6 * LX + e : 6 * LX + e + 1], h[x : x + 1], h[6 * LX + 2 + e : 6 * LX + 3 + e]]
        pieces.append(jnp.concatenate(ends + ends[:2], axis=0))
        messages.append(jnp.concatenate(pieces, axis=0))
    sx_far[...], sx_near[...] = facing(even_x(), *messages)


def residual_kernel(part, gx, fz, sx_far, sx_near, sz_far, sz_near, out, rx, rz, face):
    x_low, x_high = sides(even_x(), sx_far[...], sx_near[...])
    z_low, z_high = sides(even_z(), sz_far[...], sz_near[...])
    masks = iotas()
    for f in range(3):
        rows = slice(f * LX, (f + 1) * LX)
        spread_rows(face, f, z_low[rows], z_high[rows])
        slab = slice(f * LZ, (f + 1) * LZ)
        for start in range(0, ROWS, CHUNK):
            here = slice(start, start + CHUNK)
            out[f, here] = (
                part[f, here]
                - jnp.where(masks[0], face_rows(face, 0, f, here) * 0.5, 0.0)
                + jnp.where(masks[1], face_rows(face, 1, f, here) * 0.5, 0.0)
            )
        out[f, 0:LZ] = out[f, 0:LZ] - x_low[slab] * 0.5
        out[f, ROWS - LZ : ROWS] = out[f, ROWS - LZ : ROWS] + x_high[slab] * 0.5
    has_low, has_high = place(GX)
    rx[0] = jnp.where(has_low, x_low[3 * LZ : 6 * LZ] + gx[0] * 0.5, 0.0)
    rx[1] = jnp.where(has_high, x_high[3 * LZ : 6 * LZ] - gx[1] * 0.5, 0.0)
    x = lax.broadcasted_iota(jnp.int32, (LX, NY), 0)
    for side, (has, slab, sign) in enumerate(zip(place(GZ), (z_low, z_high), (0.5, -0.5))):
        for f in range(3):
            rows = slice(f * LX, (f + 1) * LX)
            end = 6 * LZ + 3 * side + f
            value = (
                slab[(3 + f) * LX : (4 + f) * LX]
                + fz[side, rows] * sign
                - jnp.where(x == 0, x_low[end : end + 1] * 0.5, 0.0)
                + jnp.where(x == LX - 1, x_high[end : end + 1] * 0.5, 0.0)
            )
            rz[side, rows] = jnp.where(has, value, 0.0)


def last_residual_kernel(held, sx_far, sx_near, sz_far, sz_near, out, face):
    residual(held, sx_far, sx_near, sz_far, sz_near, out, face)


def relay_kernel(gx, sz_far, sz_near, row, row_out, sx_far, sx_near):
    relay_row(row, row_out)
    sx_far[...], sx_near[...] = facing(even_x(), gx[0], gx[1])


def second_kernel(
    v, res, vx, vz, rx, rz, row,
    old, pressure, plastic, eta_in, cohesion,
    stress, pres, total, v_out, held, row_out, gx, sz_far, sz_near,
    face, slots, fz,
):
    top, peak = row_values(row, (0, 1))
    step = 0.125 / peak
    for f in range(3):
        v_out[f] = v[f] + step * res[f]
    x_low, x_high = vx[0] + step * rx[0], vx[1] + step * rx[1]
    z_low, z_high = vz[0] + step * rz[0], vz[1] + step * rz[1]
    for f in range(3):
        rows = slice(f * LX, (f + 1) * LX)
        spread_rows(face, f, z_low[rows], z_high[rows])
    masks = iotas()
    top_yield = jnp.full((CHUNK, NY), -jnp.inf, F32)
    top_eta = jnp.full((CHUNK, NY), -jnp.inf, F32)
    for start in range(0, ROWS, CHUNK):
        here = slice(start, start + CHUNK)
        dxv, dzv, dyv = [], [], []
        for f in range(3):
            value = v_out[f, here]
            slab = slice(f * LZ, (f + 1) * LZ)
            dxv.append(diff_x(v_out, f, start, x_low[slab], x_high[slab]))
            dzv.append(diff_z(value, face_rows(face, 0, f, here), face_rows(face, 1, f, here), masks))
            dyv.append(diff_y(value, masks))
        p, tau, eta_shrink, yield_f, dlam = return_map(
            dxv, dzv, dyv, [old[i, here] for i in range(6)], eta_in[here], pressure[here], cohesion[here]
        )
        for i in range(6):
            stress[i, here] = tau[i]
            held[i, here] = tau[i] - p if i < 3 else tau[i]
        pres[here] = p
        total[here] = plastic[here] + dlam
        top_yield = jnp.maximum(top_yield, yield_f)
        top_eta = jnp.maximum(top_eta, eta_shrink)
    store_row(row_out, top_yield, top_eta, top)
    x_faces(held, ALONG_X, gx)
    z_faces(held, ALONG_Z, fz, slots)
    sz_far[...], sz_near[...] = facing(even_z(), fz[0], fz[1])


def final_kernel(v, res, row, v_out, peaks):
    top, peak, first_top = row_values(row, (0, 1, 2))
    step = 0.125 / peak
    for f in range(3):
        v_out[f] = v[f] + step * res[f]
    peaks[0] = jnp.max(first_top)
    peaks[1] = jnp.max(top)


def per_device(velocity, pressure, stress_old, plastic, viscosity, weak_seed):
    shapes = [a.shape for a in (velocity, pressure, stress_old, plastic)]
    one = (ROWS, NY)
    v = velocity.reshape((3,) + one)
    old = again = stress_old.reshape((6,) + one)
    pressure, plastic, viscosity, weak_seed = (
        a.reshape(one) for a in (pressure, plastic, viscosity, weak_seed)
    )
    three, six = (3,) + one, (6,) + one
    face = pltpu.VMEM((2, 3, 2, ROWS, 128), F32)
    slots = pltpu.VMEM((6, 2, ROWS, 128), F32)
    level_1, level_2 = lax.axis_size(YCORE), lax.axis_size(XZ)
    row_1, row_2 = (level_1, 8, 128), (level_2, 2, 128)
    x_3, z_3, x_9, z_9 = (3 * LZ, NY), (3 * LX, NY), (9 * LZ, NY), (9 * LX, NY)

    dma = pltpu.SemaphoreType.DMA
    x_msgs = call(faces_kernel, [x_9, x_9], [v, plastic], 0, [dma((8,))], None, [HBM, HBM], 60)
    x_msgs = exchange(GX, *x_msgs)
    v, plastic, pressure, old, eta, weak = call(
        load_kernel,
        [three, one, one, six, one, one],
        [v, plastic, pressure, old, viscosity, weak_seed],
        10**5,
        [pltpu.VMEM(one, F32), pltpu.VMEM(one, jnp.int32), dma((6,))],
        None,
        [HBM] * 6,
    )
    along, *z_msgs = call(smooth_x_kernel, [one, z_9, z_9], [v, plastic, *x_msgs], 10**6, [slots])
    z_msgs = exchange(GZ, *z_msgs)
    x_two, z_two, x_full, z_full = (2,) + x_3, (2,) + z_3, (7 * LZ, NY), (6 * LX + 8, NY)
    part, pres, total, cohesion, vx, vz, gx, fz, row, *sent = call(
        first_kernel,
        [three, one, one, one, x_two, z_two, x_two, z_two, row_1, z_full, z_full],
        [v, pressure, old, along, plastic, eta, weak, *x_msgs, *z_msgs],
        10**7,
        [face, slots, pltpu.VMEM(six, F32)],
    )
    row = spread(row, YCORE)
    z_got = exchange(GZ, *sent)
    row, *sent = call(
        x_pack_kernel, [row_2, x_full, x_full], [part, gx, *z_got, row], 10**5
    )
    row = spread(row, XZ)
    x_got = exchange(GX, *sent)
    res, rx, rz = call(
        residual_kernel, [three, x_two, z_two], [part, gx, fz, *x_got, *z_got], 10**6, [face]
    )
    stress, pres, total, v, held, row, gx, *sent = call(
        second_kernel,
        [six, one, one, three, six, row_1, x_two, z_3, z_3],
        [v, res, vx, vz, rx, rz, row, again, pres, total, eta, cohesion],
        10**7,
        [face, slots, pltpu.VMEM(z_two, F32)],
    )
    row = spread(row, YCORE)
    z_got = exchange(GZ, *sent)
    row, *sent = call(relay_kernel, [row_2, x_3, x_3], [gx, *z_got, row], 10**4)
    row = spread(row, XZ)
    x_got = exchange(GX, *sent)
    (res,) = call(last_residual_kernel, [three], [held, *x_got, *z_got], 10**6, [face])
    v, peaks = call(final_kernel, [three, (2,)], [v, res, row], 10**5, (), [VMEM, SMEM])
    outs = [a.reshape(s) for a, s in zip((v, pres, stress, total), shapes)]
    return (*outs, peaks)


def solution(mesh):
    split = Mesh(mesh.devices.reshape(4, 8, 2, 4, 2), ("gx_0", "gx_1", "gx_2", "gz_0", "gz_1"))
    return jax.shard_map(
        per_device,
        mesh=split,
        in_specs=(
            P(None, GX, GZ, None),
            P(GX, GZ, None),
            P(None, GX, GZ, None),
            P(GX, GZ, None),
            P(GX, GZ, None),
            P(GX, GZ, None),
        ),
        out_specs=(
            P(None, GX, GZ, None),
            P(GX, GZ, None),
            P(None, GX, GZ, None),
            P(GX, GZ, None),
            P(),
        ),
        check_vma=False,
    )
```

```python
import math

import jax
import jax.numpy as jnp
from jax import lax
from jax.experimental import pallas as pl
from jax.experimental.pallas import tpu as pltpu
from jax.sharding import Mesh
from jax.sharding import PartitionSpec as P

GX = ("gx_0", "gx_1", "gx_2")
GZ = ("gz_0", "gz_1")
YCORE = ("gx_2", "gz_0", "gz_1")
XZ = ("gx_0", "gx_1")

WEIGHT_TOTAL = sum(math.exp(-(k * k) / 18.0) for k in range(-6, 7))
WEIGHTS = [math.exp(-(k * k) / 18.0) / WEIGHT_TOTAL for k in range(-6, 7)]
SHEAR = 20.0
F32 = jnp.float32
LX, LZ, NY = 16, 8, 256
ROWS = LX * LZ
CHUNK = 16
XX, ZZ, YY, XZ_, XY, ZY = range(6)
ALONG_X = (XX, XZ_, XY)
ALONG_Z = (XZ_, ZZ, ZY)
ALONG_Y = (XY, ZY, YY)
VMEM = pl.BlockSpec(memory_space=pltpu.VMEM)
SMEM = pl.BlockSpec(memory_space=pltpu.SMEM)
HBM = pl.BlockSpec(memory_space=pltpu.HBM)


def call(kernel, outs, operands, flops, scratch=(), out_specs=None, in_specs=None, limit=14):
    size = sum(math.prod(a.shape) * 4 for a in operands)
    size += sum(math.prod(s) * 4 for s in outs)
    return pl.pallas_call(
        kernel,
        out_shape=[jax.ShapeDtypeStruct(s, F32) for s in outs],
        in_specs=in_specs or [VMEM] * len(operands),
        out_specs=out_specs or [VMEM] * len(outs),
        scratch_shapes=list(scratch),
        compiler_params=pltpu.CompilerParams(vmem_limit_bytes=limit * 1024 * 1024),
        cost_estimate=pl.CostEstimate(flops=flops, bytes_accessed=size, transcendentals=0),
    )(*operands)


def pairs(count, first):
    out = []
    for i in range(first, count - 1, 2):
        out += [(i, i + 1), (i + 1, i)]
    return out


def exchange(axis, far, near):
    count = lax.axis_size(axis)
    return (
        lax.ppermute(far, axis, pairs(count, 1)),
        lax.ppermute(near, axis, pairs(count, 0)),
    )


def spread(row, axes):
    return lax.all_to_all(row, axes, 0, 0, tiled=True)


def even_x():
    return lax.axis_index("gx_2") == 0


def even_z():
    return lax.axis_index("gz_1") == 0


def facing(even, first, last):
    return jnp.where(even, first, last), jnp.where(even, last, first)


def sides(even, far, near):
    return jnp.where(even, far, near), jnp.where(even, near, far)


def iotas():
    row = lax.broadcasted_iota(jnp.int32, (CHUNK, NY), 0) % LZ
    col = lax.broadcasted_iota(jnp.int32, (CHUNK, NY), 1)
    return row == 0, row == LZ - 1, col == 0, col == NY - 1


def below(ref, f, start, low):
    if start == 0:
        return jnp.concatenate([low, ref[f, 0 : CHUNK - LZ]], axis=0)
    return ref[f, start - LZ : start - LZ + CHUNK]


def above(ref, f, start, high):
    if start == ROWS - CHUNK:
        return jnp.concatenate([ref[f, start + LZ : ROWS], high], axis=0)
    return ref[f, start + LZ : start + LZ + CHUNK]


def diff_x(ref, f, start, low, high):
    return (above(ref, f, start, high) - below(ref, f, start, low)) * 0.5


def diff_z(value, low, high, masks):
    up = jnp.where(masks[1], high, pltpu.roll(value, CHUNK - 1, 0))
    down = jnp.where(masks[0], low, pltpu.roll(value, 1, 0))
    return (up - down) * 0.5


def diff_y(value, masks):
    up = jnp.where(masks[3], 0.0, pltpu.roll(value, NY - 1, 1))
    down = jnp.where(masks[2], 0.0, pltpu.roll(value, 1, 1))
    return (up - down) * 0.5


def spread_rows(face, f, low, high):
    for h in range(2):
        lanes = slice(h * 128, (h + 1) * 128)
        face[0, f, h, pl.ds(0, LX, stride=LZ), :] = low[:, lanes]
        face[1, f, h, pl.ds(LZ - 1, LX, stride=LZ), :] = high[:, lanes]


def face_rows(face, side, f, here):
    return jnp.concatenate([face[side, f, h, here] for h in range(2)], axis=1)


def keep(slots, f, value):
    for h in range(2):
        slots[f, h] = value[:, h * 128 : (h + 1) * 128]


def layer(slots, f, z):
    return jnp.concatenate([slots[f, h, pl.ds(z, LX, stride=LZ), :] for h in range(2)], axis=1)


def place(axes):
    index, count = 0, 1
    for axis in axes:
        size = lax.axis_size(axis)
        index, count = index * size + lax.axis_index(axis), count * size
    return index > 0, index < count - 1


def x_faces(ref, fields, out):
    for i, f in enumerate(fields):
        out[0, i * LZ : (i + 1) * LZ] = ref[f, 0:LZ]
        out[1, i * LZ : (i + 1) * LZ] = ref[f, ROWS - LZ : ROWS]


def z_faces(ref, fields, out, slots):
    for i, f in enumerate(fields):
        keep(slots, i, ref[f])
        out[0, i * LX : (i + 1) * LX] = layer(slots, i, 0)
        out[1, i * LX : (i + 1) * LX] = layer(slots, i, LZ - 1)


def faces_kernel(v, plastic, x_far, x_near, sem):
    even = even_x()
    for i, (out, low) in enumerate(((x_far, even), (x_near, jnp.logical_not(even)))):
        top = pl.multiple_of(jnp.where(low, 0, ROWS - LZ), LZ)
        deep = pl.multiple_of(jnp.where(low, 0, ROWS - 6 * LZ), LZ)
        copies = [
            pltpu.make_async_copy(
                v.at[f, pl.ds(top, LZ)], out.at[pl.ds(f * LZ, LZ)], sem.at[4 * i + f]
            )
            for f in range(3)
        ]
        copies.append(
            pltpu.make_async_copy(
                plastic.at[pl.ds(deep, 6 * LZ)], out.at[pl.ds(3 * LZ, 6 * LZ)], sem.at[4 * i + 3]
            )
        )
        for copy in copies:
            copy.start()
    for i, out in enumerate((x_far, x_near)):
        for f in range(3):
            rows = pl.ds(f * LZ, LZ)
            pltpu.make_async_copy(v.at[f, pl.ds(0, LZ)], out.at[rows], sem.at[4 * i + f]).wait()
        rows = pl.ds(3 * LZ, 6 * LZ)
        pltpu.make_async_copy(plastic.at[pl.ds(0, 6 * LZ)], out.at[rows], sem.at[4 * i + 3]).wait()


def eta_kernel(viscosity, seed, eta, weak):
    eta[...] = 1.0 / (1.0 / viscosity[...] + 1.0 / SHEAR)
    weak[...] = 1.0 - 0.6 * seed[...].astype(F32)


def store_row(out, top_yield, top_eta, earlier=None):
    a = jnp.max(top_yield, axis=(0, 1), keepdims=True)
    b = jnp.max(top_eta, axis=(0, 1), keepdims=True)
    lane = lax.broadcasted_iota(jnp.int32, (1, 128), 1)
    row = jnp.where(lane == 0, a, b)
    if earlier is not None:
        row = jnp.where(lane == 2, earlier, row)
    out[...] = jnp.broadcast_to(row[None], out.shape)


def relay_row(ref, out):
    row = jnp.max(ref[...], axis=0)[0:1]
    out[...] = jnp.broadcast_to(row[None], out.shape)


def row_values(ref, lanes):
    row = jnp.max(ref[...], axis=0)[0:1]
    lane = lax.broadcasted_iota(jnp.int32, (1, 128), 1)
    return [
        jnp.max(jnp.where(lane == i, row, -jnp.inf), axis=(0, 1), keepdims=True) for i in lanes
    ]


def return_map(dxv, dzv, dyv, old, eta, pres, cohesion):
    div = dxv[0] + dzv[1] + dyv[2]
    pres = pres - 0.25 * div
    third = div / 3.0
    strain = [
        dxv[0] - third,
        dzv[1] - third,
        dyv[2] - third,
        0.5 * (dxv[1] + dzv[0]),
        0.5 * (dxv[2] + dyv[0]),
        0.5 * (dzv[2] + dyv[1]),
    ]
    trial = [2.0 * eta * (e + o / (2.0 * SHEAR)) for e, o in zip(strain, old)]
    tau_ii = jnp.sqrt(
        0.5 * (trial[0] * trial[0] + trial[1] * trial[1] + trial[2] * trial[2])
        + trial[3] * trial[3]
        + trial[4] * trial[4]
        + trial[5] * trial[5]
    )
    yield_f = tau_ii - 0.5 * jnp.maximum(pres, 0.0) - 0.8660254 * cohesion
    dlam = jnp.maximum(yield_f, 0.0) / (eta + 0.5)
    shrink = 1.0 - eta * dlam / jnp.maximum(tau_ii, 0.5)
    return pres, [t * shrink for t in trial], eta * shrink, yield_f, dlam


def partial_residual(held, part, masks):
    nothing = jnp.zeros((LZ, NY), F32)
    for start in range(0, ROWS, CHUNK):
        here = slice(start, start + CHUNK)
        for f in range(3):
            part[f, here] = (
                diff_x(held, ALONG_X[f], start, nothing, nothing)
                + diff_z(held[ALONG_Z[f], here], 0.0, 0.0, masks)
                + diff_y(held[ALONG_Y[f], here], masks)
            )


def whole_residual(part, x_low, x_high, z_low, z_high, face, masks):
    for f in range(3):
        rows = slice(f * LX, (f + 1) * LX)
        spread_rows(face, f, z_low[rows], z_high[rows])
        slab = slice(f * LZ, (f + 1) * LZ)
        for start in range(0, ROWS, CHUNK):
            here = slice(start, start + CHUNK)
            value = (
                part[f, here]
                - jnp.where(masks[0], face_rows(face, 0, f, here) * 0.5, 0.0)
                + jnp.where(masks[1], face_rows(face, 1, f, here) * 0.5, 0.0)
            )
            if start == 0:
                value = jnp.concatenate([value[:LZ] - x_low[slab] * 0.5, value[LZ:]], axis=0)
            if start == ROWS - CHUNK:
                value = jnp.concatenate([value[:LZ], value[LZ:] + x_high[slab] * 0.5], axis=0)
            yield f, here, value


def own_x_kernel(plastic, along):
    for x in range(LX):
        total = None
        for k in range(max(-6, -x), min(6, LX - 1 - x) + 1):
            term = WEIGHTS[k + 6] * plastic[(x + k) * LZ : (x + k + 1) * LZ]
            total = term if total is None else total + term
        along[x * LZ : (x + 1) * LZ] = total


def smooth_x_kernel(v, own, x_far, x_near, along, z_far, z_near, slots):
    low, high = sides(even_x(), x_far[3 * LZ :], x_near[3 * LZ :])
    layers = []
    for x in range(LX):
        total = own[x * LZ : (x + 1) * LZ]
        for j in range(6):
            if x + 6 - j <= 6:
                total = total + WEIGHTS[j - x] * low[j * LZ : (j + 1) * LZ]
            if LX + j - x <= 6:
                total = total + WEIGHTS[LX + j - x + 6] * high[j * LZ : (j + 1) * LZ]
        layers.append(total)
    total = jnp.concatenate(layers, axis=0)
    along[...] = total
    keep(slots, 3, total)
    even = even_z()
    for i in range(9):
        if i < 3:
            keep(slots, i, v[i])
            a, b = facing(even, layer(slots, i, 0), layer(slots, i, LZ - 1))
        else:
            a, b = facing(even, layer(slots, 3, i - 3), layer(slots, 3, i - 1))
        z_far[i * LX : (i + 1) * LX] = a
        z_near[i * LX : (i + 1) * LX] = b


def gauss(gap, inside):
    g = gap.astype(F32)
    return jnp.where(inside & (jnp.abs(gap) <= 6), jnp.exp(g * g * (-1.0 / 18.0)) / WEIGHT_TOTAL, 0.0)


def dot(a, b):
    return jnp.dot(a, b, precision=lax.Precision.HIGHEST, preferred_element_type=F32)


def first_kernel(
    v, pressure, old, along, plastic, eta_in, weak, x_far, x_near, z_far, z_near,
    part, pres, total, cohesion_out, vx_out, vz_out, gx, fz, row_out, sz_far, sz_near,
    face, slots, held,
):
    low, high = sides(even_z(), z_far[...], z_near[...])
    r = lax.broadcasted_iota(jnp.int32, (ROWS, ROWS), 0)
    c = lax.broadcasted_iota(jnp.int32, (ROWS, ROWS), 1)
    own = gauss(c % LZ - r % LZ, c // LZ == r // LZ)
    r = lax.broadcasted_iota(jnp.int32, (ROWS, 6 * LX), 0)
    c = lax.broadcasted_iota(jnp.int32, (ROWS, 6 * LX), 1)
    same = c % LX == r // LZ
    from_low = gauss(c // LX - 6 - r % LZ, same)
    from_high = gauss(c // LX + LZ - r % LZ, same)
    along_z = dot(own, along[...]) + dot(from_low, low[3 * LX :]) + dot(from_high, high[3 * LX :])
    r = lax.broadcasted_iota(jnp.int32, (NY, NY), 0)
    c = lax.broadcasted_iota(jnp.int32, (NY, NY), 1)
    smoothed = dot(along_z, gauss(r - c, r >= 0))
    cohesion_out[...] = weak[...] / (1.0 + 2.0 * smoothed)
    for f in range(3):
        spread_rows(face, f, low[f * LX : (f + 1) * LX], high[f * LX : (f + 1) * LX])
    x_low, x_high = sides(even_x(), x_far[0 : 3 * LZ], x_near[0 : 3 * LZ])
    vx_out[0], vx_out[1] = x_low, x_high
    vz_out[0], vz_out[1] = low[0 : 3 * LX], high[0 : 3 * LX]
    masks = iotas()
    top_yield = jnp.full((CHUNK, NY), -jnp.inf, F32)
    top_eta = jnp.full((CHUNK, NY), -jnp.inf, F32)
    for start in range(0, ROWS, CHUNK):
        here = slice(start, start + CHUNK)
        eta = eta_in[here]
        dxv, dzv, dyv = [], [], []
        for f in range(3):
            value = v[f, here]
            slab = slice(f * LZ, (f + 1) * LZ)
            dxv.append(diff_x(v, f, start, x_low[slab], x_high[slab]))
            dzv.append(diff_z(value, face_rows(face, 0, f, here), face_rows(face, 1, f, here), masks))
            dyv.append(diff_y(value, masks))
        p, tau, eta_shrink, yield_f, dlam = return_map(
            dxv, dzv, dyv, [old[i, here] for i in range(6)], eta, pressure[here], cohesion_out[here]
        )
        for i in range(6):
            held[i, here] = tau[i] - p if i < 3 else tau[i]
        pres[here] = p
        total[here] = plastic[here] + dlam
        top_yield = jnp.maximum(top_yield, yield_f)
        top_eta = jnp.maximum(top_eta, eta_shrink)
    store_row(row_out, top_yield, top_eta)
    partial_residual(held, part, masks)
    x_faces(held, ALONG_X, gx)
    z_faces(held, ALONG_Z, fz, slots)
    even = even_z()
    a, b = facing(even, fz[0], fz[1])
    sz_far[0 : 3 * LX], sz_near[0 : 3 * LX] = a, b
    for i in range(3):
        keep(slots, 3 + i, part[i])
        a, b = facing(even, layer(slots, 3 + i, 0), layer(slots, 3 + i, LZ - 1))
        sz_far[(3 + i) * LX : (4 + i) * LX] = a
        sz_near[(3 + i) * LX : (4 + i) * LX] = b
    corners = []
    for z in (0, LZ - 1):
        ends = [held[f, x * LZ + z : x * LZ + z + 1] for f in (XX, XY) for x in (0, LX - 1)]
        corners.append(jnp.concatenate(ends + ends, axis=0))
    a, b = facing(even, *corners)
    sz_far[6 * LX :], sz_near[6 * LX :] = a, b


def x_pack_kernel(part, gx, sz_far, sz_near, row, row_out, sx_far, sx_near):
    relay_row(row, row_out)
    low, high = sides(even_z(), sz_far[...], sz_near[...])
    z = lax.broadcasted_iota(jnp.int32, (LZ, NY), 0)
    messages = []
    for e, x in enumerate((0, LX - 1)):
        pieces = [gx[e]]
        for f in range(3):
            below_z, above_z = (h[f * LX + x : f * LX + x + 1] for h in (low, high))
            pieces.append(
                part[f, x * LZ : (x + 1) * LZ]
                - jnp.where(z == 0, below_z * 0.5, 0.0)
                + jnp.where(z == LZ - 1, above_z * 0.5, 0.0)
            )
        ends = []
        for h in (low, high):
            ends += [h[6 * LX + e : 6 * LX + e + 1], h[x : x + 1], h[6 * LX + 2 + e : 6 * LX + 3 + e]]
        pieces.append(jnp.concatenate(ends + ends[:2], axis=0))
        messages.append(jnp.concatenate(pieces, axis=0))
    sx_far[...], sx_near[...] = facing(even_x(), *messages)


def residual_kernel(part, gx, fz, sx_far, sx_near, sz_far, sz_near, out, rx, rz, face):
    x_low, x_high = sides(even_x(), sx_far[...], sx_near[...])
    z_low, z_high = sides(even_z(), sz_far[...], sz_near[...])
    for f, here, value in whole_residual(part, x_low, x_high, z_low, z_high, face, iotas()):
        out[f, here] = value
    has_low, has_high = place(GX)
    rx[0] = jnp.where(has_low, x_low[3 * LZ : 6 * LZ] + gx[0] * 0.5, 0.0)
    rx[1] = jnp.where(has_high, x_high[3 * LZ : 6 * LZ] - gx[1] * 0.5, 0.0)
    x = lax.broadcasted_iota(jnp.int32, (LX, NY), 0)
    for side, (has, slab, sign) in enumerate(zip(place(GZ), (z_low, z_high), (0.5, -0.5))):
        for f in range(3):
            rows = slice(f * LX, (f + 1) * LX)
            end = 6 * LZ + 3 * side + f
            value = (
                slab[(3 + f) * LX : (4 + f) * LX]
                + fz[side, rows] * sign
                - jnp.where(x == 0, x_low[end : end + 1] * 0.5, 0.0)
                + jnp.where(x == LX - 1, x_high[end : end + 1] * 0.5, 0.0)
            )
            rz[side, rows] = jnp.where(has, value, 0.0)


def relay_kernel(gx, sz_far, sz_near, row, row_out, sx_far, sx_near):
    relay_row(row, row_out)
    sx_far[...], sx_near[...] = facing(even_x(), gx[0], gx[1])


def second_kernel(
    v, res, vx, vz, rx, rz, row,
    old, pressure, plastic, eta_in, cohesion,
    stress, pres, total, v_out, part, row_out, gx, sz_far, sz_near,
    face, slots, fz, held,
):
    top, peak = row_values(row, (0, 1))
    step = 0.125 / peak
    for f in range(3):
        v_out[f] = v[f] + step * res[f]
    x_low, x_high = vx[0] + step * rx[0], vx[1] + step * rx[1]
    z_low, z_high = vz[0] + step * rz[0], vz[1] + step * rz[1]
    for f in range(3):
        rows = slice(f * LX, (f + 1) * LX)
        spread_rows(face, f, z_low[rows], z_high[rows])
    masks = iotas()
    top_yield = jnp.full((CHUNK, NY), -jnp.inf, F32)
    top_eta = jnp.full((CHUNK, NY), -jnp.inf, F32)
    for start in range(0, ROWS, CHUNK):
        here = slice(start, start + CHUNK)
        dxv, dzv, dyv = [], [], []
        for f in range(3):
            value = v_out[f, here]
            slab = slice(f * LZ, (f + 1) * LZ)
            dxv.append(diff_x(v_out, f, start, x_low[slab], x_high[slab]))
            dzv.append(diff_z(value, face_rows(face, 0, f, here), face_rows(face, 1, f, here), masks))
            dyv.append(diff_y(value, masks))
        p, tau, eta_shrink, yield_f, dlam = return_map(
            dxv, dzv, dyv, [old[i, here] for i in range(6)], eta_in[here], pressure[here], cohesion[here]
        )
        for i in range(6):
            stress[i, here] = tau[i]
            held[i, here] = tau[i] - p if i < 3 else tau[i]
        pres[here] = p
        total[here] = plastic[here] + dlam
        top_yield = jnp.maximum(top_yield, yield_f)
        top_eta = jnp.maximum(top_eta, eta_shrink)
    store_row(row_out, top_yield, top_eta, top)
    partial_residual(held, part, masks)
    x_faces(held, ALONG_X, gx)
    z_faces(held, ALONG_Z, fz, slots)
    sz_far[...], sz_near[...] = facing(even_z(), fz[0], fz[1])


def final_kernel(v, part, sx_far, sx_near, sz_far, sz_near, row, v_out, peaks, face):
    top, peak, first_top = row_values(row, (0, 1, 2))
    step = 0.125 / peak
    slabs = sides(even_x(), sx_far[...], sx_near[...]) + sides(even_z(), sz_far[...], sz_near[...])
    for f, here, value in whole_residual(part, *slabs, face, iotas()):
        v_out[f, here] = v[f, here] + step * value
    peaks[0] = jnp.max(first_top)
    peaks[1] = jnp.max(top)


def per_device(velocity, pressure, stress_old, plastic, viscosity, weak_seed):
    shapes = [a.shape for a in (velocity, pressure, stress_old, plastic)]
    one = (ROWS, NY)
    v = velocity.reshape((3,) + one)
    old = stress_old.reshape((6,) + one)
    pressure, plastic, viscosity, weak_seed = (
        a.reshape(one) for a in (pressure, plastic, viscosity, weak_seed)
    )
    three, six = (3,) + one, (6,) + one
    face = pltpu.VMEM((2, 3, 2, ROWS, 128), F32)
    slots = pltpu.VMEM((6, 2, ROWS, 128), F32)
    level_1, level_2 = lax.axis_size(YCORE), lax.axis_size(XZ)
    row_1, row_2 = (level_1, 8, 128), (level_2, 2, 128)
    x_3, z_3, x_9, z_9 = (3 * LZ, NY), (3 * LX, NY), (9 * LZ, NY), (9 * LX, NY)

    dma = pltpu.SemaphoreType.DMA
    x_msgs = call(faces_kernel, [x_9, x_9], [v, plastic], 0, [dma((8,))], [HBM, HBM], [HBM, HBM], 60)
    x_msgs = exchange(GX, *x_msgs)
    eta, weak = call(eta_kernel, [one, one], [viscosity, weak_seed], 10**5)
    (along,) = call(own_x_kernel, [one], [plastic], 10**6)
    along, *z_msgs = call(smooth_x_kernel, [one, z_9, z_9], [v, along, *x_msgs], 10**6, [slots])
    z_msgs = exchange(GZ, *z_msgs)
    x_two, z_two, x_full, z_full = (2,) + x_3, (2,) + z_3, (7 * LZ, NY), (6 * LX + 8, NY)
    part, pres, total, cohesion, vx, vz, gx, fz, row, *sent = call(
        first_kernel,
        [three, one, one, one, x_two, z_two, x_two, z_two, row_1, z_full, z_full],
        [v, pressure, old, along, plastic, eta, weak, *x_msgs, *z_msgs],
        10**7,
        [face, slots, pltpu.VMEM(six, F32)],
    )
    row = spread(row, YCORE)
    z_got = exchange(GZ, *sent)
    row, *sent = call(
        x_pack_kernel, [row_2, x_full, x_full], [part, gx, *z_got, row], 10**5
    )
    row = spread(row, XZ)
    x_got = exchange(GX, *sent)
    res, rx, rz = call(
        residual_kernel, [three, x_two, z_two], [part, gx, fz, *x_got, *z_got], 10**6, [face]
    )
    stress, pres, total, v, part, row, gx, *sent = call(
        second_kernel,
        [six, one, one, three, three, row_1, x_two, z_3, z_3],
        [v, res, vx, vz, rx, rz, row, old, pres, total, eta, cohesion],
        10**7,
        [face, slots, pltpu.VMEM(z_two, F32), pltpu.VMEM(six, F32)],
    )
    row = spread(row, YCORE)
    z_got = exchange(GZ, *sent)
    row, *sent = call(relay_kernel, [row_2, x_3, x_3], [gx, *z_got, row], 10**4)
    row = spread(row, XZ)
    x_got = exchange(GX, *sent)
    v, peaks = call(
        final_kernel,
        [three, (2,)],
        [v, part, *x_got, *z_got, row],
        10**6,
        [face],
        [VMEM, SMEM],
    )
    outs = [a.reshape(s) for a, s in zip((v, pres, stress, total), shapes)]
    return (*outs, peaks)


def solution(mesh):
    split = Mesh(mesh.devices.reshape(4, 8, 2, 4, 2), ("gx_0", "gx_1", "gx_2", "gz_0", "gz_1"))
    return jax.shard_map(
        per_device,
        mesh=split,
        in_specs=(
            P(None, GX, GZ, None),
            P(GX, GZ, None),
            P(None, GX, GZ, None),
            P(GX, GZ, None),
            P(GX, GZ, None),
            P(GX, GZ, None),
        ),
        out_specs=(
            P(None, GX, GZ, None),
            P(GX, GZ, None),
            P(None, GX, GZ, None),
            P(GX, GZ, None),
            P(),
        ),
        check_vma=False,
    )
```

```python
import math

import jax
import jax.numpy as jnp
from jax import lax
from jax.experimental import pallas as pl
from jax.experimental.pallas import tpu as pltpu
from jax.sharding import Mesh
from jax.sharding import PartitionSpec as P

GX = ("gx_0", "gx_1", "gx_2")
GZ = ("gz_0", "gz_1")
YCORE = ("gx_2", "gz_0", "gz_1")
XZ = ("gx_0", "gx_1")

WEIGHT_TOTAL = sum(math.exp(-(k * k) / 18.0) for k in range(-6, 7))
WEIGHTS = [math.exp(-(k * k) / 18.0) / WEIGHT_TOTAL for k in range(-6, 7)]
SHEAR = 20.0
F32 = jnp.float32
LX, LZ, NY = 16, 8, 256
ROWS = LX * LZ
CHUNK = 16
XX, ZZ, YY, XZ_, XY, ZY = range(6)
ALONG_X = (XX, XZ_, XY)
ALONG_Z = (XZ_, ZZ, ZY)
ALONG_Y = (XY, ZY, YY)
VMEM = pl.BlockSpec(memory_space=pltpu.VMEM)
SMEM = pl.BlockSpec(memory_space=pltpu.SMEM)
HBM = pl.BlockSpec(memory_space=pltpu.HBM)


def call(kernel, outs, operands, flops, scratch=(), out_specs=None, in_specs=None, limit=14):
    size = sum(math.prod(a.shape) * 4 for a in operands)
    size += sum(math.prod(s) * 4 for s in outs)
    return pl.pallas_call(
        kernel,
        out_shape=[jax.ShapeDtypeStruct(s, F32) for s in outs],
        in_specs=in_specs or [VMEM] * len(operands),
        out_specs=out_specs or [VMEM] * len(outs),
        scratch_shapes=list(scratch),
        compiler_params=pltpu.CompilerParams(vmem_limit_bytes=limit * 1024 * 1024),
        cost_estimate=pl.CostEstimate(flops=flops, bytes_accessed=size, transcendentals=0),
    )(*operands)


def pairs(count, first):
    out = []
    for i in range(first, count - 1, 2):
        out += [(i, i + 1), (i + 1, i)]
    return out


def exchange(axis, far, near):
    count = lax.axis_size(axis)
    return (
        lax.ppermute(far, axis, pairs(count, 1)),
        lax.ppermute(near, axis, pairs(count, 0)),
    )


def spread(row, axes):
    return lax.all_to_all(row, axes, 0, 0, tiled=True)


def even_x():
    return lax.axis_index("gx_2") == 0


def even_z():
    return lax.axis_index("gz_1") == 0


def facing(even, first, last):
    return jnp.where(even, first, last), jnp.where(even, last, first)


def sides(even, far, near):
    return jnp.where(even, far, near), jnp.where(even, near, far)


def iotas():
    row = lax.broadcasted_iota(jnp.int32, (CHUNK, NY), 0) % LZ
    col = lax.broadcasted_iota(jnp.int32, (CHUNK, NY), 1)
    return row == 0, row == LZ - 1, col == 0, col == NY - 1


def below(ref, f, start, low):
    if start == 0:
        return jnp.concatenate([low, ref[f, 0 : CHUNK - LZ]], axis=0)
    return ref[f, start - LZ : start - LZ + CHUNK]


def above(ref, f, start, high):
    if start == ROWS - CHUNK:
        return jnp.concatenate([ref[f, start + LZ : ROWS], high], axis=0)
    return ref[f, start + LZ : start + LZ + CHUNK]


def diff_x(ref, f, start, low, high):
    return (above(ref, f, start, high) - below(ref, f, start, low)) * 0.5


def diff_z(value, low, high, masks):
    up = jnp.where(masks[1], high, pltpu.roll(value, CHUNK - 1, 0))
    down = jnp.where(masks[0], low, pltpu.roll(value, 1, 0))
    return (up - down) * 0.5


def diff_y(value, masks):
    up = jnp.where(masks[3], 0.0, pltpu.roll(value, NY - 1, 1))
    down = jnp.where(masks[2], 0.0, pltpu.roll(value, 1, 1))
    return (up - down) * 0.5


def spread_rows(face, f, low, high):
    for h in range(2):
        lanes = slice(h * 128, (h + 1) * 128)
        face[0, f, h, pl.ds(0, LX, stride=LZ), :] = low[:, lanes]
        face[1, f, h, pl.ds(LZ - 1, LX, stride=LZ), :] = high[:, lanes]


def face_rows(face, side, f, here):
    return jnp.concatenate([face[side, f, h, here] for h in range(2)], axis=1)


def keep(slots, f, value):
    for h in range(2):
        slots[f, h] = value[:, h * 128 : (h + 1) * 128]


def layer(slots, f, z):
    return jnp.concatenate([slots[f, h, pl.ds(z, LX, stride=LZ), :] for h in range(2)], axis=1)


def place(axes):
    index, count = 0, 1
    for axis in axes:
        size = lax.axis_size(axis)
        index, count = index * size + lax.axis_index(axis), count * size
    return index > 0, index < count - 1


def x_faces(ref, fields, out):
    for i, f in enumerate(fields):
        out[0, i * LZ : (i + 1) * LZ] = ref[f, 0:LZ]
        out[1, i * LZ : (i + 1) * LZ] = ref[f, ROWS - LZ : ROWS]


def z_faces(ref, fields, out, slots):
    for i, f in enumerate(fields):
        keep(slots, i, ref[f])
        out[0, i * LX : (i + 1) * LX] = layer(slots, i, 0)
        out[1, i * LX : (i + 1) * LX] = layer(slots, i, LZ - 1)


def faces_kernel(v, plastic, x_far, x_near, sem):
    even = even_x()
    for i, (out, low) in enumerate(((x_far, even), (x_near, jnp.logical_not(even)))):
        top = pl.multiple_of(jnp.where(low, 0, ROWS - LZ), LZ)
        deep = pl.multiple_of(jnp.where(low, 0, ROWS - 6 * LZ), LZ)
        copies = [
            pltpu.make_async_copy(
                v.at[f, pl.ds(top, LZ)], out.at[pl.ds(f * LZ, LZ)], sem.at[4 * i + f]
            )
            for f in range(3)
        ]
        copies.append(
            pltpu.make_async_copy(
                plastic.at[pl.ds(deep, 6 * LZ)], out.at[pl.ds(3 * LZ, 6 * LZ)], sem.at[4 * i + 3]
            )
        )
        for copy in copies:
            copy.start()
    for i, out in enumerate((x_far, x_near)):
        for f in range(3):
            rows = pl.ds(f * LZ, LZ)
            pltpu.make_async_copy(v.at[f, pl.ds(0, LZ)], out.at[rows], sem.at[4 * i + f]).wait()
        rows = pl.ds(3 * LZ, 6 * LZ)
        pltpu.make_async_copy(plastic.at[pl.ds(0, 6 * LZ)], out.at[rows], sem.at[4 * i + 3]).wait()


def store_row(out, top_yield, top_eta, earlier=None):
    a = jnp.max(top_yield, axis=(0, 1), keepdims=True)
    b = jnp.max(top_eta, axis=(0, 1), keepdims=True)
    lane = lax.broadcasted_iota(jnp.int32, (1, 128), 1)
    row = jnp.where(lane == 0, a, b)
    if earlier is not None:
        row = jnp.where(lane == 2, earlier, row)
    out[...] = jnp.broadcast_to(row[None], out.shape)


def relay_row(ref, out):
    row = jnp.max(ref[...], axis=0)[0:1]
    out[...] = jnp.broadcast_to(row[None], out.shape)


def row_values(ref, lanes):
    row = jnp.max(ref[...], axis=0)[0:1]
    lane = lax.broadcasted_iota(jnp.int32, (1, 128), 1)
    return [
        jnp.max(jnp.where(lane == i, row, -jnp.inf), axis=(0, 1), keepdims=True) for i in lanes
    ]


def return_map(dxv, dzv, dyv, old, eta, pres, cohesion):
    div = dxv[0] + dzv[1] + dyv[2]
    pres = pres - 0.25 * div
    third = div / 3.0
    strain = [
        dxv[0] - third,
        dzv[1] - third,
        dyv[2] - third,
        0.5 * (dxv[1] + dzv[0]),
        0.5 * (dxv[2] + dyv[0]),
        0.5 * (dzv[2] + dyv[1]),
    ]
    trial = [2.0 * eta * (e + o / (2.0 * SHEAR)) for e, o in zip(strain, old)]
    tau_ii = jnp.sqrt(
        0.5 * (trial[0] * trial[0] + trial[1] * trial[1] + trial[2] * trial[2])
        + trial[3] * trial[3]
        + trial[4] * trial[4]
        + trial[5] * trial[5]
    )
    yield_f = tau_ii - 0.5 * jnp.maximum(pres, 0.0) - 0.8660254 * cohesion
    dlam = jnp.maximum(yield_f, 0.0) / (eta + 0.5)
    shrink = 1.0 - eta * dlam / jnp.maximum(tau_ii, 0.5)
    return pres, [t * shrink for t in trial], eta * shrink, yield_f, dlam


def partial_residual(held, part, masks):
    nothing = jnp.zeros((LZ, NY), F32)
    for start in range(0, ROWS, CHUNK):
        here = slice(start, start + CHUNK)
        for f in range(3):
            part[f, here] = (
                diff_x(held, ALONG_X[f], start, nothing, nothing)
                + diff_z(held[ALONG_Z[f], here], 0.0, 0.0, masks)
                + diff_y(held[ALONG_Y[f], here], masks)
            )


def whole_residual(part, x_low, x_high, z_low, z_high, face, masks):
    for f in range(3):
        rows = slice(f * LX, (f + 1) * LX)
        spread_rows(face, f, z_low[rows], z_high[rows])
        slab = slice(f * LZ, (f + 1) * LZ)
        for start in range(0, ROWS, CHUNK):
            here = slice(start, start + CHUNK)
            value = (
                part[f, here]
                - jnp.where(masks[0], face_rows(face, 0, f, here) * 0.5, 0.0)
                + jnp.where(masks[1], face_rows(face, 1, f, here) * 0.5, 0.0)
            )
            if start == 0:
                value = jnp.concatenate([value[:LZ] - x_low[slab] * 0.5, value[LZ:]], axis=0)
            if start == ROWS - CHUNK:
                value = jnp.concatenate([value[:LZ], value[LZ:] + x_high[slab] * 0.5], axis=0)
            yield f, here, value


def own_x_kernel(plastic, along):
    for x in range(LX):
        total = None
        for k in range(max(-6, -x), min(6, LX - 1 - x) + 1):
            term = WEIGHTS[k + 6] * plastic[(x + k) * LZ : (x + k + 1) * LZ]
            total = term if total is None else total + term
        along[x * LZ : (x + 1) * LZ] = total


def smooth_x_kernel(v, own, x_far, x_near, along, z_far, z_near, slots):
    low, high = sides(even_x(), x_far[3 * LZ :], x_near[3 * LZ :])
    layers = []
    for x in range(LX):
        total = own[x * LZ : (x + 1) * LZ]
        for j in range(6):
            if x + 6 - j <= 6:
                total = total + WEIGHTS[j - x] * low[j * LZ : (j + 1) * LZ]
            if LX + j - x <= 6:
                total = total + WEIGHTS[LX + j - x + 6] * high[j * LZ : (j + 1) * LZ]
        layers.append(total)
    total = jnp.concatenate(layers, axis=0)
    along[...] = total
    keep(slots, 3, total)
    even = even_z()
    for i in range(9):
        if i < 3:
            keep(slots, i, v[i])
            a, b = facing(even, layer(slots, i, 0), layer(slots, i, LZ - 1))
        else:
            a, b = facing(even, layer(slots, 3, i - 3), layer(slots, 3, i - 1))
        z_far[i * LX : (i + 1) * LX] = a
        z_near[i * LX : (i + 1) * LX] = b


def gauss(gap, inside):
    g = gap.astype(F32)
    return jnp.where(inside & (jnp.abs(gap) <= 6), jnp.exp(g * g * (-1.0 / 18.0)) / WEIGHT_TOTAL, 0.0)


def own_kernel(along, viscosity, seed, eta, weak, own, from_z, along_y):
    eta[...] = 1.0 / (1.0 / viscosity[...] + 1.0 / SHEAR)
    weak[...] = 1.0 - 0.6 * seed[...].astype(F32)
    r = lax.broadcasted_iota(jnp.int32, (ROWS, ROWS), 0)
    c = lax.broadcasted_iota(jnp.int32, (ROWS, ROWS), 1)
    own_z = gauss(c % LZ - r % LZ, c // LZ == r // LZ)
    r = lax.broadcasted_iota(jnp.int32, (ROWS, NY), 0)
    c = lax.broadcasted_iota(jnp.int32, (ROWS, NY), 1)
    j = c // LX
    from_z[...] = gauss(jnp.where(j < 6, j - 6, j - 6 + LZ) - r % LZ, c % LX == r // LZ)
    r = lax.broadcasted_iota(jnp.int32, (NY, NY), 0)
    c = lax.broadcasted_iota(jnp.int32, (NY, NY), 1)
    along_y[...] = gauss(r - c, r >= 0)
    own[...] = dot(dot(own_z, along[...]), along_y[...])


def dot(a, b):
    return jnp.dot(a, b, precision=lax.Precision.HIGHEST, preferred_element_type=F32)


def first_kernel(
    v, pressure, old, plastic, eta_in, weak, own, from_z, along_y, x_far, x_near, z_far, z_near,
    part, pres, total, cohesion_out, vx_out, vz_out, gx, fz, row_out, sz_far, sz_near,
    face, slots, held,
):
    low, high = sides(even_z(), z_far[...], z_near[...])
    beside = jnp.concatenate([low[3 * LX :], high[3 * LX :]], axis=0)
    smoothed = own[...] + dot(dot(from_z[:, : 12 * LX], beside), along_y[...])
    cohesion_out[...] = weak[...] / (1.0 + 2.0 * smoothed)
    for f in range(3):
        spread_rows(face, f, low[f * LX : (f + 1) * LX], high[f * LX : (f + 1) * LX])
    x_low, x_high = sides(even_x(), x_far[0 : 3 * LZ], x_near[0 : 3 * LZ])
    vx_out[0], vx_out[1] = x_low, x_high
    vz_out[0], vz_out[1] = low[0 : 3 * LX], high[0 : 3 * LX]
    masks = iotas()
    top_yield = jnp.full((CHUNK, NY), -jnp.inf, F32)
    top_eta = jnp.full((CHUNK, NY), -jnp.inf, F32)
    for start in range(0, ROWS, CHUNK):
        here = slice(start, start + CHUNK)
        eta = eta_in[here]
        dxv, dzv, dyv = [], [], []
        for f in range(3):
            value = v[f, here]
            slab = slice(f * LZ, (f + 1) * LZ)
            dxv.append(diff_x(v, f, start, x_low[slab], x_high[slab]))
            dzv.append(diff_z(value, face_rows(face, 0, f, here), face_rows(face, 1, f, here), masks))
            dyv.append(diff_y(value, masks))
        p, tau, eta_shrink, yield_f, dlam = return_map(
            dxv, dzv, dyv, [old[i, here] for i in range(6)], eta, pressure[here], cohesion_out[here]
        )
        for i in range(6):
            held[i, here] = tau[i] - p if i < 3 else tau[i]
        pres[here] = p
        total[here] = plastic[here] + dlam
        top_yield = jnp.maximum(top_yield, yield_f)
        top_eta = jnp.maximum(top_eta, eta_shrink)
    store_row(row_out, top_yield, top_eta)
    partial_residual(held, part, masks)
    x_faces(held, ALONG_X, gx)
    z_faces(held, ALONG_Z, fz, slots)
    even = even_z()
    a, b = facing(even, fz[0], fz[1])
    sz_far[0 : 3 * LX], sz_near[0 : 3 * LX] = a, b
    for i in range(3):
        keep(slots, 3 + i, part[i])
        a, b = facing(even, layer(slots, 3 + i, 0), layer(slots, 3 + i, LZ - 1))
        sz_far[(3 + i) * LX : (4 + i) * LX] = a
        sz_near[(3 + i) * LX : (4 + i) * LX] = b
    corners = []
    for z in (0, LZ - 1):
        ends = [held[f, x * LZ + z : x * LZ + z + 1] for f in (XX, XY) for x in (0, LX - 1)]
        corners.append(jnp.concatenate(ends + ends, axis=0))
    a, b = facing(even, *corners)
    sz_far[6 * LX :], sz_near[6 * LX :] = a, b


def x_pack_kernel(part, gx, sz_far, sz_near, row, row_out, sx_far, sx_near):
    relay_row(row, row_out)
    low, high = sides(even_z(), sz_far[...], sz_near[...])
    z = lax.broadcasted_iota(jnp.int32, (LZ, NY), 0)
    messages = []
    for e, x in enumerate((0, LX - 1)):
        pieces = [gx[e]]
        for f in range(3):
            below_z, above_z = (h[f * LX + x : f * LX + x + 1] for h in (low, high))
            pieces.append(
                part[f, x * LZ : (x + 1) * LZ]
                - jnp.where(z == 0, below_z * 0.5, 0.0)
                + jnp.where(z == LZ - 1, above_z * 0.5, 0.0)
            )
        ends = []
        for h in (low, high):
            ends += [h[6 * LX + e : 6 * LX + e + 1], h[x : x + 1], h[6 * LX + 2 + e : 6 * LX + 3 + e]]
        pieces.append(jnp.concatenate(ends + ends[:2], axis=0))
        messages.append(jnp.concatenate(pieces, axis=0))
    sx_far[...], sx_near[...] = facing(even_x(), *messages)


def residual_kernel(part, gx, fz, sx_far, sx_near, sz_far, sz_near, out, rx, rz, face):
    x_low, x_high = sides(even_x(), sx_far[...], sx_near[...])
    z_low, z_high = sides(even_z(), sz_far[...], sz_near[...])
    for f, here, value in whole_residual(part, x_low, x_high, z_low, z_high, face, iotas()):
        out[f, here] = value
    has_low, has_high = place(GX)
    rx[0] = jnp.where(has_low, x_low[3 * LZ : 6 * LZ] + gx[0] * 0.5, 0.0)
    rx[1] = jnp.where(has_high, x_high[3 * LZ : 6 * LZ] - gx[1] * 0.5, 0.0)
    x = lax.broadcasted_iota(jnp.int32, (LX, NY), 0)
    for side, (has, slab, sign) in enumerate(zip(place(GZ), (z_low, z_high), (0.5, -0.5))):
        for f in range(3):
            rows = slice(f * LX, (f + 1) * LX)
            end = 6 * LZ + 3 * side + f
            value = (
                slab[(3 + f) * LX : (4 + f) * LX]
                + fz[side, rows] * sign
                - jnp.where(x == 0, x_low[end : end + 1] * 0.5, 0.0)
                + jnp.where(x == LX - 1, x_high[end : end + 1] * 0.5, 0.0)
            )
            rz[side, rows] = jnp.where(has, value, 0.0)


def relay_kernel(gx, sz_far, sz_near, row, row_out, sx_far, sx_near):
    relay_row(row, row_out)
    sx_far[...], sx_near[...] = facing(even_x(), gx[0], gx[1])


def second_kernel(
    v, res, vx, vz, rx, rz, row,
    old, pressure, plastic, eta_in, cohesion,
    stress, pres, total, v_out, part, row_out, gx, sz_far, sz_near,
    face, slots, fz, held,
):
    top, peak = row_values(row, (0, 1))
    step = 0.125 / peak
    for f in range(3):
        v_out[f] = v[f] + step * res[f]
    x_low, x_high = vx[0] + step * rx[0], vx[1] + step * rx[1]
    z_low, z_high = vz[0] + step * rz[0], vz[1] + step * rz[1]
    for f in range(3):
        rows = slice(f * LX, (f + 1) * LX)
        spread_rows(face, f, z_low[rows], z_high[rows])
    masks = iotas()
    top_yield = jnp.full((CHUNK, NY), -jnp.inf, F32)
    top_eta = jnp.full((CHUNK, NY), -jnp.inf, F32)
    for start in range(0, ROWS, CHUNK):
        here = slice(start, start + CHUNK)
        dxv, dzv, dyv = [], [], []
        for f in range(3):
            value = v_out[f, here]
            slab = slice(f * LZ, (f + 1) * LZ)
            dxv.append(diff_x(v_out, f, start, x_low[slab], x_high[slab]))
            dzv.append(diff_z(value, face_rows(face, 0, f, here), face_rows(face, 1, f, here), masks))
            dyv.append(diff_y(value, masks))
        p, tau, eta_shrink, yield_f, dlam = return_map(
            dxv, dzv, dyv, [old[i, here] for i in range(6)], eta_in[here], pressure[here], cohesion[here]
        )
        for i in range(6):
            stress[i, here] = tau[i]
            held[i, here] = tau[i] - p if i < 3 else tau[i]
        pres[here] = p
        total[here] = plastic[here] + dlam
        top_yield = jnp.maximum(top_yield, yield_f)
        top_eta = jnp.maximum(top_eta, eta_shrink)
    store_row(row_out, top_yield, top_eta, top)
    partial_residual(held, part, masks)
    x_faces(held, ALONG_X, gx)
    z_faces(held, ALONG_Z, fz, slots)
    sz_far[...], sz_near[...] = facing(even_z(), fz[0], fz[1])


def final_kernel(v, part, sx_far, sx_near, sz_far, sz_near, row, v_out, peaks, face):
    top, peak, first_top = row_values(row, (0, 1, 2))
    step = 0.125 / peak
    slabs = sides(even_x(), sx_far[...], sx_near[...]) + sides(even_z(), sz_far[...], sz_near[...])
    for f, here, value in whole_residual(part, *slabs, face, iotas()):
        v_out[f, here] = v[f, here] + step * value
    peaks[0] = jnp.max(first_top)
    peaks[1] = jnp.max(top)


def per_device(velocity, pressure, stress_old, plastic, viscosity, weak_seed):
    shapes = [a.shape for a in (velocity, pressure, stress_old, plastic)]
    one = (ROWS, NY)
    v = velocity.reshape((3,) + one)
    old = stress_old.reshape((6,) + one)
    pressure, plastic, viscosity, weak_seed = (
        a.reshape(one) for a in (pressure, plastic, viscosity, weak_seed)
    )
    three, six = (3,) + one, (6,) + one
    face = pltpu.VMEM((2, 3, 2, ROWS, 128), F32)
    slots = pltpu.VMEM((6, 2, ROWS, 128), F32)
    level_1, level_2 = lax.axis_size(YCORE), lax.axis_size(XZ)
    row_1, row_2 = (level_1, 8, 128), (level_2, 2, 128)
    x_3, z_3, x_9, z_9 = (3 * LZ, NY), (3 * LX, NY), (9 * LZ, NY), (9 * LX, NY)

    dma = pltpu.SemaphoreType.DMA
    x_msgs = call(faces_kernel, [x_9, x_9], [v, plastic], 0, [dma((8,))], None, [HBM, HBM], 60)
    x_msgs = exchange(GX, *x_msgs)
    (along,) = call(own_x_kernel, [one], [plastic], 10**6)
    along, *z_msgs = call(smooth_x_kernel, [one, z_9, z_9], [v, along, *x_msgs], 10**6, [slots])
    z_msgs = exchange(GZ, *z_msgs)
    eta, weak, *tables = call(
        own_kernel, [one, one, one, one, (NY, NY)], [along, viscosity, weak_seed], 10**7
    )
    x_two, z_two, x_full, z_full = (2,) + x_3, (2,) + z_3, (7 * LZ, NY), (6 * LX + 8, NY)
    part, pres, total, cohesion, vx, vz, gx, fz, row, *sent = call(
        first_kernel,
        [three, one, one, one, x_two, z_two, x_two, z_two, row_1, z_full, z_full],
        [v, pressure, old, plastic, eta, weak, *tables, *x_msgs, *z_msgs],
        10**7,
        [face, slots, pltpu.VMEM(six, F32)],
    )
    row = spread(row, YCORE)
    z_got = exchange(GZ, *sent)
    row, *sent = call(
        x_pack_kernel, [row_2, x_full, x_full], [part, gx, *z_got, row], 10**5
    )
    row = spread(row, XZ)
    x_got = exchange(GX, *sent)
    res, rx, rz = call(
        residual_kernel, [three, x_two, z_two], [part, gx, fz, *x_got, *z_got], 10**6, [face]
    )
    stress, pres, total, v, part, row, gx, *sent = call(
        second_kernel,
        [six, one, one, three, three, row_1, x_two, z_3, z_3],
        [v, res, vx, vz, rx, rz, row, old, pres, total, eta, cohesion],
        10**7,
        [face, slots, pltpu.VMEM(z_two, F32), pltpu.VMEM(six, F32)],
    )
    row = spread(row, YCORE)
    z_got = exchange(GZ, *sent)
    row, *sent = call(relay_kernel, [row_2, x_3, x_3], [gx, *z_got, row], 10**4)
    row = spread(row, XZ)
    x_got = exchange(GX, *sent)
    v, peaks = call(
        final_kernel,
        [three, (2,)],
        [v, part, *x_got, *z_got, row],
        10**6,
        [face],
        [VMEM, SMEM],
    )
    outs = [a.reshape(s) for a, s in zip((v, pres, stress, total), shapes)]
    return (*outs, peaks)


def solution(mesh):
    split = Mesh(mesh.devices.reshape(4, 8, 2, 4, 2), ("gx_0", "gx_1", "gx_2", "gz_0", "gz_1"))
    return jax.shard_map(
        per_device,
        mesh=split,
        in_specs=(
            P(None, GX, GZ, None),
            P(GX, GZ, None),
            P(None, GX, GZ, None),
            P(GX, GZ, None),
            P(GX, GZ, None),
            P(GX, GZ, None),
        ),
        out_specs=(
            P(None, GX, GZ, None),
            P(GX, GZ, None),
            P(None, GX, GZ, None),
            P(GX, GZ, None),
            P(),
        ),
        check_vma=False,
    )
```

```python
import math

import jax
import jax.numpy as jnp
from jax import lax
from jax.experimental import pallas as pl
from jax.experimental.pallas import tpu as pltpu
from jax.sharding import Mesh
from jax.sharding import PartitionSpec as P

GX = ("gx_0", "gx_1", "gx_2")
GZ = ("gz_0", "gz_1")
YCORE = ("gx_2", "gz_0", "gz_1")
XZ = ("gx_0", "gx_1")

WEIGHT_TOTAL = sum(math.exp(-(k * k) / 18.0) for k in range(-6, 7))
WEIGHTS = [math.exp(-(k * k) / 18.0) / WEIGHT_TOTAL for k in range(-6, 7)]
SHEAR = 20.0
F32 = jnp.float32
LX, LZ, NY = 16, 8, 256
ROWS = LX * LZ
CHUNK = 16
XX, ZZ, YY, XZ_, XY, ZY = range(6)
ALONG_X = (XX, XZ_, XY)
ALONG_Z = (XZ_, ZZ, ZY)
ALONG_Y = (XY, ZY, YY)
VMEM = pl.BlockSpec(memory_space=pltpu.VMEM)
SMEM = pl.BlockSpec(memory_space=pltpu.SMEM)
HBM = pl.BlockSpec(memory_space=pltpu.HBM)


def call(kernel, outs, operands, flops, scratch=(), out_specs=None, in_specs=None, limit=14):
    size = sum(math.prod(a.shape) * 4 for a in operands)
    size += sum(math.prod(s) * 4 for s in outs)
    return pl.pallas_call(
        kernel,
        out_shape=[jax.ShapeDtypeStruct(s, F32) for s in outs],
        in_specs=in_specs or [VMEM] * len(operands),
        out_specs=out_specs or [VMEM] * len(outs),
        scratch_shapes=list(scratch),
        compiler_params=pltpu.CompilerParams(vmem_limit_bytes=limit * 1024 * 1024),
        cost_estimate=pl.CostEstimate(flops=flops, bytes_accessed=size, transcendentals=0),
    )(*operands)


def pairs(count, first):
    out = []
    for i in range(first, count - 1, 2):
        out += [(i, i + 1), (i + 1, i)]
    return out


def exchange(axis, far, near):
    count = lax.axis_size(axis)
    return (
        lax.ppermute(far, axis, pairs(count, 1)),
        lax.ppermute(near, axis, pairs(count, 0)),
    )


def spread(row, axes):
    return lax.all_to_all(row, axes, 0, 0, tiled=True)


def even_x():
    return lax.axis_index("gx_2") == 0


def even_z():
    return lax.axis_index("gz_1") == 0


def facing(even, first, last):
    return jnp.where(even, first, last), jnp.where(even, last, first)


def sides(even, far, near):
    return jnp.where(even, far, near), jnp.where(even, near, far)


def iotas():
    row = lax.broadcasted_iota(jnp.int32, (CHUNK, NY), 0) % LZ
    col = lax.broadcasted_iota(jnp.int32, (CHUNK, NY), 1)
    return row == 0, row == LZ - 1, col == 0, col == NY - 1


def below(ref, f, start, low):
    if start == 0:
        return jnp.concatenate([low, ref[f, 0 : CHUNK - LZ]], axis=0)
    return ref[f, start - LZ : start - LZ + CHUNK]


def above(ref, f, start, high):
    if start == ROWS - CHUNK:
        return jnp.concatenate([ref[f, start + LZ : ROWS], high], axis=0)
    return ref[f, start + LZ : start + LZ + CHUNK]


def diff_x(ref, f, start, low, high):
    return (above(ref, f, start, high) - below(ref, f, start, low)) * 0.5


def diff_z(value, low, high, masks):
    up = jnp.where(masks[1], high, pltpu.roll(value, CHUNK - 1, 0))
    down = jnp.where(masks[0], low, pltpu.roll(value, 1, 0))
    return (up - down) * 0.5


def diff_y(value, masks):
    up = jnp.where(masks[3], 0.0, pltpu.roll(value, NY - 1, 1))
    down = jnp.where(masks[2], 0.0, pltpu.roll(value, 1, 1))
    return (up - down) * 0.5


def spread_rows(face, f, low, high):
    for h in range(2):
        lanes = slice(h * 128, (h + 1) * 128)
        face[0, f, h, pl.ds(0, LX, stride=LZ), :] = low[:, lanes]
        face[1, f, h, pl.ds(LZ - 1, LX, stride=LZ), :] = high[:, lanes]


def face_rows(face, side, f, here):
    return jnp.concatenate([face[side, f, h, here] for h in range(2)], axis=1)


def keep(slots, f, value):
    for h in range(2):
        slots[f, h] = value[:, h * 128 : (h + 1) * 128]


def layer(slots, f, z):
    return jnp.concatenate([slots[f, h, pl.ds(z, LX, stride=LZ), :] for h in range(2)], axis=1)


def place(axes):
    index, count = 0, 1
    for axis in axes:
        size = lax.axis_size(axis)
        index, count = index * size + lax.axis_index(axis), count * size
    return index > 0, index < count - 1


def x_faces(ref, fields, out):
    for i, f in enumerate(fields):
        out[0, i * LZ : (i + 1) * LZ] = ref[f, 0:LZ]
        out[1, i * LZ : (i + 1) * LZ] = ref[f, ROWS - LZ : ROWS]


def z_faces(ref, fields, out, slots):
    for i, f in enumerate(fields):
        keep(slots, i, ref[f])
        out[0, i * LX : (i + 1) * LX] = layer(slots, i, 0)
        out[1, i * LX : (i + 1) * LX] = layer(slots, i, LZ - 1)


def faces_kernel(v, plastic, x_far, x_near, sem):
    even = even_x()
    for i, (out, low) in enumerate(((x_far, even), (x_near, jnp.logical_not(even)))):
        top = pl.multiple_of(jnp.where(low, 0, ROWS - LZ), LZ)
        deep = pl.multiple_of(jnp.where(low, 0, ROWS - 6 * LZ), LZ)
        copies = [
            pltpu.make_async_copy(
                v.at[f, pl.ds(top, LZ)], out.at[pl.ds(f * LZ, LZ)], sem.at[4 * i + f]
            )
            for f in range(3)
        ]
        copies.append(
            pltpu.make_async_copy(
                plastic.at[pl.ds(deep, 6 * LZ)], out.at[pl.ds(3 * LZ, 6 * LZ)], sem.at[4 * i + 3]
            )
        )
        for copy in copies:
            copy.start()
    for i, out in enumerate((x_far, x_near)):
        for f in range(3):
            rows = pl.ds(f * LZ, LZ)
            pltpu.make_async_copy(v.at[f, pl.ds(0, LZ)], out.at[rows], sem.at[4 * i + f]).wait()
        rows = pl.ds(3 * LZ, 6 * LZ)
        pltpu.make_async_copy(plastic.at[pl.ds(0, 6 * LZ)], out.at[rows], sem.at[4 * i + 3]).wait()


def store_row(out, top_yield, top_eta, earlier=None):
    a = jnp.max(top_yield, axis=(0, 1), keepdims=True)
    b = jnp.max(top_eta, axis=(0, 1), keepdims=True)
    lane = lax.broadcasted_iota(jnp.int32, (1, 128), 1)
    row = jnp.where(lane == 0, a, b)
    if earlier is not None:
        row = jnp.where(lane == 2, earlier, row)
    out[...] = jnp.broadcast_to(row[None], out.shape)


def relay_row(ref, out):
    row = jnp.max(ref[...], axis=0)[0:1]
    out[...] = jnp.broadcast_to(row[None], out.shape)


def row_values(ref, lanes):
    row = jnp.max(ref[...], axis=0)[0:1]
    lane = lax.broadcasted_iota(jnp.int32, (1, 128), 1)
    return [
        jnp.max(jnp.where(lane == i, row, -jnp.inf), axis=(0, 1), keepdims=True) for i in lanes
    ]


def return_map(dxv, dzv, dyv, old, eta, pres, cohesion):
    div = dxv[0] + dzv[1] + dyv[2]
    pres = pres - 0.25 * div
    third = div / 3.0
    strain = [
        dxv[0] - third,
        dzv[1] - third,
        dyv[2] - third,
        0.5 * (dxv[1] + dzv[0]),
        0.5 * (dxv[2] + dyv[0]),
        0.5 * (dzv[2] + dyv[1]),
    ]
    trial = [2.0 * eta * (e + o / (2.0 * SHEAR)) for e, o in zip(strain, old)]
    tau_ii = jnp.sqrt(
        0.5 * (trial[0] * trial[0] + trial[1] * trial[1] + trial[2] * trial[2])
        + trial[3] * trial[3]
        + trial[4] * trial[4]
        + trial[5] * trial[5]
    )
    yield_f = tau_ii - 0.5 * jnp.maximum(pres, 0.0) - 0.8660254 * cohesion
    dlam = jnp.maximum(yield_f, 0.0) / (eta + 0.5)
    shrink = 1.0 - eta * dlam / jnp.maximum(tau_ii, 0.5)
    return pres, [t * shrink for t in trial], eta * shrink, yield_f, dlam


def partial_residual(held, part, masks):
    nothing = jnp.zeros((LZ, NY), F32)
    for start in range(0, ROWS, CHUNK):
        here = slice(start, start + CHUNK)
        for f in range(3):
            part[f, here] = (
                diff_x(held, ALONG_X[f], start, nothing, nothing)
                + diff_z(held[ALONG_Z[f], here], 0.0, 0.0, masks)
                + diff_y(held[ALONG_Y[f], here], masks)
            )


def whole_residual(part, x_low, x_high, z_low, z_high, face, masks):
    for f in range(3):
        rows = slice(f * LX, (f + 1) * LX)
        spread_rows(face, f, z_low[rows], z_high[rows])
        slab = slice(f * LZ, (f + 1) * LZ)
        for start in range(0, ROWS, CHUNK):
            here = slice(start, start + CHUNK)
            value = (
                part[f, here]
                - jnp.where(masks[0], face_rows(face, 0, f, here) * 0.5, 0.0)
                + jnp.where(masks[1], face_rows(face, 1, f, here) * 0.5, 0.0)
            )
            if start == 0:
                value = jnp.concatenate([value[:LZ] - x_low[slab] * 0.5, value[LZ:]], axis=0)
            if start == ROWS - CHUNK:
                value = jnp.concatenate([value[:LZ], value[LZ:] + x_high[slab] * 0.5], axis=0)
            yield f, here, value


def own_x_kernel(plastic, along):
    for x in range(LX):
        total = None
        for k in range(max(-6, -x), min(6, LX - 1 - x) + 1):
            term = WEIGHTS[k + 6] * plastic[(x + k) * LZ : (x + k + 1) * LZ]
            total = term if total is None else total + term
        along[x * LZ : (x + 1) * LZ] = total


def smooth_x_kernel(v, own, x_far, x_near, along, z_far, z_near, slots):
    low, high = sides(even_x(), x_far[3 * LZ :], x_near[3 * LZ :])
    layers = []
    for x in range(LX):
        total = own[x * LZ : (x + 1) * LZ]
        for j in range(6):
            if x + 6 - j <= 6:
                total = total + WEIGHTS[j - x] * low[j * LZ : (j + 1) * LZ]
            if LX + j - x <= 6:
                total = total + WEIGHTS[LX + j - x + 6] * high[j * LZ : (j + 1) * LZ]
        layers.append(total)
    total = jnp.concatenate(layers, axis=0)
    along[...] = total
    keep(slots, 3, total)
    even = even_z()
    for i in range(9):
        if i < 3:
            keep(slots, i, v[i])
            a, b = facing(even, layer(slots, i, 0), layer(slots, i, LZ - 1))
        else:
            a, b = facing(even, layer(slots, 3, i - 3), layer(slots, 3, i - 1))
        z_far[i * LX : (i + 1) * LX] = a
        z_near[i * LX : (i + 1) * LX] = b


def gauss(gap, inside):
    g = gap.astype(F32)
    return jnp.where(inside & (jnp.abs(gap) <= 6), jnp.exp(g * g * (-1.0 / 18.0)) / WEIGHT_TOTAL, 0.0)


def own_kernel(along, viscosity, seed, eta, weak, own, from_z, along_y):
    eta[...] = 1.0 / (1.0 / viscosity[...] + 1.0 / SHEAR)
    weak[...] = 1.0 - 0.6 * seed[...].astype(F32)
    r = lax.broadcasted_iota(jnp.int32, (ROWS, ROWS), 0)
    c = lax.broadcasted_iota(jnp.int32, (ROWS, ROWS), 1)
    own_z = gauss(c % LZ - r % LZ, c // LZ == r // LZ)
    r = lax.broadcasted_iota(jnp.int32, (ROWS, NY), 0)
    c = lax.broadcasted_iota(jnp.int32, (ROWS, NY), 1)
    j = c // LX
    from_z[...] = gauss(jnp.where(j < 6, j - 6, j - 6 + LZ) - r % LZ, c % LX == r // LZ)
    r = lax.broadcasted_iota(jnp.int32, (NY, NY), 0)
    c = lax.broadcasted_iota(jnp.int32, (NY, NY), 1)
    along_y[...] = gauss(r - c, r >= 0)
    own[...] = dot(dot(own_z, along[...]), along_y[...])


def dot(a, b):
    return jnp.dot(a, b, precision=lax.Precision.HIGHEST, preferred_element_type=F32)


def first_kernel(
    v, pressure, old, plastic, eta_in, weak, own, from_z, along_y, x_far, x_near, z_far, z_near,
    part, pres, total, cohesion_out, vx_out, vz_out, gx, fz, row_out, sz_far, sz_near,
    face, slots, held,
):
    low, high = sides(even_z(), z_far[...], z_near[...])
    beside = jnp.concatenate([low[3 * LX :], high[3 * LX :]], axis=0)
    smoothed = own[...] + dot(dot(from_z[:, : 12 * LX], beside), along_y[...])
    cohesion_out[...] = weak[...] / (1.0 + 2.0 * smoothed)
    for f in range(3):
        spread_rows(face, f, low[f * LX : (f + 1) * LX], high[f * LX : (f + 1) * LX])
    x_low, x_high = sides(even_x(), x_far[0 : 3 * LZ], x_near[0 : 3 * LZ])
    vx_out[0], vx_out[1] = x_low, x_high
    vz_out[0], vz_out[1] = low[0 : 3 * LX], high[0 : 3 * LX]
    masks = iotas()
    top_yield = jnp.full((CHUNK, NY), -jnp.inf, F32)
    top_eta = jnp.full((CHUNK, NY), -jnp.inf, F32)
    for start in range(0, ROWS, CHUNK):
        here = slice(start, start + CHUNK)
        eta = eta_in[here]
        dxv, dzv, dyv = [], [], []
        for f in range(3):
            value = v[f, here]
            slab = slice(f * LZ, (f + 1) * LZ)
            dxv.append(diff_x(v, f, start, x_low[slab], x_high[slab]))
            dzv.append(diff_z(value, face_rows(face, 0, f, here), face_rows(face, 1, f, here), masks))
            dyv.append(diff_y(value, masks))
        p, tau, eta_shrink, yield_f, dlam = return_map(
            dxv, dzv, dyv, [old[i, here] for i in range(6)], eta, pressure[here], cohesion_out[here]
        )
        for i in range(6):
            held[i, here] = tau[i] - p if i < 3 else tau[i]
        pres[here] = p
        total[here] = plastic[here] + dlam
        top_yield = jnp.maximum(top_yield, yield_f)
        top_eta = jnp.maximum(top_eta, eta_shrink)
    store_row(row_out, top_yield, top_eta)
    partial_residual(held, part, masks)
    x_faces(held, ALONG_X, gx)
    z_faces(held, ALONG_Z, fz, slots)
    even = even_z()
    a, b = facing(even, fz[0], fz[1])
    sz_far[0 : 3 * LX], sz_near[0 : 3 * LX] = a, b
    for i in range(3):
        keep(slots, 3 + i, part[i])
        a, b = facing(even, layer(slots, 3 + i, 0), layer(slots, 3 + i, LZ - 1))
        sz_far[(3 + i) * LX : (4 + i) * LX] = a
        sz_near[(3 + i) * LX : (4 + i) * LX] = b
    corners = []
    for z in (0, LZ - 1):
        ends = [held[f, x * LZ + z : x * LZ + z + 1] for f in (XX, XY) for x in (0, LX - 1)]
        corners.append(jnp.concatenate(ends + ends, axis=0))
    a, b = facing(even, *corners)
    sz_far[6 * LX :], sz_near[6 * LX :] = a, b


def x_pack_kernel(part, gx, sz_far, sz_near, sx_far, sx_near):
    low, high = sides(even_z(), sz_far[...], sz_near[...])
    z = lax.broadcasted_iota(jnp.int32, (LZ, NY), 0)
    messages = []
    for e, x in enumerate((0, LX - 1)):
        pieces = [gx[e]]
        for f in range(3):
            below_z, above_z = (h[f * LX + x : f * LX + x + 1] for h in (low, high))
            pieces.append(
                part[f, x * LZ : (x + 1) * LZ]
                - jnp.where(z == 0, below_z * 0.5, 0.0)
                + jnp.where(z == LZ - 1, above_z * 0.5, 0.0)
            )
        ends = []
        for h in (low, high):
            ends += [h[6 * LX + e : 6 * LX + e + 1], h[x : x + 1], h[6 * LX + 2 + e : 6 * LX + 3 + e]]
        pieces.append(jnp.concatenate(ends + ends[:2], axis=0))
        messages.append(jnp.concatenate(pieces, axis=0))
    sx_far[...], sx_near[...] = facing(even_x(), *messages)


def residual_kernel(part, gx, fz, sx_far, sx_near, sz_far, sz_near, out, rx, rz, face):
    x_low, x_high = sides(even_x(), sx_far[...], sx_near[...])
    z_low, z_high = sides(even_z(), sz_far[...], sz_near[...])
    for f, here, value in whole_residual(part, x_low, x_high, z_low, z_high, face, iotas()):
        out[f, here] = value
    has_low, has_high = place(GX)
    rx[0] = jnp.where(has_low, x_low[3 * LZ : 6 * LZ] + gx[0] * 0.5, 0.0)
    rx[1] = jnp.where(has_high, x_high[3 * LZ : 6 * LZ] - gx[1] * 0.5, 0.0)
    x = lax.broadcasted_iota(jnp.int32, (LX, NY), 0)
    for side, (has, slab, sign) in enumerate(zip(place(GZ), (z_low, z_high), (0.5, -0.5))):
        for f in range(3):
            rows = slice(f * LX, (f + 1) * LX)
            end = 6 * LZ + 3 * side + f
            value = (
                slab[(3 + f) * LX : (4 + f) * LX]
                + fz[side, rows] * sign
                - jnp.where(x == 0, x_low[end : end + 1] * 0.5, 0.0)
                + jnp.where(x == LX - 1, x_high[end : end + 1] * 0.5, 0.0)
            )
            rz[side, rows] = jnp.where(has, value, 0.0)


def relay_kernel(near, row, row_out):
    relay_row(row, row_out)


def z_pack_kernel(fz, sx_far, sz_far, sz_near):
    sz_far[...], sz_near[...] = facing(even_z(), fz[0], fz[1])


def second_kernel(
    v, res, vx, vz, rx, rz, row,
    old, pressure, plastic, eta_in, cohesion,
    stress, pres, total, v_out, part, row_out, fz, sx_far, sx_near,
    face, slots, gx, held,
):
    top, peak = row_values(row, (0, 1))
    step = 0.125 / peak
    for f in range(3):
        v_out[f] = v[f] + step * res[f]
    x_low, x_high = vx[0] + step * rx[0], vx[1] + step * rx[1]
    z_low, z_high = vz[0] + step * rz[0], vz[1] + step * rz[1]
    for f in range(3):
        rows = slice(f * LX, (f + 1) * LX)
        spread_rows(face, f, z_low[rows], z_high[rows])
    masks = iotas()
    top_yield = jnp.full((CHUNK, NY), -jnp.inf, F32)
    top_eta = jnp.full((CHUNK, NY), -jnp.inf, F32)
    for start in range(0, ROWS, CHUNK):
        here = slice(start, start + CHUNK)
        dxv, dzv, dyv = [], [], []
        for f in range(3):
            value = v_out[f, here]
            slab = slice(f * LZ, (f + 1) * LZ)
            dxv.append(diff_x(v_out, f, start, x_low[slab], x_high[slab]))
            dzv.append(diff_z(value, face_rows(face, 0, f, here), face_rows(face, 1, f, here), masks))
            dyv.append(diff_y(value, masks))
        p, tau, eta_shrink, yield_f, dlam = return_map(
            dxv, dzv, dyv, [old[i, here] for i in range(6)], eta_in[here], pressure[here], cohesion[here]
        )
        for i in range(6):
            stress[i, here] = tau[i]
            held[i, here] = tau[i] - p if i < 3 else tau[i]
        pres[here] = p
        total[here] = plastic[here] + dlam
        top_yield = jnp.maximum(top_yield, yield_f)
        top_eta = jnp.maximum(top_eta, eta_shrink)
    store_row(row_out, top_yield, top_eta, top)
    partial_residual(held, part, masks)
    x_faces(held, ALONG_X, gx)
    z_faces(held, ALONG_Z, fz, slots)
    sx_far[0 : 3 * LZ], sx_near[...] = facing(even_x(), gx[0], gx[1])
    sx_far[3 * LZ :] = jnp.zeros((sx_far.shape[0] - 3 * LZ, NY), F32)


def final_kernel(v, part, sx_far, sx_near, sz_far, sz_near, row, v_out, peaks, face):
    top, peak, first_top = row_values(row, (0, 1, 2))
    step = 0.125 / peak
    slabs = sides(even_x(), sx_far[0 : 3 * LZ], sx_near[...]) + sides(
        even_z(), sz_far[...], sz_near[...]
    )
    for f, here, value in whole_residual(part, *slabs, face, iotas()):
        v_out[f, here] = v[f, here] + step * value
    peaks[0] = jnp.max(first_top)
    peaks[1] = jnp.max(top)


def per_device(velocity, pressure, stress_old, plastic, viscosity, weak_seed):
    shapes = [a.shape for a in (velocity, pressure, stress_old, plastic)]
    one = (ROWS, NY)
    v = velocity.reshape((3,) + one)
    old = stress_old.reshape((6,) + one)
    pressure, plastic, viscosity, weak_seed = (
        a.reshape(one) for a in (pressure, plastic, viscosity, weak_seed)
    )
    three, six = (3,) + one, (6,) + one
    face = pltpu.VMEM((2, 3, 2, ROWS, 128), F32)
    slots = pltpu.VMEM((6, 2, ROWS, 128), F32)
    level_1, level_2 = lax.axis_size(YCORE), lax.axis_size(XZ)
    row_1, row_2 = (level_1, 8, 128), (level_2, 2, 128)
    x_3, z_3, x_9, z_9 = (3 * LZ, NY), (3 * LX, NY), (9 * LZ, NY), (9 * LX, NY)

    dma = pltpu.SemaphoreType.DMA
    x_msgs = call(faces_kernel, [x_9, x_9], [v, plastic], 0, [dma((8,))], None, [HBM, HBM], 60)
    x_msgs = exchange(GX, *x_msgs)
    (along,) = call(own_x_kernel, [one], [plastic], 10**6)
    along, *z_msgs = call(smooth_x_kernel, [one, z_9, z_9], [v, along, *x_msgs], 10**6, [slots])
    z_msgs = exchange(GZ, *z_msgs)
    eta, weak, *tables = call(
        own_kernel, [one, one, one, one, (NY, NY)], [along, viscosity, weak_seed], 10**7
    )
    x_two, z_two, x_full, z_full = (2,) + x_3, (2,) + z_3, (7 * LZ, NY), (6 * LX + 8, NY)
    part, pres, total, cohesion, vx, vz, gx, fz, row, *sent = call(
        first_kernel,
        [three, one, one, one, x_two, z_two, x_two, z_two, row_1, z_full, z_full],
        [v, pressure, old, plastic, eta, weak, *tables, *x_msgs, *z_msgs],
        10**7,
        [face, slots, pltpu.VMEM(six, F32)],
    )
    row = spread(row, YCORE)
    z_got = exchange(GZ, *sent)
    (row,) = call(relay_kernel, [row_2], [z_got[1], row], 10**4)
    row = spread(row, XZ)
    sent = call(x_pack_kernel, [x_full, x_full], [part, gx, *z_got], 10**5)
    x_got = exchange(GX, *sent)
    res, rx, rz = call(
        residual_kernel, [three, x_two, z_two], [part, gx, fz, *x_got, *z_got], 10**6, [face]
    )
    stress, pres, total, v, part, row, fz, *sent = call(
        second_kernel,
        [six, one, one, three, three, row_2, z_two, (72, NY), x_3],
        [v, res, vx, vz, rx, rz, row, old, pres, total, eta, cohesion],
        10**7,
        [face, slots, pltpu.VMEM(x_two, F32), pltpu.VMEM(six, F32)],
    )
    row = spread(row, XZ)
    x_got = exchange(GX, *sent)
    (row,) = call(relay_kernel, [row_1], [x_got[1], row], 10**4)
    row = spread(row, YCORE)
    z_got = exchange(GZ, *call(z_pack_kernel, [z_3, z_3], [fz, x_got[0]], 10**4))
    v, peaks = call(
        final_kernel,
        [three, (2,)],
        [v, part, *x_got, *z_got, row],
        10**6,
        [face],
        [VMEM, SMEM],
    )
    outs = [a.reshape(s) for a, s in zip((v, pres, stress, total), shapes)]
    return (*outs, peaks)


def solution(mesh):
    split = Mesh(mesh.devices.reshape(4, 8, 2, 4, 2), ("gx_0", "gx_1", "gx_2", "gz_0", "gz_1"))
    return jax.shard_map(
        per_device,
        mesh=split,
        in_specs=(
            P(None, GX, GZ, None),
            P(GX, GZ, None),
            P(None, GX, GZ, None),
            P(GX, GZ, None),
            P(GX, GZ, None),
            P(GX, GZ, None),
        ),
        out_specs=(
            P(None, GX, GZ, None),
            P(GX, GZ, None),
            P(None, GX, GZ, None),
            P(GX, GZ, None),
            P(),
        ),
        check_vma=False,
    )
```

```python
import math

import jax
import jax.numpy as jnp
from jax import lax
from jax.experimental import pallas as pl
from jax.experimental.pallas import tpu as pltpu
from jax.sharding import Mesh
from jax.sharding import PartitionSpec as P

GX = ("gx_0", "gx_1", "gx_2")
GZ = ("gz_0", "gz_1")
YCORE = ("gx_2", "gz_0", "gz_1")
XZ = ("gx_0", "gx_1")

WEIGHT_TOTAL = sum(math.exp(-(k * k) / 18.0) for k in range(-6, 7))
WEIGHTS = [math.exp(-(k * k) / 18.0) / WEIGHT_TOTAL for k in range(-6, 7)]
SHEAR = 20.0
F32 = jnp.float32
LX, LZ, NY = 16, 8, 256
ROWS = LX * LZ
CHUNK = 16
XX, ZZ, YY, XZ_, XY, ZY = range(6)
ALONG_X = (XX, XZ_, XY)
ALONG_Z = (XZ_, ZZ, ZY)
ALONG_Y = (XY, ZY, YY)
VMEM = pl.BlockSpec(memory_space=pltpu.VMEM)
SMEM = pl.BlockSpec(memory_space=pltpu.SMEM)
HBM = pl.BlockSpec(memory_space=pltpu.HBM)


def call(kernel, outs, operands, flops, scratch=(), out_specs=None, in_specs=None, limit=14):
    size = sum(math.prod(a.shape) * 4 for a in operands)
    size += sum(math.prod(s) * 4 for s in outs)
    return pl.pallas_call(
        kernel,
        out_shape=[jax.ShapeDtypeStruct(s, F32) for s in outs],
        in_specs=in_specs or [VMEM] * len(operands),
        out_specs=out_specs or [VMEM] * len(outs),
        scratch_shapes=list(scratch),
        compiler_params=pltpu.CompilerParams(vmem_limit_bytes=limit * 1024 * 1024),
        cost_estimate=pl.CostEstimate(flops=flops, bytes_accessed=size, transcendentals=0),
    )(*operands)


def pairs(count, first):
    out = []
    for i in range(first, count - 1, 2):
        out += [(i, i + 1), (i + 1, i)]
    return out


def exchange(axis, far, near):
    count = lax.axis_size(axis)
    return (
        lax.ppermute(far, axis, pairs(count, 1)),
        lax.ppermute(near, axis, pairs(count, 0)),
    )


def spread(row, axes):
    return lax.all_to_all(row, axes, 0, 0, tiled=True)


def even_x():
    return lax.axis_index("gx_2") == 0


def even_z():
    return lax.axis_index("gz_1") == 0


def facing(even, first, last):
    return jnp.where(even, first, last), jnp.where(even, last, first)


def sides(even, far, near):
    return jnp.where(even, far, near), jnp.where(even, near, far)


def iotas():
    row = lax.broadcasted_iota(jnp.int32, (CHUNK, NY), 0) % LZ
    col = lax.broadcasted_iota(jnp.int32, (CHUNK, NY), 1)
    return row == 0, row == LZ - 1, col == 0, col == NY - 1


def below(ref, f, start, low):
    if start == 0:
        return jnp.concatenate([low, ref[f, 0 : CHUNK - LZ]], axis=0)
    return ref[f, start - LZ : start - LZ + CHUNK]


def above(ref, f, start, high):
    if start == ROWS - CHUNK:
        return jnp.concatenate([ref[f, start + LZ : ROWS], high], axis=0)
    return ref[f, start + LZ : start + LZ + CHUNK]


def diff_x(ref, f, start, low, high):
    return (above(ref, f, start, high) - below(ref, f, start, low)) * 0.5


def diff_z(value, low, high, masks):
    up = jnp.where(masks[1], high, pltpu.roll(value, CHUNK - 1, 0))
    down = jnp.where(masks[0], low, pltpu.roll(value, 1, 0))
    return (up - down) * 0.5


def diff_y(value, masks):
    up = jnp.where(masks[3], 0.0, pltpu.roll(value, NY - 1, 1))
    down = jnp.where(masks[2], 0.0, pltpu.roll(value, 1, 1))
    return (up - down) * 0.5


def spread_rows(face, f, low, high):
    for h in range(2):
        lanes = slice(h * 128, (h + 1) * 128)
        face[0, f, h, pl.ds(0, LX, stride=LZ), :] = low[:, lanes]
        face[1, f, h, pl.ds(LZ - 1, LX, stride=LZ), :] = high[:, lanes]


def face_rows(face, side, f, here):
    return jnp.concatenate([face[side, f, h, here] for h in range(2)], axis=1)


def keep(slots, f, value):
    for h in range(2):
        slots[f, h] = value[:, h * 128 : (h + 1) * 128]


def layer(slots, f, z):
    return jnp.concatenate([slots[f, h, pl.ds(z, LX, stride=LZ), :] for h in range(2)], axis=1)


def place(axes):
    index, count = 0, 1
    for axis in axes:
        size = lax.axis_size(axis)
        index, count = index * size + lax.axis_index(axis), count * size
    return index > 0, index < count - 1


def x_faces(ref, fields, out):
    for i, f in enumerate(fields):
        out[0, i * LZ : (i + 1) * LZ] = ref[f, 0:LZ]
        out[1, i * LZ : (i + 1) * LZ] = ref[f, ROWS - LZ : ROWS]


def z_faces(ref, fields, out, slots):
    for i, f in enumerate(fields):
        keep(slots, i, ref[f])
        out[0, i * LX : (i + 1) * LX] = layer(slots, i, 0)
        out[1, i * LX : (i + 1) * LX] = layer(slots, i, LZ - 1)


def faces_kernel(v, plastic, x_far, x_near, sem):
    even = even_x()
    for i, (out, low) in enumerate(((x_far, even), (x_near, jnp.logical_not(even)))):
        top = pl.multiple_of(jnp.where(low, 0, ROWS - LZ), LZ)
        deep = pl.multiple_of(jnp.where(low, 0, ROWS - 6 * LZ), LZ)
        copies = [
            pltpu.make_async_copy(
                v.at[f, pl.ds(top, LZ)], out.at[pl.ds(f * LZ, LZ)], sem.at[4 * i + f]
            )
            for f in range(3)
        ]
        copies.append(
            pltpu.make_async_copy(
                plastic.at[pl.ds(deep, 6 * LZ)], out.at[pl.ds(3 * LZ, 6 * LZ)], sem.at[4 * i + 3]
            )
        )
        for copy in copies:
            copy.start()
    for i, out in enumerate((x_far, x_near)):
        for f in range(3):
            rows = pl.ds(f * LZ, LZ)
            pltpu.make_async_copy(v.at[f, pl.ds(0, LZ)], out.at[rows], sem.at[4 * i + f]).wait()
        rows = pl.ds(3 * LZ, 6 * LZ)
        pltpu.make_async_copy(plastic.at[pl.ds(0, 6 * LZ)], out.at[rows], sem.at[4 * i + 3]).wait()


def store_row(out, top_yield, top_eta, earlier=None):
    a = jnp.max(top_yield, axis=(0, 1), keepdims=True)
    b = jnp.max(top_eta, axis=(0, 1), keepdims=True)
    lane = lax.broadcasted_iota(jnp.int32, (1, 128), 1)
    row = jnp.where(lane == 0, a, b)
    if earlier is not None:
        row = jnp.where(lane == 2, earlier, row)
    out[...] = jnp.broadcast_to(row[None], out.shape)


def relay_row(ref, out):
    row = jnp.max(ref[...], axis=0)[0:1]
    out[...] = jnp.broadcast_to(row[None], out.shape)


def row_values(ref, lanes):
    row = jnp.max(ref[...], axis=0)[0:1]
    lane = lax.broadcasted_iota(jnp.int32, (1, 128), 1)
    return [
        jnp.max(jnp.where(lane == i, row, -jnp.inf), axis=(0, 1), keepdims=True) for i in lanes
    ]


def return_map(dxv, dzv, dyv, old, eta, pres, cohesion):
    div = dxv[0] + dzv[1] + dyv[2]
    pres = pres - 0.25 * div
    third = div / 3.0
    strain = [
        dxv[0] - third,
        dzv[1] - third,
        dyv[2] - third,
        0.5 * (dxv[1] + dzv[0]),
        0.5 * (dxv[2] + dyv[0]),
        0.5 * (dzv[2] + dyv[1]),
    ]
    trial = [2.0 * eta * (e + o / (2.0 * SHEAR)) for e, o in zip(strain, old)]
    tau_ii = jnp.sqrt(
        0.5 * (trial[0] * trial[0] + trial[1] * trial[1] + trial[2] * trial[2])
        + trial[3] * trial[3]
        + trial[4] * trial[4]
        + trial[5] * trial[5]
    )
    yield_f = tau_ii - 0.5 * jnp.maximum(pres, 0.0) - 0.8660254 * cohesion
    dlam = jnp.maximum(yield_f, 0.0) / (eta + 0.5)
    shrink = 1.0 - eta * dlam / jnp.maximum(tau_ii, 0.5)
    return pres, [t * shrink for t in trial], eta * shrink, yield_f, dlam


def partial_residual(held, part, masks):
    nothing = jnp.zeros((LZ, NY), F32)
    for start in range(0, ROWS, CHUNK):
        here = slice(start, start + CHUNK)
        for f in range(3):
            part[f, here] = (
                diff_x(held, ALONG_X[f], start, nothing, nothing)
                + diff_z(held[ALONG_Z[f], here], 0.0, 0.0, masks)
                + diff_y(held[ALONG_Y[f], here], masks)
            )


def whole_residual(part, x_low, x_high, z_low, z_high, face, masks):
    for f in range(3):
        rows = slice(f * LX, (f + 1) * LX)
        spread_rows(face, f, z_low[rows], z_high[rows])
        slab = slice(f * LZ, (f + 1) * LZ)
        for start in range(0, ROWS, CHUNK):
            here = slice(start, start + CHUNK)
            value = (
                part[f, here]
                - jnp.where(masks[0], face_rows(face, 0, f, here) * 0.5, 0.0)
                + jnp.where(masks[1], face_rows(face, 1, f, here) * 0.5, 0.0)
            )
            if start == 0:
                value = jnp.concatenate([value[:LZ] - x_low[slab] * 0.5, value[LZ:]], axis=0)
            if start == ROWS - CHUNK:
                value = jnp.concatenate([value[:LZ], value[LZ:] + x_high[slab] * 0.5], axis=0)
            yield f, here, value


def own_x_kernel(plastic, along):
    for x in range(LX):
        total = None
        for k in range(max(-6, -x), min(6, LX - 1 - x) + 1):
            term = WEIGHTS[k + 6] * plastic[(x + k) * LZ : (x + k + 1) * LZ]
            total = term if total is None else total + term
        along[x * LZ : (x + 1) * LZ] = total


def smooth_x_kernel(v, own, x_far, x_near, along, z_far, z_near, slots):
    low, high = sides(even_x(), x_far[3 * LZ :], x_near[3 * LZ :])
    layers = []
    for x in range(LX):
        total = own[x * LZ : (x + 1) * LZ]
        for j in range(6):
            if x + 6 - j <= 6:
                total = total + WEIGHTS[j - x] * low[j * LZ : (j + 1) * LZ]
            if LX + j - x <= 6:
                total = total + WEIGHTS[LX + j - x + 6] * high[j * LZ : (j + 1) * LZ]
        layers.append(total)
    total = jnp.concatenate(layers, axis=0)
    along[...] = total
    keep(slots, 3, total)
    even = even_z()
    for i in range(9):
        if i < 3:
            keep(slots, i, v[i])
            a, b = facing(even, layer(slots, i, 0), layer(slots, i, LZ - 1))
        else:
            a, b = facing(even, layer(slots, 3, i - 3), layer(slots, 3, i - 1))
        z_far[i * LX : (i + 1) * LX] = a
        z_near[i * LX : (i + 1) * LX] = b


def gauss(gap, inside):
    g = gap.astype(F32)
    return jnp.where(inside & (jnp.abs(gap) <= 6), jnp.exp(g * g * (-1.0 / 18.0)) / WEIGHT_TOTAL, 0.0)


def own_kernel(along, viscosity, seed, eta, weak, own, from_z, along_y):
    eta[...] = 1.0 / (1.0 / viscosity[...] + 1.0 / SHEAR)
    weak[...] = 1.0 - 0.6 * seed[...].astype(F32)
    r = lax.broadcasted_iota(jnp.int32, (ROWS, ROWS), 0)
    c = lax.broadcasted_iota(jnp.int32, (ROWS, ROWS), 1)
    own_z = gauss(c % LZ - r % LZ, c // LZ == r // LZ)
    r = lax.broadcasted_iota(jnp.int32, (ROWS, NY), 0)
    c = lax.broadcasted_iota(jnp.int32, (ROWS, NY), 1)
    j = c // LX
    from_z[...] = gauss(jnp.where(j < 6, j - 6, j - 6 + LZ) - r % LZ, c % LX == r // LZ)
    r = lax.broadcasted_iota(jnp.int32, (NY, NY), 0)
    c = lax.broadcasted_iota(jnp.int32, (NY, NY), 1)
    along_y[...] = gauss(r - c, r >= 0)
    own[...] = dot(dot(own_z, along[...]), along_y[...])


def dot(a, b):
    return jnp.dot(a, b, precision=lax.Precision.HIGHEST, preferred_element_type=F32)


def first_kernel(
    v, pressure, old, plastic, eta_in, weak, own, from_z, along_y, x_far, x_near, z_far, z_near,
    part, pres, total, cohesion_out, vx_out, vz_out, gx, fz, pz, row_out, sx_far, sx_near,
    face, slots, held,
):
    low, high = sides(even_z(), z_far[...], z_near[...])
    beside = jnp.concatenate([low[3 * LX :], high[3 * LX :]], axis=0)
    smoothed = own[...] + dot(dot(from_z[:, : 12 * LX], beside), along_y[...])
    cohesion_out[...] = weak[...] / (1.0 + 2.0 * smoothed)
    for f in range(3):
        spread_rows(face, f, low[f * LX : (f + 1) * LX], high[f * LX : (f + 1) * LX])
    x_low, x_high = sides(even_x(), x_far[0 : 3 * LZ], x_near[0 : 3 * LZ])
    vx_out[0], vx_out[1] = x_low, x_high
    vz_out[0], vz_out[1] = low[0 : 3 * LX], high[0 : 3 * LX]
    masks = iotas()
    top_yield = jnp.full((CHUNK, NY), -jnp.inf, F32)
    top_eta = jnp.full((CHUNK, NY), -jnp.inf, F32)
    for start in range(0, ROWS, CHUNK):
        here = slice(start, start + CHUNK)
        eta = eta_in[here]
        dxv, dzv, dyv = [], [], []
        for f in range(3):
            value = v[f, here]
            slab = slice(f * LZ, (f + 1) * LZ)
            dxv.append(diff_x(v, f, start, x_low[slab], x_high[slab]))
            dzv.append(diff_z(value, face_rows(face, 0, f, here), face_rows(face, 1, f, here), masks))
            dyv.append(diff_y(value, masks))
        p, tau, eta_shrink, yield_f, dlam = return_map(
            dxv, dzv, dyv, [old[i, here] for i in range(6)], eta, pressure[here], cohesion_out[here]
        )
        for i in range(6):
            held[i, here] = tau[i] - p if i < 3 else tau[i]
        pres[here] = p
        total[here] = plastic[here] + dlam
        top_yield = jnp.maximum(top_yield, yield_f)
        top_eta = jnp.maximum(top_eta, eta_shrink)
    store_row(row_out, top_yield, top_eta)
    partial_residual(held, part, masks)
    x_faces(held, ALONG_X, gx)
    z_faces(held, ALONG_Z, fz, slots)
    z_faces(part, range(3), pz, slots)
    messages = []
    for e, x in enumerate((0, LX - 1)):
        layer_x = slice(x * LZ, (x + 1) * LZ)
        ends = [held[f, x * LZ + z : x * LZ + z + 1] for f in (ZZ, ZY) for z in (0, LZ - 1)]
        pieces = [gx[e]] + [part[f, layer_x] for f in range(3)] + [jnp.concatenate(ends + ends, axis=0)]
        messages.append(jnp.concatenate(pieces, axis=0))
    for out, message in zip((sx_far, sx_near), facing(even_x(), *messages)):
        out[0 : 7 * LZ] = message
        if out.shape[0] > 7 * LZ:
            out[7 * LZ :] = jnp.zeros((out.shape[0] - 7 * LZ, NY), F32)


def z_share_kernel(fz, pz, sx_far, sx_near, sz_far, sz_near):
    low, high = sides(even_x(), sx_far[0 : 7 * LZ], sx_near[0 : 7 * LZ])
    x = lax.broadcasted_iota(jnp.int32, (LX, NY), 0)
    messages = []
    for e, z in enumerate((0, LZ - 1)):
        pieces = [fz[e]]
        for f in range(3):
            at = slice(f * LZ + z, f * LZ + z + 1)
            pieces.append(
                pz[e, f * LX : (f + 1) * LX]
                - jnp.where(x == 0, low[at] * 0.5, 0.0)
                + jnp.where(x == LX - 1, high[at] * 0.5, 0.0)
            )
        ends = []
        for h in (low, high):
            rows = (LZ + z, 6 * LZ + e, 6 * LZ + 2 + e)
            ends += [h[at : at + 1] for at in rows]
        pieces.append(jnp.concatenate(ends + ends[:2], axis=0))
        messages.append(jnp.concatenate(pieces, axis=0))
    sz_far[...], sz_near[...] = facing(even_z(), *messages)


def residual_kernel(part, gx, fz, sx_far, sx_near, sz_far, sz_near, out, rx, rz, face):
    x_low, x_high = sides(even_x(), sx_far[0 : 7 * LZ], sx_near[0 : 7 * LZ])
    z_low, z_high = sides(even_z(), sz_far[...], sz_near[...])
    for f, here, value in whole_residual(part, x_low, x_high, z_low, z_high, face, iotas()):
        out[f, here] = value
    z = lax.broadcasted_iota(jnp.int32, (LZ, NY), 0)
    for side, (has, slab, sign) in enumerate(zip(place(GX), (x_low, x_high), (0.5, -0.5))):
        for f in range(3):
            rows = slice(f * LZ, (f + 1) * LZ)
            end = 6 * LX + 3 * side + f
            value = (
                slab[(3 + f) * LZ : (4 + f) * LZ]
                + gx[side, rows] * sign
                - jnp.where(z == 0, z_low[end : end + 1] * 0.5, 0.0)
                + jnp.where(z == LZ - 1, z_high[end : end + 1] * 0.5, 0.0)
            )
            rx[side, rows] = jnp.where(has, value, 0.0)
    for side, (has, slab, sign) in enumerate(zip(place(GZ), (z_low, z_high), (0.5, -0.5))):
        rz[side] = jnp.where(has, slab[3 * LX : 6 * LX] + fz[side] * sign, 0.0)


def relay_kernel(near, row, row_out):
    relay_row(row, row_out)


def z_pack_kernel(fz, sx_far, sz_far, sz_near):
    sz_far[...], sz_near[...] = facing(even_z(), fz[0], fz[1])


def second_kernel(
    v, res, vx, vz, rx, rz, row,
    old, pressure, plastic, eta_in, cohesion,
    stress, pres, total, v_out, part, row_out, fz, sx_far, sx_near,
    face, slots, gx, held,
):
    top, peak = row_values(row, (0, 1))
    step = 0.125 / peak
    for f in range(3):
        v_out[f] = v[f] + step * res[f]
    x_low, x_high = vx[0] + step * rx[0], vx[1] + step * rx[1]
    z_low, z_high = vz[0] + step * rz[0], vz[1] + step * rz[1]
    for f in range(3):
        rows = slice(f * LX, (f + 1) * LX)
        spread_rows(face, f, z_low[rows], z_high[rows])
    masks = iotas()
    top_yield = jnp.full((CHUNK, NY), -jnp.inf, F32)
    top_eta = jnp.full((CHUNK, NY), -jnp.inf, F32)
    for start in range(0, ROWS, CHUNK):
        here = slice(start, start + CHUNK)
        dxv, dzv, dyv = [], [], []
        for f in range(3):
            value = v_out[f, here]
            slab = slice(f * LZ, (f + 1) * LZ)
            dxv.append(diff_x(v_out, f, start, x_low[slab], x_high[slab]))
            dzv.append(diff_z(value, face_rows(face, 0, f, here), face_rows(face, 1, f, here), masks))
            dyv.append(diff_y(value, masks))
        p, tau, eta_shrink, yield_f, dlam = return_map(
            dxv, dzv, dyv, [old[i, here] for i in range(6)], eta_in[here], pressure[here], cohesion[here]
        )
        for i in range(6):
            stress[i, here] = tau[i]
            held[i, here] = tau[i] - p if i < 3 else tau[i]
        pres[here] = p
        total[here] = plastic[here] + dlam
        top_yield = jnp.maximum(top_yield, yield_f)
        top_eta = jnp.maximum(top_eta, eta_shrink)
    store_row(row_out, top_yield, top_eta, top)
    partial_residual(held, part, masks)
    x_faces(held, ALONG_X, gx)
    z_faces(held, ALONG_Z, fz, slots)
    sx_far[0 : 3 * LZ], sx_near[...] = facing(even_x(), gx[0], gx[1])
    sx_far[3 * LZ :] = jnp.zeros((sx_far.shape[0] - 3 * LZ, NY), F32)


def final_kernel(v, part, sx_far, sx_near, sz_far, sz_near, row, v_out, peaks, face):
    top, peak, first_top = row_values(row, (0, 1, 2))
    step = 0.125 / peak
    slabs = sides(even_x(), sx_far[0 : 3 * LZ], sx_near[...]) + sides(
        even_z(), sz_far[...], sz_near[...]
    )
    for f, here, value in whole_residual(part, *slabs, face, iotas()):
        v_out[f, here] = v[f, here] + step * value
    peaks[0] = jnp.max(first_top)
    peaks[1] = jnp.max(top)


def per_device(velocity, pressure, stress_old, plastic, viscosity, weak_seed):
    shapes = [a.shape for a in (velocity, pressure, stress_old, plastic)]
    one = (ROWS, NY)
    v = velocity.reshape((3,) + one)
    old = stress_old.reshape((6,) + one)
    pressure, plastic, viscosity, weak_seed = (
        a.reshape(one) for a in (pressure, plastic, viscosity, weak_seed)
    )
    three, six = (3,) + one, (6,) + one
    face = pltpu.VMEM((2, 3, 2, ROWS, 128), F32)
    slots = pltpu.VMEM((6, 2, ROWS, 128), F32)
    level_1, level_2 = lax.axis_size(YCORE), lax.axis_size(XZ)
    row_1, row_2 = (level_1, 8, 128), (level_2, 2, 128)
    x_3, z_3, x_9, z_9 = (3 * LZ, NY), (3 * LX, NY), (9 * LZ, NY), (9 * LX, NY)

    dma = pltpu.SemaphoreType.DMA
    x_msgs = call(faces_kernel, [x_9, x_9], [v, plastic], 0, [dma((8,))], None, [HBM, HBM], 60)
    x_msgs = exchange(GX, *x_msgs)
    (along,) = call(own_x_kernel, [one], [plastic], 10**6)
    along, *z_msgs = call(smooth_x_kernel, [one, z_9, z_9], [v, along, *x_msgs], 10**6, [slots])
    z_msgs = exchange(GZ, *z_msgs)
    eta, weak, *tables = call(
        own_kernel, [one, one, one, one, (NY, NY)], [along, viscosity, weak_seed], 10**7
    )
    x_two, z_two, z_full = (2,) + x_3, (2,) + z_3, (6 * LX + 8, NY)
    part, pres, total, cohesion, vx, vz, gx, fz, pz, row, *sent = call(
        first_kernel,
        [three, one, one, one, x_two, z_two, x_two, z_two, z_two, row_2, (56, NY), (56, NY)],
        [v, pressure, old, plastic, eta, weak, *tables, *x_msgs, *z_msgs],
        10**7,
        [face, slots, pltpu.VMEM(six, F32)],
    )
    row = spread(row, XZ)
    x_got = exchange(GX, *sent)
    (row,) = call(relay_kernel, [row_1], [x_got[1], row], 10**4)
    row = spread(row, YCORE)
    z_got = exchange(GZ, *call(z_share_kernel, [z_full, z_full], [fz, pz, *x_got], 10**5))
    res, rx, rz = call(
        residual_kernel, [three, x_two, z_two], [part, gx, fz, *x_got, *z_got], 10**6, [face]
    )
    stress, pres, total, v, part, row, fz, *sent = call(
        second_kernel,
        [six, one, one, three, three, row_2, z_two, (72, NY), x_3],
        [v, res, vx, vz, rx, rz, row, old, pres, total, eta, cohesion],
        10**7,
        [face, slots, pltpu.VMEM(x_two, F32), pltpu.VMEM(six, F32)],
    )
    row = spread(row, XZ)
    x_got = exchange(GX, *sent)
    (row,) = call(relay_kernel, [row_1], [x_got[1], row], 10**4)
    row = spread(row, YCORE)
    z_got = exchange(GZ, *call(z_pack_kernel, [z_3, z_3], [fz, x_got[0]], 10**4))
    v, peaks = call(
        final_kernel,
        [three, (2,)],
        [v, part, *x_got, *z_got, row],
        10**6,
        [face],
        [VMEM, SMEM],
    )
    outs = [a.reshape(s) for a, s in zip((v, pres, stress, total), shapes)]
    return (*outs, peaks)


def solution(mesh):
    split = Mesh(mesh.devices.reshape(4, 8, 2, 4, 2), ("gx_0", "gx_1", "gx_2", "gz_0", "gz_1"))
    return jax.shard_map(
        per_device,
        mesh=split,
        in_specs=(
            P(None, GX, GZ, None),
            P(GX, GZ, None),
            P(None, GX, GZ, None),
            P(GX, GZ, None),
            P(GX, GZ, None),
            P(GX, GZ, None),
        ),
        out_specs=(
            P(None, GX, GZ, None),
            P(GX, GZ, None),
            P(None, GX, GZ, None),
            P(GX, GZ, None),
            P(),
        ),
        check_vma=False,
    )
```

```python
import math

import jax
import jax.numpy as jnp
from jax import lax
from jax.experimental import pallas as pl
from jax.experimental.pallas import tpu as pltpu
from jax.sharding import Mesh
from jax.sharding import PartitionSpec as P

GX = ("gx_0", "gx_1", "gx_2")
GZ = ("gz_0", "gz_1")

WEIGHT_TOTAL = sum(math.exp(-(k * k) / 18.0) for k in range(-6, 7))
WEIGHTS = [math.exp(-(k * k) / 18.0) / WEIGHT_TOTAL for k in range(-6, 7)]
SHEAR = 20.0
F32 = jnp.float32
LX, LZ, NY = 16, 8, 256
ROWS = LX * LZ
CHUNK = 16
XX, ZZ, YY, XZ_, XY, ZY = range(6)
ALONG_X = (XX, XZ_, XY)
ALONG_Z = (XZ_, ZZ, ZY)
ALONG_Y = (XY, ZY, YY)
VMEM = pl.BlockSpec(memory_space=pltpu.VMEM)
SMEM = pl.BlockSpec(memory_space=pltpu.SMEM)
HBM = pl.BlockSpec(memory_space=pltpu.HBM)


def call(kernel, outs, operands, flops, scratch=(), out_specs=None, in_specs=None, limit=14):
    size = sum(math.prod(a.shape) * 4 for a in operands)
    size += sum(math.prod(s) * 4 for s in outs)
    return pl.pallas_call(
        kernel,
        out_shape=[jax.ShapeDtypeStruct(s, F32) for s in outs],
        in_specs=in_specs or [VMEM] * len(operands),
        out_specs=out_specs or [VMEM] * len(outs),
        scratch_shapes=list(scratch),
        compiler_params=pltpu.CompilerParams(vmem_limit_bytes=limit * 1024 * 1024),
        cost_estimate=pl.CostEstimate(flops=flops, bytes_accessed=size, transcendentals=0),
    )(*operands)


def pairs(count, first):
    out = []
    for i in range(first, count - 1, 2):
        out += [(i, i + 1), (i + 1, i)]
    return out


def exchange(axis, far, near):
    count = lax.axis_size(axis)
    return (
        lax.ppermute(far, axis, pairs(count, 1)),
        lax.ppermute(near, axis, pairs(count, 0)),
    )


def spread(row, axes):
    return lax.all_to_all(row, axes, 0, 0, tiled=True)


def even_x():
    return lax.axis_index("gx_2") == 0


def even_z():
    return lax.axis_index("gz_1") == 0


def facing(even, first, last):
    return jnp.where(even, first, last), jnp.where(even, last, first)


def sides(even, far, near):
    return jnp.where(even, far, near), jnp.where(even, near, far)


def iotas():
    row = lax.broadcasted_iota(jnp.int32, (CHUNK, NY), 0) % LZ
    col = lax.broadcasted_iota(jnp.int32, (CHUNK, NY), 1)
    return row == 0, row == LZ - 1, col == 0, col == NY - 1


def below(ref, f, start, low):
    if start == 0:
        return jnp.concatenate([low, ref[f, 0 : CHUNK - LZ]], axis=0)
    return ref[f, start - LZ : start - LZ + CHUNK]


def above(ref, f, start, high):
    if start == ROWS - CHUNK:
        return jnp.concatenate([ref[f, start + LZ : ROWS], high], axis=0)
    return ref[f, start + LZ : start + LZ + CHUNK]


def diff_x(ref, f, start, low, high):
    return (above(ref, f, start, high) - below(ref, f, start, low)) * 0.5


def diff_z(value, low, high, masks):
    up = jnp.where(masks[1], high, pltpu.roll(value, CHUNK - 1, 0))
    down = jnp.where(masks[0], low, pltpu.roll(value, 1, 0))
    return (up - down) * 0.5


def diff_y(value, masks):
    up = jnp.where(masks[3], 0.0, pltpu.roll(value, NY - 1, 1))
    down = jnp.where(masks[2], 0.0, pltpu.roll(value, 1, 1))
    return (up - down) * 0.5


def spread_rows(face, f, low, high):
    for h in range(2):
        lanes = slice(h * 128, (h + 1) * 128)
        face[0, f, h, pl.ds(0, LX, stride=LZ), :] = low[:, lanes]
        face[1, f, h, pl.ds(LZ - 1, LX, stride=LZ), :] = high[:, lanes]


def face_rows(face, side, f, here):
    return jnp.concatenate([face[side, f, h, here] for h in range(2)], axis=1)


def keep(slots, f, value):
    for h in range(2):
        slots[f, h] = value[:, h * 128 : (h + 1) * 128]


def layer(slots, f, z):
    return jnp.concatenate([slots[f, h, pl.ds(z, LX, stride=LZ), :] for h in range(2)], axis=1)


def place(axes):
    index, count = 0, 1
    for axis in axes:
        size = lax.axis_size(axis)
        index, count = index * size + lax.axis_index(axis), count * size
    return index > 0, index < count - 1


def x_faces(ref, fields, out):
    for i, f in enumerate(fields):
        out[0, i * LZ : (i + 1) * LZ] = ref[f, 0:LZ]
        out[1, i * LZ : (i + 1) * LZ] = ref[f, ROWS - LZ : ROWS]


def z_faces(ref, fields, out, slots):
    for i, f in enumerate(fields):
        keep(slots, i, ref[f])
        out[0, i * LX : (i + 1) * LX] = layer(slots, i, 0)
        out[1, i * LX : (i + 1) * LX] = layer(slots, i, LZ - 1)


def faces_kernel(v, plastic, x_far, x_near, sem):
    even = even_x()
    for i, (out, low) in enumerate(((x_far, even), (x_near, jnp.logical_not(even)))):
        top = pl.multiple_of(jnp.where(low, 0, ROWS - LZ), LZ)
        deep = pl.multiple_of(jnp.where(low, 0, ROWS - 6 * LZ), LZ)
        copies = [
            pltpu.make_async_copy(
                v.at[f, pl.ds(top, LZ)], out.at[pl.ds(f * LZ, LZ)], sem.at[4 * i + f]
            )
            for f in range(3)
        ]
        copies.append(
            pltpu.make_async_copy(
                plastic.at[pl.ds(deep, 6 * LZ)], out.at[pl.ds(3 * LZ, 6 * LZ)], sem.at[4 * i + 3]
            )
        )
        for copy in copies:
            copy.start()
    for i, out in enumerate((x_far, x_near)):
        for f in range(3):
            rows = pl.ds(f * LZ, LZ)
            pltpu.make_async_copy(v.at[f, pl.ds(0, LZ)], out.at[rows], sem.at[4 * i + f]).wait()
        rows = pl.ds(3 * LZ, 6 * LZ)
        pltpu.make_async_copy(plastic.at[pl.ds(0, 6 * LZ)], out.at[rows], sem.at[4 * i + 3]).wait()


def store_row(out, top_yield, top_eta, earlier=None):
    a = jnp.max(top_yield, axis=(0, 1), keepdims=True)
    b = jnp.max(top_eta, axis=(0, 1), keepdims=True)
    lane = lax.broadcasted_iota(jnp.int32, (1, 128), 1)
    row = jnp.where(lane == 0, a, b)
    if earlier is not None:
        row = jnp.where(lane == 2, earlier, row)
    out[...] = jnp.broadcast_to(row[None], out.shape)


def relay_row(ref, out):
    row = jnp.max(ref[...], axis=0)[0:1]
    out[...] = jnp.broadcast_to(row[None], out.shape)


def row_values(ref, lanes):
    row = jnp.max(ref[...], axis=0)[0:1]
    lane = lax.broadcasted_iota(jnp.int32, (1, 128), 1)
    return [
        jnp.max(jnp.where(lane == i, row, -jnp.inf), axis=(0, 1), keepdims=True) for i in lanes
    ]


def return_map(dxv, dzv, dyv, old, eta, pres, cohesion):
    div = dxv[0] + dzv[1] + dyv[2]
    pres = pres - 0.25 * div
    third = div / 3.0
    strain = [
        dxv[0] - third,
        dzv[1] - third,
        dyv[2] - third,
        0.5 * (dxv[1] + dzv[0]),
        0.5 * (dxv[2] + dyv[0]),
        0.5 * (dzv[2] + dyv[1]),
    ]
    trial = [2.0 * eta * (e + o / (2.0 * SHEAR)) for e, o in zip(strain, old)]
    tau_ii = jnp.sqrt(
        0.5 * (trial[0] * trial[0] + trial[1] * trial[1] + trial[2] * trial[2])
        + trial[3] * trial[3]
        + trial[4] * trial[4]
        + trial[5] * trial[5]
    )
    yield_f = tau_ii - 0.5 * jnp.maximum(pres, 0.0) - 0.8660254 * cohesion
    dlam = jnp.maximum(yield_f, 0.0) / (eta + 0.5)
    shrink = 1.0 - eta * dlam / jnp.maximum(tau_ii, 0.5)
    return pres, [t * shrink for t in trial], eta * shrink, yield_f, dlam


def partial_residual(held, part, masks):
    nothing = jnp.zeros((LZ, NY), F32)
    for start in range(0, ROWS, CHUNK):
        here = slice(start, start + CHUNK)
        for f in range(3):
            part[f, here] = (
                diff_x(held, ALONG_X[f], start, nothing, nothing)
                + diff_z(held[ALONG_Z[f], here], 0.0, 0.0, masks)
                + diff_y(held[ALONG_Y[f], here], masks)
            )


def whole_residual(part, x_low, x_high, z_low, z_high, face, masks):
    for f in range(3):
        rows = slice(f * LX, (f + 1) * LX)
        spread_rows(face, f, z_low[rows], z_high[rows])
        slab = slice(f * LZ, (f + 1) * LZ)
        for start in range(0, ROWS, CHUNK):
            here = slice(start, start + CHUNK)
            value = (
                part[f, here]
                - jnp.where(masks[0], face_rows(face, 0, f, here) * 0.5, 0.0)
                + jnp.where(masks[1], face_rows(face, 1, f, here) * 0.5, 0.0)
            )
            if start == 0:
                value = jnp.concatenate([value[:LZ] - x_low[slab] * 0.5, value[LZ:]], axis=0)
            if start == ROWS - CHUNK:
                value = jnp.concatenate([value[:LZ], value[LZ:] + x_high[slab] * 0.5], axis=0)
            yield f, here, value


def own_x_kernel(plastic, along):
    for x in range(LX):
        total = None
        for k in range(max(-6, -x), min(6, LX - 1 - x) + 1):
            term = WEIGHTS[k + 6] * plastic[(x + k) * LZ : (x + k + 1) * LZ]
            total = term if total is None else total + term
        along[x * LZ : (x + 1) * LZ] = total


def smooth_x_kernel(v, own, x_far, x_near, along, z_far, z_near, slots):
    low, high = sides(even_x(), x_far[3 * LZ :], x_near[3 * LZ :])
    layers = []
    for x in range(LX):
        total = own[x * LZ : (x + 1) * LZ]
        for j in range(6):
            if x + 6 - j <= 6:
                total = total + WEIGHTS[j - x] * low[j * LZ : (j + 1) * LZ]
            if LX + j - x <= 6:
                total = total + WEIGHTS[LX + j - x + 6] * high[j * LZ : (j + 1) * LZ]
        layers.append(total)
    total = jnp.concatenate(layers, axis=0)
    along[...] = total
    keep(slots, 3, total)
    even = even_z()
    for i in range(9):
        if i < 3:
            keep(slots, i, v[i])
            a, b = facing(even, layer(slots, i, 0), layer(slots, i, LZ - 1))
        else:
            a, b = facing(even, layer(slots, 3, i - 3), layer(slots, 3, i - 1))
        z_far[i * LX : (i + 1) * LX] = a
        z_near[i * LX : (i + 1) * LX] = b


def gauss(gap, inside):
    g = gap.astype(F32)
    return jnp.where(inside & (jnp.abs(gap) <= 6), jnp.exp(g * g * (-1.0 / 18.0)) / WEIGHT_TOTAL, 0.0)


def own_kernel(along, viscosity, seed, eta, weak, own, from_z, along_y):
    eta[...] = 1.0 / (1.0 / viscosity[...] + 1.0 / SHEAR)
    weak[...] = 1.0 - 0.6 * seed[...].astype(F32)
    r = lax.broadcasted_iota(jnp.int32, (ROWS, ROWS), 0)
    c = lax.broadcasted_iota(jnp.int32, (ROWS, ROWS), 1)
    own_z = gauss(c % LZ - r % LZ, c // LZ == r // LZ)
    r = lax.broadcasted_iota(jnp.int32, (ROWS, NY), 0)
    c = lax.broadcasted_iota(jnp.int32, (ROWS, NY), 1)
    j = c // LX
    from_z[...] = gauss(jnp.where(j < 6, j - 6, j - 6 + LZ) - r % LZ, c % LX == r // LZ)
    r = lax.broadcasted_iota(jnp.int32, (NY, NY), 0)
    c = lax.broadcasted_iota(jnp.int32, (NY, NY), 1)
    along_y[...] = gauss(r - c, r >= 0)
    own[...] = dot(dot(own_z, along[...]), along_y[...])


def dot(a, b):
    return jnp.dot(a, b, precision=lax.Precision.HIGHEST, preferred_element_type=F32)


def first_kernel(
    v, pressure, old, plastic, eta_in, weak, own, from_z, along_y, x_far, x_near, z_far, z_near,
    part, pres, total, cohesion_out, vx_out, vz_out, gx, fz, row_out, sz_far, sz_near,
    face, slots, held,
):
    low, high = sides(even_z(), z_far[...], z_near[...])
    beside = jnp.concatenate([low[3 * LX :], high[3 * LX :]], axis=0)
    smoothed = own[...] + dot(dot(from_z[:, : 12 * LX], beside), along_y[...])
    cohesion_out[...] = weak[...] / (1.0 + 2.0 * smoothed)
    for f in range(3):
        spread_rows(face, f, low[f * LX : (f + 1) * LX], high[f * LX : (f + 1) * LX])
    x_low, x_high = sides(even_x(), x_far[0 : 3 * LZ], x_near[0 : 3 * LZ])
    vx_out[0], vx_out[1] = x_low, x_high
    vz_out[0], vz_out[1] = low[0 : 3 * LX], high[0 : 3 * LX]
    masks = iotas()
    top_yield = jnp.full((CHUNK, NY), -jnp.inf, F32)
    top_eta = jnp.full((CHUNK, NY), -jnp.inf, F32)
    for start in range(0, ROWS, CHUNK):
        here = slice(start, start + CHUNK)
        eta = eta_in[here]
        dxv, dzv, dyv = [], [], []
        for f in range(3):
            value = v[f, here]
            slab = slice(f * LZ, (f + 1) * LZ)
            dxv.append(diff_x(v, f, start, x_low[slab], x_high[slab]))
            dzv.append(diff_z(value, face_rows(face, 0, f, here), face_rows(face, 1, f, here), masks))
            dyv.append(diff_y(value, masks))
        p, tau, eta_shrink, yield_f, dlam = return_map(
            dxv, dzv, dyv, [old[i, here] for i in range(6)], eta, pressure[here], cohesion_out[here]
        )
        for i in range(6):
            held[i, here] = tau[i] - p if i < 3 else tau[i]
        pres[here] = p
        total[here] = plastic[here] + dlam
        top_yield = jnp.maximum(top_yield, yield_f)
        top_eta = jnp.maximum(top_eta, eta_shrink)
    store_row(row_out, top_yield, top_eta)
    partial_residual(held, part, masks)
    x_faces(held, ALONG_X, gx)
    z_faces(held, ALONG_Z, fz, slots)
    even = even_z()
    a, b = facing(even, fz[0], fz[1])
    sz_far[0 : 3 * LX], sz_near[0 : 3 * LX] = a, b
    for i in range(3):
        keep(slots, 3 + i, part[i])
        a, b = facing(even, layer(slots, 3 + i, 0), layer(slots, 3 + i, LZ - 1))
        sz_far[(3 + i) * LX : (4 + i) * LX] = a
        sz_near[(3 + i) * LX : (4 + i) * LX] = b
    corners = []
    for z in (0, LZ - 1):
        ends = [held[f, x * LZ + z : x * LZ + z + 1] for f in (XX, XY) for x in (0, LX - 1)]
        corners.append(jnp.concatenate(ends + ends, axis=0))
    a, b = facing(even, *corners)
    sz_far[6 * LX :], sz_near[6 * LX :] = a, b


def x_pack_kernel(part, gx, sz_far, sz_near, sx_far, sx_near):
    low, high = sides(even_z(), sz_far[...], sz_near[...])
    z = lax.broadcasted_iota(jnp.int32, (LZ, NY), 0)
    messages = []
    for e, x in enumerate((0, LX - 1)):
        pieces = [gx[e]]
        for f in range(3):
            below_z, above_z = (h[f * LX + x : f * LX + x + 1] for h in (low, high))
            pieces.append(
                part[f, x * LZ : (x + 1) * LZ]
                - jnp.where(z == 0, below_z * 0.5, 0.0)
                + jnp.where(z == LZ - 1, above_z * 0.5, 0.0)
            )
        ends = []
        for h in (low, high):
            ends += [h[6 * LX + e : 6 * LX + e + 1], h[x : x + 1], h[6 * LX + 2 + e : 6 * LX + 3 + e]]
        pieces.append(jnp.concatenate(ends + ends[:2], axis=0))
        messages.append(jnp.concatenate(pieces, axis=0))
    sx_far[...], sx_near[...] = facing(even_x(), *messages)


def residual_kernel(part, gx, fz, sx_far, sx_near, sz_far, sz_near, out, rx, rz, face):
    x_low, x_high = sides(even_x(), sx_far[...], sx_near[...])
    z_low, z_high = sides(even_z(), sz_far[...], sz_near[...])
    for f, here, value in whole_residual(part, x_low, x_high, z_low, z_high, face, iotas()):
        out[f, here] = value
    has_low, has_high = place(GX)
    rx[0] = jnp.where(has_low, x_low[3 * LZ : 6 * LZ] + gx[0] * 0.5, 0.0)
    rx[1] = jnp.where(has_high, x_high[3 * LZ : 6 * LZ] - gx[1] * 0.5, 0.0)
    x = lax.broadcasted_iota(jnp.int32, (LX, NY), 0)
    for side, (has, slab, sign) in enumerate(zip(place(GZ), (z_low, z_high), (0.5, -0.5))):
        for f in range(3):
            rows = slice(f * LX, (f + 1) * LX)
            end = 6 * LZ + 3 * side + f
            value = (
                slab[(3 + f) * LX : (4 + f) * LX]
                + fz[side, rows] * sign
                - jnp.where(x == 0, x_low[end : end + 1] * 0.5, 0.0)
                + jnp.where(x == LX - 1, x_high[end : end + 1] * 0.5, 0.0)
            )
            rz[side, rows] = jnp.where(has, value, 0.0)


def relay_kernel(near, row, row_out):
    relay_row(row, row_out)


def z_pack_kernel(fz, sx_far, sz_far, sz_near):
    sz_far[...], sz_near[...] = facing(even_z(), fz[0], fz[1])


def second_kernel(
    v, res, vx, vz, rx, rz, row,
    old, pressure, plastic, eta_in, cohesion,
    stress, pres, total, v_out, part, row_out, fz, sx_far, sx_near,
    face, slots, gx, held,
):
    top, peak = row_values(row, (0, 1))
    step = 0.125 / peak
    for f in range(3):
        v_out[f] = v[f] + step * res[f]
    x_low, x_high = vx[0] + step * rx[0], vx[1] + step * rx[1]
    z_low, z_high = vz[0] + step * rz[0], vz[1] + step * rz[1]
    for f in range(3):
        rows = slice(f * LX, (f + 1) * LX)
        spread_rows(face, f, z_low[rows], z_high[rows])
    masks = iotas()
    top_yield = jnp.full((CHUNK, NY), -jnp.inf, F32)
    top_eta = jnp.full((CHUNK, NY), -jnp.inf, F32)
    for start in range(0, ROWS, CHUNK):
        here = slice(start, start + CHUNK)
        dxv, dzv, dyv = [], [], []
        for f in range(3):
            value = v_out[f, here]
            slab = slice(f * LZ, (f + 1) * LZ)
            dxv.append(diff_x(v_out, f, start, x_low[slab], x_high[slab]))
            dzv.append(diff_z(value, face_rows(face, 0, f, here), face_rows(face, 1, f, here), masks))
            dyv.append(diff_y(value, masks))
        p, tau, eta_shrink, yield_f, dlam = return_map(
            dxv, dzv, dyv, [old[i, here] for i in range(6)], eta_in[here], pressure[here], cohesion[here]
        )
        for i in range(6):
            stress[i, here] = tau[i]
            held[i, here] = tau[i] - p if i < 3 else tau[i]
        pres[here] = p
        total[here] = plastic[here] + dlam
        top_yield = jnp.maximum(top_yield, yield_f)
        top_eta = jnp.maximum(top_eta, eta_shrink)
    store_row(row_out, top_yield, top_eta, top)
    partial_residual(held, part, masks)
    x_faces(held, ALONG_X, gx)
    z_faces(held, ALONG_Z, fz, slots)
    sx_far[0 : 3 * LZ], sx_near[...] = facing(even_x(), gx[0], gx[1])
    sx_far[3 * LZ :] = jnp.zeros((sx_far.shape[0] - 3 * LZ, NY), F32)


def final_kernel(v, part, sx_far, sx_near, sz_far, sz_near, row, v_out, peaks, face):
    top, peak, first_top = row_values(row, (0, 1, 2))
    step = 0.125 / peak
    slabs = sides(even_x(), sx_far[0 : 3 * LZ], sx_near[...]) + sides(
        even_z(), sz_far[...], sz_near[...]
    )
    for f, here, value in whole_residual(part, *slabs, face, iotas()):
        v_out[f, here] = v[f, here] + step * value
    peaks[0] = jnp.max(first_top)
    peaks[1] = jnp.max(top)


def per_device(velocity, pressure, stress_old, plastic, viscosity, weak_seed):
    shapes = [a.shape for a in (velocity, pressure, stress_old, plastic)]
    one = (ROWS, NY)
    v = velocity.reshape((3,) + one)
    old = stress_old.reshape((6,) + one)
    pressure, plastic, viscosity, weak_seed = (
        a.reshape(one) for a in (pressure, plastic, viscosity, weak_seed)
    )
    three, six = (3,) + one, (6,) + one
    face = pltpu.VMEM((2, 3, 2, ROWS, 128), F32)
    slots = pltpu.VMEM((6, 2, ROWS, 128), F32)
    level_1, level_2 = lax.axis_size(GZ), lax.axis_size(GX)
    row_1, row_2 = (level_1, 16, 128), (level_2, 1, 128)
    x_3, z_3, x_9, z_9 = (3 * LZ, NY), (3 * LX, NY), (9 * LZ, NY), (9 * LX, NY)

    dma = pltpu.SemaphoreType.DMA
    x_msgs = call(faces_kernel, [x_9, x_9], [v, plastic], 0, [dma((8,))], None, [HBM, HBM], 60)
    x_msgs = exchange(GX, *x_msgs)
    (along,) = call(own_x_kernel, [one], [plastic], 10**6)
    along, *z_msgs = call(smooth_x_kernel, [one, z_9, z_9], [v, along, *x_msgs], 10**6, [slots])
    z_msgs = exchange(GZ, *z_msgs)
    eta, weak, *tables = call(
        own_kernel, [one, one, one, one, (NY, NY)], [along, viscosity, weak_seed], 10**7
    )
    x_two, z_two, x_full, z_full = (2,) + x_3, (2,) + z_3, (7 * LZ, NY), (6 * LX + 8, NY)
    part, pres, total, cohesion, vx, vz, gx, fz, row, *sent = call(
        first_kernel,
        [three, one, one, one, x_two, z_two, x_two, z_two, row_1, z_full, z_full],
        [v, pressure, old, plastic, eta, weak, *tables, *x_msgs, *z_msgs],
        10**7,
        [face, slots, pltpu.VMEM(six, F32)],
    )
    row = spread(row, GZ)
    z_got = exchange(GZ, *sent)
    (row,) = call(relay_kernel, [row_2], [z_got[1], row], 10**4)
    row = spread(row, GX)
    sent = call(x_pack_kernel, [x_full, x_full], [part, gx, *z_got], 10**5)
    x_got = exchange(GX, *sent)
    res, rx, rz = call(
        residual_kernel, [three, x_two, z_two], [part, gx, fz, *x_got, *z_got], 10**6, [face]
    )
    stress, pres, total, v, part, row, fz, *sent = call(
        second_kernel,
        [six, one, one, three, three, row_2, z_two, (72, NY), x_3],
        [v, res, vx, vz, rx, rz, row, old, pres, total, eta, cohesion],
        10**7,
        [face, slots, pltpu.VMEM(x_two, F32), pltpu.VMEM(six, F32)],
    )
    row = spread(row, GX)
    x_got = exchange(GX, *sent)
    (row,) = call(relay_kernel, [row_1], [x_got[1], row], 10**4)
    row = spread(row, GZ)
    z_got = exchange(GZ, *call(z_pack_kernel, [z_3, z_3], [fz, x_got[0]], 10**4))
    v, peaks = call(
        final_kernel,
        [three, (2,)],
        [v, part, *x_got, *z_got, row],
        10**6,
        [face],
        [VMEM, SMEM],
    )
    outs = [a.reshape(s) for a, s in zip((v, pres, stress, total), shapes)]
    return (*outs, peaks)


def solution(mesh):
    split = Mesh(mesh.devices.reshape(4, 8, 2, 4, 2), ("gx_0", "gx_1", "gx_2", "gz_0", "gz_1"))
    return jax.shard_map(
        per_device,
        mesh=split,
        in_specs=(
            P(None, GX, GZ, None),
            P(GX, GZ, None),
            P(None, GX, GZ, None),
            P(GX, GZ, None),
            P(GX, GZ, None),
            P(GX, GZ, None),
        ),
        out_specs=(
            P(None, GX, GZ, None),
            P(GX, GZ, None),
            P(None, GX, GZ, None),
            P(GX, GZ, None),
            P(),
        ),
        check_vma=False,
    )
```

```python
import math

import jax
import jax.numpy as jnp
from jax import lax
from jax.experimental import pallas as pl
from jax.experimental.pallas import tpu as pltpu
from jax.sharding import Mesh
from jax.sharding import PartitionSpec as P

GX = ("gx_0", "gx_1", "gx_2")
GZ = ("gz_0", "gz_1")
YCORE = ("gx_2", "gz_0", "gz_1")
XZ = ("gx_0", "gx_1")

WEIGHT_TOTAL = sum(math.exp(-(k * k) / 18.0) for k in range(-6, 7))
WEIGHTS = [math.exp(-(k * k) / 18.0) / WEIGHT_TOTAL for k in range(-6, 7)]
SHEAR = 20.0
F32 = jnp.float32
LX, LZ, NY = 16, 8, 256
ROWS = LX * LZ
CHUNK = 16
XX, ZZ, YY, XZ_, XY, ZY = range(6)
ALONG_X = (XX, XZ_, XY)
ALONG_Z = (XZ_, ZZ, ZY)
ALONG_Y = (XY, ZY, YY)
VMEM = pl.BlockSpec(memory_space=pltpu.VMEM)
SMEM = pl.BlockSpec(memory_space=pltpu.SMEM)
HBM = pl.BlockSpec(memory_space=pltpu.HBM)


def call(kernel, outs, operands, flops, scratch=(), out_specs=None, in_specs=None, limit=14):
    size = sum(math.prod(a.shape) * 4 for a in operands)
    size += sum(math.prod(s) * 4 for s in outs)
    return pl.pallas_call(
        kernel,
        out_shape=[jax.ShapeDtypeStruct(s, F32) for s in outs],
        in_specs=in_specs or [VMEM] * len(operands),
        out_specs=out_specs or [VMEM] * len(outs),
        scratch_shapes=list(scratch),
        compiler_params=pltpu.CompilerParams(vmem_limit_bytes=limit * 1024 * 1024),
        cost_estimate=pl.CostEstimate(flops=flops, bytes_accessed=size, transcendentals=0),
    )(*operands)


def pairs(count, first):
    out = []
    for i in range(first, count - 1, 2):
        out += [(i, i + 1), (i + 1, i)]
    return out


def exchange(axis, far, near):
    count = lax.axis_size(axis)
    return (
        lax.ppermute(far, axis, pairs(count, 1)),
        lax.ppermute(near, axis, pairs(count, 0)),
    )


def spread(row, axes):
    return lax.all_to_all(row, axes, 0, 0, tiled=True)


def even_x():
    return lax.axis_index("gx_2") == 0


def even_z():
    return lax.axis_index("gz_1") == 0


def facing(even, first, last):
    return jnp.where(even, first, last), jnp.where(even, last, first)


def sides(even, far, near):
    return jnp.where(even, far, near), jnp.where(even, near, far)


def iotas():
    row = lax.broadcasted_iota(jnp.int32, (CHUNK, NY), 0) % LZ
    col = lax.broadcasted_iota(jnp.int32, (CHUNK, NY), 1)
    return row == 0, row == LZ - 1, col == 0, col == NY - 1


def below(ref, f, start, low):
    if start == 0:
        return jnp.concatenate([low, ref[f, 0 : CHUNK - LZ]], axis=0)
    return ref[f, start - LZ : start - LZ + CHUNK]


def above(ref, f, start, high):
    if start == ROWS - CHUNK:
        return jnp.concatenate([ref[f, start + LZ : ROWS], high], axis=0)
    return ref[f, start + LZ : start + LZ + CHUNK]


def diff_x(ref, f, start, low, high):
    return (above(ref, f, start, high) - below(ref, f, start, low)) * 0.5


def diff_z(value, low, high, masks):
    up = jnp.where(masks[1], high, pltpu.roll(value, CHUNK - 1, 0))
    down = jnp.where(masks[0], low, pltpu.roll(value, 1, 0))
    return (up - down) * 0.5


def diff_y(value, masks):
    up = jnp.where(masks[3], 0.0, pltpu.roll(value, NY - 1, 1))
    down = jnp.where(masks[2], 0.0, pltpu.roll(value, 1, 1))
    return (up - down) * 0.5


def spread_rows(face, f, low, high):
    for h in range(2):
        lanes = slice(h * 128, (h + 1) * 128)
        face[0, f, h, pl.ds(0, LX, stride=LZ), :] = low[:, lanes]
        face[1, f, h, pl.ds(LZ - 1, LX, stride=LZ), :] = high[:, lanes]


def face_rows(face, side, f, here):
    return jnp.concatenate([face[side, f, h, here] for h in range(2)], axis=1)


def keep(slots, f, value):
    for h in range(2):
        slots[f, h] = value[:, h * 128 : (h + 1) * 128]


def layer(slots, f, z):
    return jnp.concatenate([slots[f, h, pl.ds(z, LX, stride=LZ), :] for h in range(2)], axis=1)


def place(axes):
    index, count = 0, 1
    for axis in axes:
        size = lax.axis_size(axis)
        index, count = index * size + lax.axis_index(axis), count * size
    return index > 0, index < count - 1


def x_faces(ref, fields, out):
    for i, f in enumerate(fields):
        out[0, i * LZ : (i + 1) * LZ] = ref[f, 0:LZ]
        out[1, i * LZ : (i + 1) * LZ] = ref[f, ROWS - LZ : ROWS]


def z_faces(ref, fields, out, slots):
    for i, f in enumerate(fields):
        keep(slots, i, ref[f])
        out[0, i * LX : (i + 1) * LX] = layer(slots, i, 0)
        out[1, i * LX : (i + 1) * LX] = layer(slots, i, LZ - 1)


def faces_kernel(v, plastic, x_far, x_near, sem):
    even = even_x()
    copies = []
    for i, (out, low) in enumerate(((x_far, even), (x_near, jnp.logical_not(even)))):
        top, deep = jnp.where(low, 0, LX - 1), jnp.where(low, 0, LX - 6)
        copies.append(pltpu.make_async_copy(v.at[:, top], out.at[pl.ds(0, 3)], sem.at[2 * i]))
        copies.append(
            pltpu.make_async_copy(plastic.at[pl.ds(deep, 6)], out.at[pl.ds(3, 6)], sem.at[2 * i + 1])
        )
    for copy in copies:
        copy.start()
    for copy in copies:
        copy.wait()


def store_row(out, top_yield, top_eta, earlier=None):
    a = jnp.max(top_yield, axis=(0, 1), keepdims=True)
    b = jnp.max(top_eta, axis=(0, 1), keepdims=True)
    lane = lax.broadcasted_iota(jnp.int32, (1, 128), 1)
    row = jnp.where(lane == 0, a, b)
    if earlier is not None:
        row = jnp.where(lane == 2, earlier, row)
    out[...] = jnp.broadcast_to(row[None], out.shape)


def relay_row(ref, out):
    row = jnp.max(ref[...], axis=0)[0:1]
    out[...] = jnp.broadcast_to(row[None], out.shape)


def row_values(ref, lanes):
    row = jnp.max(ref[...], axis=0)[0:1]
    lane = lax.broadcasted_iota(jnp.int32, (1, 128), 1)
    return [
        jnp.max(jnp.where(lane == i, row, -jnp.inf), axis=(0, 1), keepdims=True) for i in lanes
    ]


def return_map(dxv, dzv, dyv, old, eta, pres, cohesion):
    div = dxv[0] + dzv[1] + dyv[2]
    pres = pres - 0.25 * div
    third = div / 3.0
    strain = [
        dxv[0] - third,
        dzv[1] - third,
        dyv[2] - third,
        0.5 * (dxv[1] + dzv[0]),
        0.5 * (dxv[2] + dyv[0]),
        0.5 * (dzv[2] + dyv[1]),
    ]
    trial = [2.0 * eta * (e + o / (2.0 * SHEAR)) for e, o in zip(strain, old)]
    tau_ii = jnp.sqrt(
        0.5 * (trial[0] * trial[0] + trial[1] * trial[1] + trial[2] * trial[2])
        + trial[3] * trial[3]
        + trial[4] * trial[4]
        + trial[5] * trial[5]
    )
    yield_f = tau_ii - 0.5 * jnp.maximum(pres, 0.0) - 0.8660254 * cohesion
    dlam = jnp.maximum(yield_f, 0.0) / (eta + 0.5)
    shrink = 1.0 - eta * dlam / jnp.maximum(tau_ii, 0.5)
    return pres, [t * shrink for t in trial], eta * shrink, yield_f, dlam


def partial_residual(held, part, masks):
    nothing = jnp.zeros((LZ, NY), F32)
    for start in range(0, ROWS, CHUNK):
        here = slice(start, start + CHUNK)
        for f in range(3):
            part[f, here] = (
                diff_x(held, ALONG_X[f], start, nothing, nothing)
                + diff_z(held[ALONG_Z[f], here], 0.0, 0.0, masks)
                + diff_y(held[ALONG_Y[f], here], masks)
            )


def whole_residual(part, x_low, x_high, z_low, z_high, face, masks):
    for f in range(3):
        rows = slice(f * LX, (f + 1) * LX)
        spread_rows(face, f, z_low[rows], z_high[rows])
        slab = slice(f * LZ, (f + 1) * LZ)
        for start in range(0, ROWS, CHUNK):
            here = slice(start, start + CHUNK)
            value = (
                part[f, here]
                - jnp.where(masks[0], face_rows(face, 0, f, here) * 0.5, 0.0)
                + jnp.where(masks[1], face_rows(face, 1, f, here) * 0.5, 0.0)
            )
            if start == 0:
                value = jnp.concatenate([value[:LZ] - x_low[slab] * 0.5, value[LZ:]], axis=0)
            if start == ROWS - CHUNK:
                value = jnp.concatenate([value[:LZ], value[LZ:] + x_high[slab] * 0.5], axis=0)
            yield f, here, value


def own_x_kernel(plastic, along):
    for x in range(LX):
        total = None
        for k in range(max(-6, -x), min(6, LX - 1 - x) + 1):
            term = WEIGHTS[k + 6] * plastic[(x + k) * LZ : (x + k + 1) * LZ]
            total = term if total is None else total + term
        along[x * LZ : (x + 1) * LZ] = total


def smooth_x_kernel(v, own, x_far, x_near, along, z_far, z_near, slots):
    low, high = sides(even_x(), x_far[3 * LZ :], x_near[3 * LZ :])
    layers = []
    for x in range(LX):
        total = own[x * LZ : (x + 1) * LZ]
        for j in range(6):
            if x + 6 - j <= 6:
                total = total + WEIGHTS[j - x] * low[j * LZ : (j + 1) * LZ]
            if LX + j - x <= 6:
                total = total + WEIGHTS[LX + j - x + 6] * high[j * LZ : (j + 1) * LZ]
        layers.append(total)
    total = jnp.concatenate(layers, axis=0)
    along[...] = total
    keep(slots, 3, total)
    even = even_z()
    for i in range(9):
        if i < 3:
            keep(slots, i, v[i])
            a, b = facing(even, layer(slots, i, 0), layer(slots, i, LZ - 1))
        else:
            a, b = facing(even, layer(slots, 3, i - 3), layer(slots, 3, i - 1))
        z_far[i * LX : (i + 1) * LX] = a
        z_near[i * LX : (i + 1) * LX] = b


def gauss(gap, inside):
    g = gap.astype(F32)
    return jnp.where(inside & (jnp.abs(gap) <= 6), jnp.exp(g * g * (-1.0 / 18.0)) / WEIGHT_TOTAL, 0.0)


def own_kernel(along, viscosity, seed, eta, weak, own, from_z, along_y):
    eta[...] = 1.0 / (1.0 / viscosity[...] + 1.0 / SHEAR)
    weak[...] = 1.0 - 0.6 * seed[...].astype(F32)
    r = lax.broadcasted_iota(jnp.int32, (ROWS, ROWS), 0)
    c = lax.broadcasted_iota(jnp.int32, (ROWS, ROWS), 1)
    own_z = gauss(c % LZ - r % LZ, c // LZ == r // LZ)
    r = lax.broadcasted_iota(jnp.int32, (ROWS, NY), 0)
    c = lax.broadcasted_iota(jnp.int32, (ROWS, NY), 1)
    j = c // LX
    from_z[...] = gauss(jnp.where(j < 6, j - 6, j - 6 + LZ) - r % LZ, c % LX == r // LZ)
    r = lax.broadcasted_iota(jnp.int32, (NY, NY), 0)
    c = lax.broadcasted_iota(jnp.int32, (NY, NY), 1)
    along_y[...] = gauss(r - c, r >= 0)
    own[...] = dot(dot(own_z, along[...]), along_y[...])


def dot(a, b):
    return jnp.dot(a, b, precision=lax.Precision.HIGHEST, preferred_element_type=F32)


def first_kernel(
    v, pressure, old, plastic, eta_in, weak, own, from_z, along_y, x_far, x_near, z_far, z_near,
    part, pres, total, cohesion_out, vx_out, vz_out, gx, fz, row_out, sz_far, sz_near,
    face, slots, held,
):
    low, high = sides(even_z(), z_far[...], z_near[...])
    beside = jnp.concatenate([low[3 * LX :], high[3 * LX :]], axis=0)
    smoothed = own[...] + dot(dot(from_z[:, : 12 * LX], beside), along_y[...])
    cohesion_out[...] = weak[...] / (1.0 + 2.0 * smoothed)
    for f in range(3):
        spread_rows(face, f, low[f * LX : (f + 1) * LX], high[f * LX : (f + 1) * LX])
    x_low, x_high = sides(even_x(), x_far[0 : 3 * LZ], x_near[0 : 3 * LZ])
    vx_out[0], vx_out[1] = x_low, x_high
    vz_out[0], vz_out[1] = low[0 : 3 * LX], high[0 : 3 * LX]
    masks = iotas()
    top_yield = jnp.full((CHUNK, NY), -jnp.inf, F32)
    top_eta = jnp.full((CHUNK, NY), -jnp.inf, F32)
    for start in range(0, ROWS, CHUNK):
        here = slice(start, start + CHUNK)
        eta = eta_in[here]
        dxv, dzv, dyv = [], [], []
        for f in range(3):
            value = v[f, here]
            slab = slice(f * LZ, (f + 1) * LZ)
            dxv.append(diff_x(v, f, start, x_low[slab], x_high[slab]))
            dzv.append(diff_z(value, face_rows(face, 0, f, here), face_rows(face, 1, f, here), masks))
            dyv.append(diff_y(value, masks))
        p, tau, eta_shrink, yield_f, dlam = return_map(
            dxv, dzv, dyv, [old[i, here] for i in range(6)], eta, pressure[here], cohesion_out[here]
        )
        for i in range(6):
            held[i, here] = tau[i] - p if i < 3 else tau[i]
        pres[here] = p
        total[here] = plastic[here] + dlam
        top_yield = jnp.maximum(top_yield, yield_f)
        top_eta = jnp.maximum(top_eta, eta_shrink)
    store_row(row_out, top_yield, top_eta)
    partial_residual(held, part, masks)
    x_faces(held, ALONG_X, gx)
    z_faces(held, ALONG_Z, fz, slots)
    even = even_z()
    a, b = facing(even, fz[0], fz[1])
    sz_far[0 : 3 * LX], sz_near[0 : 3 * LX] = a, b
    for i in range(3):
        keep(slots, 3 + i, part[i])
        a, b = facing(even, layer(slots, 3 + i, 0), layer(slots, 3 + i, LZ - 1))
        sz_far[(3 + i) * LX : (4 + i) * LX] = a
        sz_near[(3 + i) * LX : (4 + i) * LX] = b
    corners = []
    for z in (0, LZ - 1):
        ends = [held[f, x * LZ + z : x * LZ + z + 1] for f in (XX, XY) for x in (0, LX - 1)]
        corners.append(jnp.concatenate(ends + ends, axis=0))
    a, b = facing(even, *corners)
    sz_far[6 * LX :], sz_near[6 * LX :] = a, b


def x_pack_kernel(part, gx, sz_far, sz_near, sx_far, sx_near):
    low, high = sides(even_z(), sz_far[...], sz_near[...])
    z = lax.broadcasted_iota(jnp.int32, (LZ, NY), 0)
    messages = []
    for e, x in enumerate((0, LX - 1)):
        pieces = [gx[e]]
        for f in range(3):
            below_z, above_z = (h[f * LX + x : f * LX + x + 1] for h in (low, high))
            pieces.append(
                part[f, x * LZ : (x + 1) * LZ]
                - jnp.where(z == 0, below_z * 0.5, 0.0)
                + jnp.where(z == LZ - 1, above_z * 0.5, 0.0)
            )
        ends = []
        for h in (low, high):
            ends += [h[6 * LX + e : 6 * LX + e + 1], h[x : x + 1], h[6 * LX + 2 + e : 6 * LX + 3 + e]]
        pieces.append(jnp.concatenate(ends + ends[:2], axis=0))
        messages.append(jnp.concatenate(pieces, axis=0))
    sx_far[...], sx_near[...] = facing(even_x(), *messages)


def residual_kernel(part, gx, fz, sx_far, sx_near, sz_far, sz_near, out, rx, rz, face):
    x_low, x_high = sides(even_x(), sx_far[...], sx_near[...])
    z_low, z_high = sides(even_z(), sz_far[...], sz_near[...])
    for f, here, value in whole_residual(part, x_low, x_high, z_low, z_high, face, iotas()):
        out[f, here] = value
    has_low, has_high = place(GX)
    rx[0] = jnp.where(has_low, x_low[3 * LZ : 6 * LZ] + gx[0] * 0.5, 0.0)
    rx[1] = jnp.where(has_high, x_high[3 * LZ : 6 * LZ] - gx[1] * 0.5, 0.0)
    x = lax.broadcasted_iota(jnp.int32, (LX, NY), 0)
    for side, (has, slab, sign) in enumerate(zip(place(GZ), (z_low, z_high), (0.5, -0.5))):
        for f in range(3):
            rows = slice(f * LX, (f + 1) * LX)
            end = 6 * LZ + 3 * side + f
            value = (
                slab[(3 + f) * LX : (4 + f) * LX]
                + fz[side, rows] * sign
                - jnp.where(x == 0, x_low[end : end + 1] * 0.5, 0.0)
                + jnp.where(x == LX - 1, x_high[end : end + 1] * 0.5, 0.0)
            )
            rz[side, rows] = jnp.where(has, value, 0.0)


def relay_kernel(near, row, row_out):
    relay_row(row, row_out)


def z_pack_kernel(fz, sx_far, sz_far, sz_near):
    sz_far[...], sz_near[...] = facing(even_z(), fz[0], fz[1])


def second_kernel(
    v, res, vx, vz, rx, rz, row,
    old, pressure, plastic, eta_in, cohesion,
    stress, pres, total, v_out, part, row_out, fz, sx_far, sx_near,
    face, slots, gx, held,
):
    top, peak = row_values(row, (0, 1))
    step = 0.125 / peak
    for f in range(3):
        v_out[f] = v[f] + step * res[f]
    x_low, x_high = vx[0] + step * rx[0], vx[1] + step * rx[1]
    z_low, z_high = vz[0] + step * rz[0], vz[1] + step * rz[1]
    for f in range(3):
        rows = slice(f * LX, (f + 1) * LX)
        spread_rows(face, f, z_low[rows], z_high[rows])
    masks = iotas()
    top_yield = jnp.full((CHUNK, NY), -jnp.inf, F32)
    top_eta = jnp.full((CHUNK, NY), -jnp.inf, F32)
    for start in range(0, ROWS, CHUNK):
        here = slice(start, start + CHUNK)
        dxv, dzv, dyv = [], [], []
        for f in range(3):
            value = v_out[f, here]
            slab = slice(f * LZ, (f + 1) * LZ)
            dxv.append(diff_x(v_out, f, start, x_low[slab], x_high[slab]))
            dzv.append(diff_z(value, face_rows(face, 0, f, here), face_rows(face, 1, f, here), masks))
            dyv.append(diff_y(value, masks))
        p, tau, eta_shrink, yield_f, dlam = return_map(
            dxv, dzv, dyv, [old[i, here] for i in range(6)], eta_in[here], pressure[here], cohesion[here]
        )
        for i in range(6):
            stress[i, here] = tau[i]
            held[i, here] = tau[i] - p if i < 3 else tau[i]
        pres[here] = p
        total[here] = plastic[here] + dlam
        top_yield = jnp.maximum(top_yield, yield_f)
        top_eta = jnp.maximum(top_eta, eta_shrink)
    store_row(row_out, top_yield, top_eta, top)
    partial_residual(held, part, masks)
    x_faces(held, ALONG_X, gx)
    z_faces(held, ALONG_Z, fz, slots)
    sx_far[0 : 3 * LZ], sx_near[...] = facing(even_x(), gx[0], gx[1])
    sx_far[3 * LZ :] = jnp.zeros((sx_far.shape[0] - 3 * LZ, NY), F32)


def final_kernel(v, part, sx_far, sx_near, sz_far, sz_near, row, v_out, peaks, face):
    top, peak, first_top = row_values(row, (0, 1, 2))
    step = 0.125 / peak
    slabs = sides(even_x(), sx_far[0 : 3 * LZ], sx_near[...]) + sides(
        even_z(), sz_far[...], sz_near[...]
    )
    for f, here, value in whole_residual(part, *slabs, face, iotas()):
        v_out[f, here] = v[f, here] + step * value
    peaks[0] = jnp.max(first_top)
    peaks[1] = jnp.max(top)


def per_device(velocity, pressure, stress_old, plastic, viscosity, weak_seed):
    shapes = [a.shape for a in (velocity, pressure, stress_old, plastic)]
    one = (ROWS, NY)
    v = velocity.reshape((3,) + one)
    old = stress_old.reshape((6,) + one)
    pressure, plastic, viscosity, weak_seed = (
        a.reshape(one) for a in (pressure, plastic, viscosity, weak_seed)
    )
    three, six = (3,) + one, (6,) + one
    face = pltpu.VMEM((2, 3, 2, ROWS, 128), F32)
    slots = pltpu.VMEM((6, 2, ROWS, 128), F32)
    level_1, level_2 = lax.axis_size(YCORE), lax.axis_size(XZ)
    row_1, row_2 = (level_1, 8, 128), (level_2, 2, 128)
    x_3, z_3, x_9, z_9 = (3 * LZ, NY), (3 * LX, NY), (9 * LZ, NY), (9 * LX, NY)

    dma = pltpu.SemaphoreType.DMA
    blocks = [v.reshape((3, LX, LZ, NY)), plastic.reshape((LX, LZ, NY))]
    x_msgs = call(faces_kernel, [(9, LZ, NY)] * 2, blocks, 0, [dma((4,))], None, [HBM, HBM], 60)
    x_msgs = [m.reshape(x_9) for m in exchange(GX, *x_msgs)]
    (along,) = call(own_x_kernel, [one], [plastic], 10**6)
    along, *z_msgs = call(smooth_x_kernel, [one, z_9, z_9], [v, along, *x_msgs], 10**6, [slots])
    z_msgs = exchange(GZ, *z_msgs)
    eta, weak, *tables = call(
        own_kernel, [one, one, one, one, (NY, NY)], [along, viscosity, weak_seed], 10**7
    )
    x_two, z_two, x_full, z_full = (2,) + x_3, (2,) + z_3, (7 * LZ, NY), (6 * LX + 8, NY)
    part, pres, total, cohesion, vx, vz, gx, fz, row, *sent = call(
        first_kernel,
        [three, one, one, one, x_two, z_two, x_two, z_two, row_1, z_full, z_full],
        [v, pressure, old, plastic, eta, weak, *tables, *x_msgs, *z_msgs],
        10**7,
        [face, slots, pltpu.VMEM(six, F32)],
    )
    row = spread(row, YCORE)
    z_got = exchange(GZ, *sent)
    (row,) = call(relay_kernel, [row_2], [z_got[1], row], 10**4)
    row = spread(row, XZ)
    sent = call(x_pack_kernel, [x_full, x_full], [part, gx, *z_got], 10**5)
    x_got = exchange(GX, *sent)
    res, rx, rz = call(
        residual_kernel, [three, x_two, z_two], [part, gx, fz, *x_got, *z_got], 10**6, [face]
    )
    stress, pres, total, v, part, row, fz, *sent = call(
        second_kernel,
        [six, one, one, three, three, row_2, z_two, (72, NY), x_3],
        [v, res, vx, vz, rx, rz, row, old, pres, total, eta, cohesion],
        10**7,
        [face, slots, pltpu.VMEM(x_two, F32), pltpu.VMEM(six, F32)],
    )
    row = spread(row, XZ)
    x_got = exchange(GX, *sent)
    (row,) = call(relay_kernel, [row_1], [x_got[1], row], 10**4)
    row = spread(row, YCORE)
    z_got = exchange(GZ, *call(z_pack_kernel, [z_3, z_3], [fz, x_got[0]], 10**4))
    v, peaks = call(
        final_kernel,
        [three, (2,)],
        [v, part, *x_got, *z_got, row],
        10**6,
        [face],
        [VMEM, SMEM],
    )
    outs = [a.reshape(s) for a, s in zip((v, pres, stress, total), shapes)]
    return (*outs, peaks)


def solution(mesh):
    split = Mesh(mesh.devices.reshape(4, 8, 2, 4, 2), ("gx_0", "gx_1", "gx_2", "gz_0", "gz_1"))
    return jax.shard_map(
        per_device,
        mesh=split,
        in_specs=(
            P(None, GX, GZ, None),
            P(GX, GZ, None),
            P(None, GX, GZ, None),
            P(GX, GZ, None),
            P(GX, GZ, None),
            P(GX, GZ, None),
        ),
        out_specs=(
            P(None, GX, GZ, None),
            P(GX, GZ, None),
            P(None, GX, GZ, None),
            P(GX, GZ, None),
            P(),
        ),
        check_vma=False,
    )
```

```python
import math

import jax
import jax.numpy as jnp
from jax import lax
from jax.experimental import pallas as pl
from jax.experimental.pallas import tpu as pltpu
from jax.sharding import Mesh
from jax.sharding import PartitionSpec as P

GX = ("gx_0", "gx_1", "gx_2")
GZ = ("gz_0", "gz_1")
YCORE = ("gx_2", "gz_0", "gz_1")
XZ = ("gx_0", "gx_1")

WEIGHT_TOTAL = sum(math.exp(-(k * k) / 18.0) for k in range(-6, 7))
WEIGHTS = [math.exp(-(k * k) / 18.0) / WEIGHT_TOTAL for k in range(-6, 7)]
SHEAR = 20.0
F32 = jnp.float32
LX, LZ, NY = 16, 8, 256
ROWS = LX * LZ
CHUNK = 32
XX, ZZ, YY, XZ_, XY, ZY = range(6)
ALONG_X = (XX, XZ_, XY)
ALONG_Z = (XZ_, ZZ, ZY)
ALONG_Y = (XY, ZY, YY)
VMEM = pl.BlockSpec(memory_space=pltpu.VMEM)
SMEM = pl.BlockSpec(memory_space=pltpu.SMEM)
HBM = pl.BlockSpec(memory_space=pltpu.HBM)


def call(kernel, outs, operands, flops, scratch=(), out_specs=None, in_specs=None, limit=14):
    size = sum(math.prod(a.shape) * 4 for a in operands)
    size += sum(math.prod(s) * 4 for s in outs)
    return pl.pallas_call(
        kernel,
        out_shape=[jax.ShapeDtypeStruct(s, F32) for s in outs],
        in_specs=in_specs or [VMEM] * len(operands),
        out_specs=out_specs or [VMEM] * len(outs),
        scratch_shapes=list(scratch),
        compiler_params=pltpu.CompilerParams(vmem_limit_bytes=limit * 1024 * 1024),
        cost_estimate=pl.CostEstimate(flops=flops, bytes_accessed=size, transcendentals=0),
    )(*operands)


def pairs(count, first):
    out = []
    for i in range(first, count - 1, 2):
        out += [(i, i + 1), (i + 1, i)]
    return out


def exchange(axis, far, near):
    count = lax.axis_size(axis)
    return (
        lax.ppermute(far, axis, pairs(count, 1)),
        lax.ppermute(near, axis, pairs(count, 0)),
    )


def spread(row, axes):
    return lax.all_to_all(row, axes, 0, 0, tiled=True)


def even_x():
    return lax.axis_index("gx_2") == 0


def even_z():
    return lax.axis_index("gz_1") == 0


def facing(even, first, last):
    return jnp.where(even, first, last), jnp.where(even, last, first)


def sides(even, far, near):
    return jnp.where(even, far, near), jnp.where(even, near, far)


def iotas():
    row = lax.broadcasted_iota(jnp.int32, (CHUNK, NY), 0) % LZ
    col = lax.broadcasted_iota(jnp.int32, (CHUNK, NY), 1)
    return row == 0, row == LZ - 1, col == 0, col == NY - 1


def below(ref, f, start, low):
    if start == 0:
        return jnp.concatenate([low, ref[f, 0 : CHUNK - LZ]], axis=0)
    return ref[f, start - LZ : start - LZ + CHUNK]


def above(ref, f, start, high):
    if start == ROWS - CHUNK:
        return jnp.concatenate([ref[f, start + LZ : ROWS], high], axis=0)
    return ref[f, start + LZ : start + LZ + CHUNK]


def diff_x(ref, f, start, low, high):
    return (above(ref, f, start, high) - below(ref, f, start, low)) * 0.5


def diff_z(value, low, high, masks):
    up = jnp.where(masks[1], high, pltpu.roll(value, CHUNK - 1, 0))
    down = jnp.where(masks[0], low, pltpu.roll(value, 1, 0))
    return (up - down) * 0.5


def diff_y(value, masks):
    up = jnp.where(masks[3], 0.0, pltpu.roll(value, NY - 1, 1))
    down = jnp.where(masks[2], 0.0, pltpu.roll(value, 1, 1))
    return (up - down) * 0.5


def spread_rows(face, f, low, high):
    for h in range(2):
        lanes = slice(h * 128, (h + 1) * 128)
        face[0, f, h, pl.ds(0, LX, stride=LZ), :] = low[:, lanes]
        face[1, f, h, pl.ds(LZ - 1, LX, stride=LZ), :] = high[:, lanes]


def face_rows(face, side, f, here):
    return jnp.concatenate([face[side, f, h, here] for h in range(2)], axis=1)


def keep(slots, f, value):
    for h in range(2):
        slots[f, h] = value[:, h * 128 : (h + 1) * 128]


def layer(slots, f, z):
    return jnp.concatenate([slots[f, h, pl.ds(z, LX, stride=LZ), :] for h in range(2)], axis=1)


def place(axes):
    index, count = 0, 1
    for axis in axes:
        size = lax.axis_size(axis)
        index, count = index * size + lax.axis_index(axis), count * size
    return index > 0, index < count - 1


def x_faces(ref, fields, out):
    for i, f in enumerate(fields):
        out[0, i * LZ : (i + 1) * LZ] = ref[f, 0:LZ]
        out[1, i * LZ : (i + 1) * LZ] = ref[f, ROWS - LZ : ROWS]


def z_faces(ref, fields, out, slots):
    for i, f in enumerate(fields):
        keep(slots, i, ref[f])
        out[0, i * LX : (i + 1) * LX] = layer(slots, i, 0)
        out[1, i * LX : (i + 1) * LX] = layer(slots, i, LZ - 1)


def faces_kernel(v, plastic, x_far, x_near, sem):
    even = even_x()
    copies = []
    for i, (out, low) in enumerate(((x_far, even), (x_near, jnp.logical_not(even)))):
        top, deep = jnp.where(low, 0, LX - 1), jnp.where(low, 0, LX - 6)
        copies.append(pltpu.make_async_copy(v.at[:, top], out.at[pl.ds(0, 3)], sem.at[2 * i]))
        copies.append(
            pltpu.make_async_copy(plastic.at[pl.ds(deep, 6)], out.at[pl.ds(3, 6)], sem.at[2 * i + 1])
        )
    for copy in copies:
        copy.start()
    for copy in copies:
        copy.wait()


def store_row(out, top_yield, top_eta, earlier=None):
    a = jnp.max(top_yield, axis=(0, 1), keepdims=True)
    b = jnp.max(top_eta, axis=(0, 1), keepdims=True)
    lane = lax.broadcasted_iota(jnp.int32, (1, 128), 1)
    row = jnp.where(lane == 0, a, b)
    if earlier is not None:
        row = jnp.where(lane == 2, earlier, row)
    out[...] = jnp.broadcast_to(row[None], out.shape)


def relay_row(ref, out):
    row = jnp.max(ref[...], axis=0)[0:1]
    out[...] = jnp.broadcast_to(row[None], out.shape)


def row_values(ref, lanes):
    row = jnp.max(ref[...], axis=0)[0:1]
    lane = lax.broadcasted_iota(jnp.int32, (1, 128), 1)
    return [
        jnp.max(jnp.where(lane == i, row, -jnp.inf), axis=(0, 1), keepdims=True) for i in lanes
    ]


def return_map(dxv, dzv, dyv, old, eta, pres, cohesion):
    div = dxv[0] + dzv[1] + dyv[2]
    pres = pres - 0.25 * div
    third = div / 3.0
    strain = [
        dxv[0] - third,
        dzv[1] - third,
        dyv[2] - third,
        0.5 * (dxv[1] + dzv[0]),
        0.5 * (dxv[2] + dyv[0]),
        0.5 * (dzv[2] + dyv[1]),
    ]
    trial = [2.0 * eta * (e + o / (2.0 * SHEAR)) for e, o in zip(strain, old)]
    tau_ii = jnp.sqrt(
        0.5 * (trial[0] * trial[0] + trial[1] * trial[1] + trial[2] * trial[2])
        + trial[3] * trial[3]
        + trial[4] * trial[4]
        + trial[5] * trial[5]
    )
    yield_f = tau_ii - 0.5 * jnp.maximum(pres, 0.0) - 0.8660254 * cohesion
    dlam = jnp.maximum(yield_f, 0.0) / (eta + 0.5)
    shrink = 1.0 - eta * dlam / jnp.maximum(tau_ii, 0.5)
    return pres, [t * shrink for t in trial], eta * shrink, yield_f, dlam


def partial_residual(held, part, masks):
    nothing = jnp.zeros((LZ, NY), F32)
    for start in range(0, ROWS, CHUNK):
        here = slice(start, start + CHUNK)
        for f in range(3):
            part[f, here] = (
                diff_x(held, ALONG_X[f], start, nothing, nothing)
                + diff_z(held[ALONG_Z[f], here], 0.0, 0.0, masks)
                + diff_y(held[ALONG_Y[f], here], masks)
            )


def whole_residual(part, x_low, x_high, z_low, z_high, face, masks):
    for f in range(3):
        rows = slice(f * LX, (f + 1) * LX)
        spread_rows(face, f, z_low[rows], z_high[rows])
        slab = slice(f * LZ, (f + 1) * LZ)
        for start in range(0, ROWS, CHUNK):
            here = slice(start, start + CHUNK)
            value = (
                part[f, here]
                - jnp.where(masks[0], face_rows(face, 0, f, here) * 0.5, 0.0)
                + jnp.where(masks[1], face_rows(face, 1, f, here) * 0.5, 0.0)
            )
            if start == 0:
                value = jnp.concatenate([value[:LZ] - x_low[slab] * 0.5, value[LZ:]], axis=0)
            if start == ROWS - CHUNK:
                value = jnp.concatenate([value[: CHUNK - LZ], value[CHUNK - LZ :] + x_high[slab] * 0.5], axis=0)
            yield f, here, value


def own_x_kernel(plastic, along):
    for x in range(LX):
        total = None
        for k in range(max(-6, -x), min(6, LX - 1 - x) + 1):
            term = WEIGHTS[k + 6] * plastic[(x + k) * LZ : (x + k + 1) * LZ]
            total = term if total is None else total + term
        along[x * LZ : (x + 1) * LZ] = total


def smooth_x_kernel(v, own, x_far, x_near, along, z_far, z_near, slots):
    low, high = sides(even_x(), x_far[3 * LZ :], x_near[3 * LZ :])
    layers = []
    for x in range(LX):
        total = own[x * LZ : (x + 1) * LZ]
        for j in range(6):
            if x + 6 - j <= 6:
                total = total + WEIGHTS[j - x] * low[j * LZ : (j + 1) * LZ]
            if LX + j - x <= 6:
                total = total + WEIGHTS[LX + j - x + 6] * high[j * LZ : (j + 1) * LZ]
        layers.append(total)
    total = jnp.concatenate(layers, axis=0)
    along[...] = total
    keep(slots, 3, total)
    even = even_z()
    for i in range(9):
        if i < 3:
            keep(slots, i, v[i])
            a, b = facing(even, layer(slots, i, 0), layer(slots, i, LZ - 1))
        else:
            a, b = facing(even, layer(slots, 3, i - 3), layer(slots, 3, i - 1))
        z_far[i * LX : (i + 1) * LX] = a
        z_near[i * LX : (i + 1) * LX] = b


def gauss(gap, inside):
    g = gap.astype(F32)
    return jnp.where(inside & (jnp.abs(gap) <= 6), jnp.exp(g * g * (-1.0 / 18.0)) / WEIGHT_TOTAL, 0.0)


def own_kernel(along, viscosity, seed, eta, weak, own, from_z, along_y):
    eta[...] = 1.0 / (1.0 / viscosity[...] + 1.0 / SHEAR)
    weak[...] = 1.0 - 0.6 * seed[...].astype(F32)
    r = lax.broadcasted_iota(jnp.int32, (ROWS, ROWS), 0)
    c = lax.broadcasted_iota(jnp.int32, (ROWS, ROWS), 1)
    own_z = gauss(c % LZ - r % LZ, c // LZ == r // LZ)
    r = lax.broadcasted_iota(jnp.int32, (ROWS, NY), 0)
    c = lax.broadcasted_iota(jnp.int32, (ROWS, NY), 1)
    j = c // LX
    from_z[...] = gauss(jnp.where(j < 6, j - 6, j - 6 + LZ) - r % LZ, c % LX == r // LZ)
    r = lax.broadcasted_iota(jnp.int32, (NY, NY), 0)
    c = lax.broadcasted_iota(jnp.int32, (NY, NY), 1)
    along_y[...] = gauss(r - c, r >= 0)
    own[...] = dot(dot(own_z, along[...]), along_y[...])


def dot(a, b):
    return jnp.dot(a, b, precision=lax.Precision.HIGHEST, preferred_element_type=F32)


def first_kernel(
    v, pressure, old, plastic, eta_in, weak, own, from_z, along_y, x_far, x_near, z_far, z_near,
    part, pres, total, cohesion_out, vx_out, vz_out, gx, fz, row_out, sz_far, sz_near,
    face, slots, held,
):
    low, high = sides(even_z(), z_far[...], z_near[...])
    beside = jnp.concatenate([low[3 * LX :], high[3 * LX :]], axis=0)
    smoothed = own[...] + dot(dot(from_z[:, : 12 * LX], beside), along_y[...])
    cohesion_out[...] = weak[...] / (1.0 + 2.0 * smoothed)
    for f in range(3):
        spread_rows(face, f, low[f * LX : (f + 1) * LX], high[f * LX : (f + 1) * LX])
    x_low, x_high = sides(even_x(), x_far[0 : 3 * LZ], x_near[0 : 3 * LZ])
    vx_out[0], vx_out[1] = x_low, x_high
    vz_out[0], vz_out[1] = low[0 : 3 * LX], high[0 : 3 * LX]
    masks = iotas()
    top_yield = jnp.full((CHUNK, NY), -jnp.inf, F32)
    top_eta = jnp.full((CHUNK, NY), -jnp.inf, F32)
    for start in range(0, ROWS, CHUNK):
        here = slice(start, start + CHUNK)
        eta = eta_in[here]
        dxv, dzv, dyv = [], [], []
        for f in range(3):
            value = v[f, here]
            slab = slice(f * LZ, (f + 1) * LZ)
            dxv.append(diff_x(v, f, start, x_low[slab], x_high[slab]))
            dzv.append(diff_z(value, face_rows(face, 0, f, here), face_rows(face, 1, f, here), masks))
            dyv.append(diff_y(value, masks))
        p, tau, eta_shrink, yield_f, dlam = return_map(
            dxv, dzv, dyv, [old[i, here] for i in range(6)], eta, pressure[here], cohesion_out[here]
        )
        for i in range(6):
            held[i, here] = tau[i] - p if i < 3 else tau[i]
        pres[here] = p
        total[here] = plastic[here] + dlam
        top_yield = jnp.maximum(top_yield, yield_f)
        top_eta = jnp.maximum(top_eta, eta_shrink)
    store_row(row_out, top_yield, top_eta)
    partial_residual(held, part, masks)
    x_faces(held, ALONG_X, gx)
    z_faces(held, ALONG_Z, fz, slots)
    even = even_z()
    a, b = facing(even, fz[0], fz[1])
    sz_far[0 : 3 * LX], sz_near[0 : 3 * LX] = a, b
    for i in range(3):
        keep(slots, 3 + i, part[i])
        a, b = facing(even, layer(slots, 3 + i, 0), layer(slots, 3 + i, LZ - 1))
        sz_far[(3 + i) * LX : (4 + i) * LX] = a
        sz_near[(3 + i) * LX : (4 + i) * LX] = b
    corners = []
    for z in (0, LZ - 1):
        ends = [held[f, x * LZ + z : x * LZ + z + 1] for f in (XX, XY) for x in (0, LX - 1)]
        corners.append(jnp.concatenate(ends + ends, axis=0))
    a, b = facing(even, *corners)
    sz_far[6 * LX :], sz_near[6 * LX :] = a, b


def x_pack_kernel(part, gx, sz_far, sz_near, sx_far, sx_near):
    low, high = sides(even_z(), sz_far[...], sz_near[...])
    z = lax.broadcasted_iota(jnp.int32, (LZ, NY), 0)
    messages = []
    for e, x in enumerate((0, LX - 1)):
        pieces = [gx[e]]
        for f in range(3):
            below_z, above_z = (h[f * LX + x : f * LX + x + 1] for h in (low, high))
            pieces.append(
                part[f, x * LZ : (x + 1) * LZ]
                - jnp.where(z == 0, below_z * 0.5, 0.0)
                + jnp.where(z == LZ - 1, above_z * 0.5, 0.0)
            )
        ends = []
        for h in (low, high):
            ends += [h[6 * LX + e : 6 * LX + e + 1], h[x : x + 1], h[6 * LX + 2 + e : 6 * LX + 3 + e]]
        pieces.append(jnp.concatenate(ends + ends[:2], axis=0))
        messages.append(jnp.concatenate(pieces, axis=0))
    sx_far[...], sx_near[...] = facing(even_x(), *messages)


def residual_kernel(part, gx, fz, sx_far, sx_near, sz_far, sz_near, out, rx, rz, face):
    x_low, x_high = sides(even_x(), sx_far[...], sx_near[...])
    z_low, z_high = sides(even_z(), sz_far[...], sz_near[...])
    for f, here, value in whole_residual(part, x_low, x_high, z_low, z_high, face, iotas()):
        out[f, here] = value
    has_low, has_high = place(GX)
    rx[0] = jnp.where(has_low, x_low[3 * LZ : 6 * LZ] + gx[0] * 0.5, 0.0)
    rx[1] = jnp.where(has_high, x_high[3 * LZ : 6 * LZ] - gx[1] * 0.5, 0.0)
    x = lax.broadcasted_iota(jnp.int32, (LX, NY), 0)
    for side, (has, slab, sign) in enumerate(zip(place(GZ), (z_low, z_high), (0.5, -0.5))):
        for f in range(3):
            rows = slice(f * LX, (f + 1) * LX)
            end = 6 * LZ + 3 * side + f
            value = (
                slab[(3 + f) * LX : (4 + f) * LX]
                + fz[side, rows] * sign
                - jnp.where(x == 0, x_low[end : end + 1] * 0.5, 0.0)
                + jnp.where(x == LX - 1, x_high[end : end + 1] * 0.5, 0.0)
            )
            rz[side, rows] = jnp.where(has, value, 0.0)


def relay_kernel(near, row, row_out):
    relay_row(row, row_out)


def z_pack_kernel(fz, sx_far, sz_far, sz_near):
    sz_far[...], sz_near[...] = facing(even_z(), fz[0], fz[1])


def second_kernel(
    v, res, vx, vz, rx, rz, row,
    old, pressure, plastic, eta_in, cohesion,
    stress, pres, total, v_out, part, row_out, fz, sx_far, sx_near,
    face, slots, gx, held,
):
    top, peak = row_values(row, (0, 1))
    step = 0.125 / peak
    for f in range(3):
        v_out[f] = v[f] + step * res[f]
    x_low, x_high = vx[0] + step * rx[0], vx[1] + step * rx[1]
    z_low, z_high = vz[0] + step * rz[0], vz[1] + step * rz[1]
    for f in range(3):
        rows = slice(f * LX, (f + 1) * LX)
        spread_rows(face, f, z_low[rows], z_high[rows])
    masks = iotas()
    top_yield = jnp.full((CHUNK, NY), -jnp.inf, F32)
    top_eta = jnp.full((CHUNK, NY), -jnp.inf, F32)
    for start in range(0, ROWS, CHUNK):
        here = slice(start, start + CHUNK)
        dxv, dzv, dyv = [], [], []
        for f in range(3):
            value = v_out[f, here]
            slab = slice(f * LZ, (f + 1) * LZ)
            dxv.append(diff_x(v_out, f, start, x_low[slab], x_high[slab]))
            dzv.append(diff_z(value, face_rows(face, 0, f, here), face_rows(face, 1, f, here), masks))
            dyv.append(diff_y(value, masks))
        p, tau, eta_shrink, yield_f, dlam = return_map(
            dxv, dzv, dyv, [old[i, here] for i in range(6)], eta_in[here], pressure[here], cohesion[here]
        )
        for i in range(6):
            stress[i, here] = tau[i]
            held[i, here] = tau[i] - p if i < 3 else tau[i]
        pres[here] = p
        total[here] = plastic[here] + dlam
        top_yield = jnp.maximum(top_yield, yield_f)
        top_eta = jnp.maximum(top_eta, eta_shrink)
    store_row(row_out, top_yield, top_eta, top)
    partial_residual(held, part, masks)
    x_faces(held, ALONG_X, gx)
    z_faces(held, ALONG_Z, fz, slots)
    sx_far[0 : 3 * LZ], sx_near[...] = facing(even_x(), gx[0], gx[1])
    sx_far[3 * LZ :] = jnp.zeros((sx_far.shape[0] - 3 * LZ, NY), F32)


def final_kernel(v, part, sx_far, sx_near, sz_far, sz_near, row, v_out, peaks, face):
    top, peak, first_top = row_values(row, (0, 1, 2))
    step = 0.125 / peak
    slabs = sides(even_x(), sx_far[0 : 3 * LZ], sx_near[...]) + sides(
        even_z(), sz_far[...], sz_near[...]
    )
    for f, here, value in whole_residual(part, *slabs, face, iotas()):
        v_out[f, here] = v[f, here] + step * value
    peaks[0] = jnp.max(first_top)
    peaks[1] = jnp.max(top)


def per_device(velocity, pressure, stress_old, plastic, viscosity, weak_seed):
    shapes = [a.shape for a in (velocity, pressure, stress_old, plastic)]
    one = (ROWS, NY)
    v = velocity.reshape((3,) + one)
    old = stress_old.reshape((6,) + one)
    pressure, plastic, viscosity, weak_seed = (
        a.reshape(one) for a in (pressure, plastic, viscosity, weak_seed)
    )
    three, six = (3,) + one, (6,) + one
    face = pltpu.VMEM((2, 3, 2, ROWS, 128), F32)
    slots = pltpu.VMEM((6, 2, ROWS, 128), F32)
    level_1, level_2 = lax.axis_size(YCORE), lax.axis_size(XZ)
    row_1, row_2 = (level_1, 8, 128), (level_2, 2, 128)
    x_3, z_3, x_9, z_9 = (3 * LZ, NY), (3 * LX, NY), (9 * LZ, NY), (9 * LX, NY)

    dma = pltpu.SemaphoreType.DMA
    blocks = [v.reshape((3, LX, LZ, NY)), plastic.reshape((LX, LZ, NY))]
    x_msgs = call(faces_kernel, [(9, LZ, NY)] * 2, blocks, 0, [dma((4,))], None, [HBM, HBM], 60)
    x_msgs = [m.reshape(x_9) for m in exchange(GX, *x_msgs)]
    (along,) = call(own_x_kernel, [one], [plastic], 10**6)
    along, *z_msgs = call(smooth_x_kernel, [one, z_9, z_9], [v, along, *x_msgs], 10**6, [slots])
    z_msgs = exchange(GZ, *z_msgs)
    eta, weak, *tables = call(
        own_kernel, [one, one, one, one, (NY, NY)], [along, viscosity, weak_seed], 10**7
    )
    x_two, z_two, x_full, z_full = (2,) + x_3, (2,) + z_3, (7 * LZ, NY), (6 * LX + 8, NY)
    part, pres, total, cohesion, vx, vz, gx, fz, row, *sent = call(
        first_kernel,
        [three, one, one, one, x_two, z_two, x_two, z_two, row_1, z_full, z_full],
        [v, pressure, old, plastic, eta, weak, *tables, *x_msgs, *z_msgs],
        10**7,
        [face, slots, pltpu.VMEM(six, F32)],
    )
    row = spread(row, YCORE)
    z_got = exchange(GZ, *sent)
    (row,) = call(relay_kernel, [row_2], [z_got[1], row], 10**4)
    row = spread(row, XZ)
    sent = call(x_pack_kernel, [x_full, x_full], [part, gx, *z_got], 10**5)
    x_got = exchange(GX, *sent)
    res, rx, rz = call(
        residual_kernel, [three, x_two, z_two], [part, gx, fz, *x_got, *z_got], 10**6, [face]
    )
    stress, pres, total, v, part, row, fz, *sent = call(
        second_kernel,
        [six, one, one, three, three, row_2, z_two, (72, NY), x_3],
        [v, res, vx, vz, rx, rz, row, old, pres, total, eta, cohesion],
        10**7,
        [face, slots, pltpu.VMEM(x_two, F32), pltpu.VMEM(six, F32)],
    )
    row = spread(row, XZ)
    x_got = exchange(GX, *sent)
    (row,) = call(relay_kernel, [row_1], [x_got[1], row], 10**4)
    row = spread(row, YCORE)
    z_got = exchange(GZ, *call(z_pack_kernel, [z_3, z_3], [fz, x_got[0]], 10**4))
    v, peaks = call(
        final_kernel,
        [three, (2,)],
        [v, part, *x_got, *z_got, row],
        10**6,
        [face],
        [VMEM, SMEM],
    )
    outs = [a.reshape(s) for a, s in zip((v, pres, stress, total), shapes)]
    return (*outs, peaks)


def solution(mesh):
    split = Mesh(mesh.devices.reshape(4, 8, 2, 4, 2), ("gx_0", "gx_1", "gx_2", "gz_0", "gz_1"))
    return jax.shard_map(
        per_device,
        mesh=split,
        in_specs=(
            P(None, GX, GZ, None),
            P(GX, GZ, None),
            P(None, GX, GZ, None),
            P(GX, GZ, None),
            P(GX, GZ, None),
            P(GX, GZ, None),
        ),
        out_specs=(
            P(None, GX, GZ, None),
            P(GX, GZ, None),
            P(None, GX, GZ, None),
            P(GX, GZ, None),
            P(),
        ),
        check_vma=False,
    )
```
